32 devices in a mesh: sec: 16 (over z, y, core), scan: 2 (over x).
Axes of the slice: x: 2, y: 2, z: 4, core: 2. Of those that a mesh axis runs over, the one named last changes fastest.
Arguments:
- obj_amp: float32 [16, 512, 512], P('sec', 'scan'), may hold values from 0.97 to 1
- obj_phase: float32 [16, 512, 512], P('sec', 'scan'), may hold values from -3.140625 to 3.140625
- forward_waves: bfloat16 [16, 16, 2, 256, 256], P('sec', 'scan'), may hold values from -6 to 6
- exit_adjoint: bfloat16 [16, 2, 256, 256], P('scan'), may hold values from -6 to 6
- offsets: int32 [16, 2], P('scan'), may hold values from 0 to 256
Outputs:
- object_grad: float32 [16, 2, 512, 512], P('sec', None, 'scan')
The draws below stay inside these ranges and needn't reach their ends.
All inputs are finite; a program needn't handle non-finite values.
Results may differ from the reference program's by a relative error of at most 0.012.
The reference program's roundings to bfloat16 on the way count: a program that leaves them out, or rounds other values in their place, can miss the bound.
Values may be sent and summed in bfloat16 or wider, within the bound.
No kernel may reach another device: no remote copies, remote signals or barrier semaphores. Data moves between devices by JAX's collectives and lax.ppermute only.
A program may use at most 64 MiB of HBM per device.

```python
import jax
import jax.numpy as jnp
from jax import lax

W = 256
OBJ = 512
SUBSTEPS = 2
POS = 16
NSL = 16


def set_ends(entries, rng, least, largest):
    index_at = [jax.random.randint(jax.random.fold_in(rng, axis), (), 0, length) for axis, length in enumerate(entries.shape)]
    widest = entries.shape.index(max(entries.shape))
    neighbour = index_at[:widest] + [(index_at[widest] + 1) % entries.shape[widest]] + index_at[widest + 1:]
    return entries.at[tuple(index_at)].set(least).at[tuple(neighbour)].set(largest)


def block_scale(rng, dims, pieces, least, largest):
    gain = 1.0
    for dim, shards_of in pieces:
        steps = jax.random.uniform(jax.random.fold_in(jax.random.fold_in(rng, 6), dim), (shards_of,), jnp.float32, least / len(pieces), largest / len(pieces))
        gain = gain * jnp.repeat(jnp.exp(steps), dims[dim] // shards_of).reshape((-1,) + (1,) * (len(dims) - 1 - dim))
    return gain


def noise(rng, shape, width, bound, pieces=(), held_as=jnp.bfloat16):
    drawn = jax.random.normal(rng, shape, jnp.float32) * width
    if len(pieces) > 0:
        drawn = block_scale(rng, shape, pieces, -0.22, 0.18) * drawn
    return jnp.clip(drawn, min=-bound, max=bound).astype(held_as)


def setup_inputs(seed: int = 0) -> dict:
    keys = jax.random.split(jax.random.key(seed), 6)
    return {
        "obj_amp": jnp.clip(0.97 + 0.029999971 * jax.random.uniform(keys[0], (NSL, OBJ, OBJ), jnp.float32) ** block_scale(keys[0], (NSL, OBJ, OBJ), ((0, 16), (1, 2)), -0.2, 0.2), 0.97, 1.0),
        "obj_phase": jnp.clip(jax.random.uniform(keys[1], (NSL, OBJ, OBJ), jnp.float32, -3.140625, 3.140625), -3.140625, 3.140625),
        "forward_waves": noise(keys[2], (NSL, POS, 2, W, W), 1.0, 6.0, ((0, 16), (1, 2))),
        "exit_adjoint": noise(keys[3], (POS, 2, W, W), 1.0, 6.0, ((0, 2),)),
        "offsets": set_ends(jax.random.randint(keys[4], (POS, 2), 0, OBJ - W + 1), jax.random.fold_in(keys[4], 1), 0, OBJ - W).astype(jnp.int32),
    }


damping = 0.0005
turning = 0.011


def laplacian(field):
    widths = [(0, 0)] * (field.ndim - 2) + [(1, 1), (1, 1)]
    padded = jnp.pad(field, widths)
    beside = padded[..., 2:, 1:-1] + padded[..., :-2, 1:-1] + padded[..., 1:-1, 2:] + padded[..., 1:-1, :-2]
    return beside - 4.0 * field


def back_step(field):
    for substep in range(SUBSTEPS):
        lap_re = laplacian(field[..., 0, :, :])
        lap_im = laplacian(field[..., 1, :, :])
        new_re = field[..., 0, :, :] + damping * lap_re + turning * lap_im
        new_im = field[..., 1, :, :] + damping * lap_im - turning * lap_re
        field = jnp.stack([new_re, new_im], axis=-3)
    return field


def reference(obj_amp, obj_phase, forward_waves, exit_adjoint, offsets):
    trans_re = obj_amp * jnp.cos(obj_phase)
    trans_im = obj_amp * jnp.sin(obj_phase)
    gradient = jnp.zeros((NSL, 2, OBJ, OBJ), jnp.float32)

    def per_position(gradient, position):
        row_at = offsets[position, 0].astype(jnp.int32)
        col_at = offsets[position, 1].astype(jnp.int32)
        adjoint = exit_adjoint[position].astype(jnp.float32)

        def per_slice(carry, layer):
            gradient, adjoint = carry
            spread = back_step(adjoint)
            incoming = forward_waves[layer, position].astype(jnp.float32)
            part_re = incoming[0] * spread[0] + incoming[1] * spread[1]
            part_im = incoming[0] * spread[1] - incoming[1] * spread[0]
            zero_index = jnp.zeros((), jnp.int32)
            current = lax.dynamic_slice(gradient, (layer, zero_index, row_at, col_at), (1, 2, W, W))
            added = current + jnp.stack([part_re, part_im])[None]
            gradient = lax.dynamic_update_slice(gradient, added, (layer, zero_index, row_at, col_at))
            win_re = lax.dynamic_slice(trans_re, (layer, row_at, col_at), (1, W, W))[0]
            win_im = lax.dynamic_slice(trans_im, (layer, row_at, col_at), (1, W, W))[0]
            out_re = win_re * spread[0] + win_im * spread[1]
            out_im = win_re * spread[1] - win_im * spread[0]
            leaving = jnp.stack([out_re, out_im]).astype(jnp.bfloat16)
            adjoint = lax.optimization_barrier(leaving).astype(jnp.float32)
            return (gradient, adjoint), None

        layers = jnp.arange(NSL, dtype=jnp.int32)
        (gradient, adjoint), unused = lax.scan(per_slice, (gradient, adjoint), layers, reverse=True)
        return gradient, None

    gradient, unused = lax.scan(per_position, gradient, jnp.arange(POS, dtype=jnp.int32))
    return gradient
```

```python
import jax
import jax.numpy as jnp
from jax import lax
from jax.experimental import pallas as pl
from jax.experimental.pallas import tpu as pltpu
from jax.sharding import PartitionSpec as P

SUBSTEPS = 2
damping = 0.0005
turning = 0.011
code_gain = 83.0
sublanes = 8
lanes = 128
vmem_bytes = 48 * 2**20


def params():
    return pltpu.CompilerParams(vmem_limit_bytes=vmem_bytes)


def around(corner_ref, position, window):
    row_at = corner_ref[position, 0]
    col_at = corner_ref[position, 1]
    row_by = lax.rem(row_at, sublanes)
    col_by = lax.rem(col_at, lanes)
    row_to = pl.multiple_of(row_at - row_by, sublanes)
    col_to = pl.multiple_of(col_at - col_by, lanes)
    return window + sublanes, window + lanes, row_to, row_by, col_to, col_by


def padded(rows, width):
    return pltpu.VMEM((2, 2 * rows + sublanes, width + lanes), jnp.float32)


def cut_kernel(corner_ref, place_ref, mine_ref, other_ref, win_ref, full_ref):
    position = pl.program_id(0)
    rows = mine_ref.shape[1]
    width = mine_ref.shape[2]
    window = win_ref.shape[-1]

    @pl.when(position == 0)
    def _():
        here = pl.multiple_of(place_ref[0] * rows, rows)
        there = pl.multiple_of((1 - place_ref[0]) * rows, rows)
        full_ref[:, pl.ds(here, rows), :width] = mine_ref[...].astype(jnp.float32)
        full_ref[:, pl.ds(there, rows), :width] = other_ref[...].astype(jnp.float32)

    tall, wide, row_to, row_by, col_to, col_by = around(corner_ref, position, window)
    for part in range(2):
        box = full_ref[part, pl.ds(row_to, tall), pl.ds(col_to, wide)]
        box = pltpu.roll(box, lax.rem(wide - col_by, wide), 1)[:, :window]
        box = pltpu.roll(box, lax.rem(tall - row_by, tall), 0)[:window]
        win_ref[0, part] = box.astype(jnp.bfloat16)


def cut_windows(offsets, place, mine, other, window):
    count = offsets.shape[0]
    _, rows, width = mine.shape
    whole = pl.BlockSpec(mine.shape, lambda p, *_: (0, 0, 0))
    return pl.pallas_call(
        cut_kernel,
        grid_spec=pltpu.PrefetchScalarGridSpec(
            num_scalar_prefetch=2,
            grid=(count,),
            in_specs=[whole, whole],
            out_specs=pl.BlockSpec((1, 2, window, window), lambda p, *_: (p, 0, 0, 0)),
            scratch_shapes=[padded(rows, width)],
        ),
        out_shape=jax.ShapeDtypeStruct((count, 2, window, window), jnp.bfloat16),
        compiler_params=params(),
    )(offsets, place, mine, other)


def second_difference(size):
    row = lax.broadcasted_iota(jnp.int32, (size, size), 0)
    col = lax.broadcasted_iota(jnp.int32, (size, size), 1)
    apart = jnp.abs(row - col)
    return jnp.where(apart == 0, -2.0, jnp.where(apart == 1, 1.0, 0.0)).astype(jnp.bfloat16)


def laplacian(band, field_re, field_im):
    def one(field):
        down = jnp.dot(band, field, preferred_element_type=jnp.float32)
        return down + jnp.dot(field, band, preferred_element_type=jnp.float32)

    return one(field_re), one(field_im)


def back(band, chi_re, chi_im):
    lap_re, lap_im = laplacian(band, chi_re, chi_im)
    lap2_re, lap2_im = laplacian(band, lap_re.astype(jnp.bfloat16), lap_im.astype(jnp.bfloat16))
    square_re = damping * damping - turning * turning
    square_im = 2.0 * damping * turning
    spread_re = chi_re.astype(jnp.float32) + (2.0 * damping) * lap_re + (2.0 * turning) * lap_im
    spread_im = chi_im.astype(jnp.float32) + (2.0 * damping) * lap_im - (2.0 * turning) * lap_re
    spread_re = spread_re + square_re * lap2_re + square_im * lap2_im
    spread_im = spread_im + square_re * lap2_im - square_im * lap2_re
    return spread_re, spread_im


def group_kernel(pick_ref, exit_ref, come_ref, win_ref, spread_ref, leave_ref, chi_ref, band_ref):
    step = pl.program_id(0)

    @pl.when(step == 0)
    def _():
        band_ref[...] = second_difference(band_ref.shape[0])

        @pl.when(pick_ref[1] == 1)
        def _():
            chi_ref[...] = exit_ref[0]

        @pl.when(pick_ref[1] == 0)
        def _():
            chi_ref[...] = come_ref[...]

    spread_re, spread_im = back(band_ref[...], chi_ref[0], chi_ref[1])
    spread_ref[0, 0] = spread_re.astype(jnp.bfloat16)
    spread_ref[0, 1] = spread_im.astype(jnp.bfloat16)
    win_re = jnp.log(win_ref[0, 0].astype(jnp.float32)) * (1.0 / code_gain)
    win_im = jnp.log(win_ref[0, 1].astype(jnp.float32)) * (1.0 / code_gain)
    chi_ref[0] = (win_re * spread_re + win_im * spread_im).astype(jnp.bfloat16)
    chi_ref[1] = (win_re * spread_im - win_im * spread_re).astype(jnp.bfloat16)

    @pl.when(step == pl.num_programs(0) - 1)
    def _():
        leave_ref[...] = chi_ref[...]


def through_group(pick, exits, come, windows):
    count, _, window, _ = windows.shape
    wave = (2, window, window)
    last = count - 1
    return pl.pallas_call(
        group_kernel,
        grid_spec=pltpu.PrefetchScalarGridSpec(
            num_scalar_prefetch=1,
            grid=(count,),
            in_specs=[
                pl.BlockSpec((1,) + wave, lambda k, pick: (pick[0], 0, 0, 0)),
                pl.BlockSpec(wave, lambda k, pick: (0, 0, 0)),
                pl.BlockSpec((1,) + wave, lambda k, pick: (last - k, 0, 0, 0)),
            ],
            out_specs=[
                pl.BlockSpec((1,) + wave, lambda k, pick: (last - k, 0, 0, 0)),
                pl.BlockSpec(wave, lambda k, pick: (0, 0, 0)),
            ],
            scratch_shapes=[
                pltpu.VMEM(wave, jnp.bfloat16),
                pltpu.VMEM((window, window), jnp.bfloat16),
            ],
        ),
        out_shape=[
            jax.ShapeDtypeStruct(windows.shape, jnp.bfloat16),
            jax.ShapeDtypeStruct(wave, jnp.bfloat16),
        ],
        compiler_params=params(),
    )(pick, exits, come, windows)


def gradient_kernel(corner_ref, place_ref, wave_ref, spread_ref, mine_ref, other_ref, sum_ref):
    position = pl.program_id(0)
    rows = mine_ref.shape[1]
    width = mine_ref.shape[2]
    window = wave_ref.shape[-1]

    @pl.when(position == 0)
    def _():
        sum_ref[...] = jnp.zeros_like(sum_ref)

    tall, wide, row_to, row_by, col_to, col_by = around(corner_ref, position, window)
    wave_re = wave_ref[0, 0].astype(jnp.float32)
    wave_im = wave_ref[0, 1].astype(jnp.float32)
    spread_re = spread_ref[0, 0].astype(jnp.float32)
    spread_im = spread_ref[0, 1].astype(jnp.float32)
    parts = (
        wave_re * spread_re + wave_im * spread_im,
        wave_re * spread_im - wave_im * spread_re,
    )
    below = jnp.zeros((tall - window, window), jnp.float32)
    beside = jnp.zeros((tall, wide - window), jnp.float32)
    for part in range(2):
        box = pltpu.roll(jnp.concatenate([parts[part], below], axis=0), row_by, 0)
        box = pltpu.roll(jnp.concatenate([box, beside], axis=1), col_by, 1)
        sum_ref[part, pl.ds(row_to, tall), pl.ds(col_to, wide)] += box

    @pl.when(position == pl.num_programs(0) - 1)
    def _():
        here = pl.multiple_of(place_ref[0] * rows, rows)
        there = pl.multiple_of((1 - place_ref[0]) * rows, rows)
        mine_ref[...] = sum_ref[:, pl.ds(here, rows), :width]
        other_ref[...] = sum_ref[:, pl.ds(there, rows), :width].astype(jnp.bfloat16)


def gradient(offsets, place, waves, spreads, half):
    count, _, window, _ = waves.shape
    block = pl.BlockSpec((1, 2, window, window), lambda p, *_: (p, 0, 0, 0))
    whole = pl.BlockSpec(half, lambda p, *_: (0, 0, 0))
    return pl.pallas_call(
        gradient_kernel,
        grid_spec=pltpu.PrefetchScalarGridSpec(
            num_scalar_prefetch=2,
            grid=(count,),
            in_specs=[block, block],
            out_specs=[whole, whole],
            scratch_shapes=[padded(half[1], half[2])],
        ),
        out_shape=[
            jax.ShapeDtypeStruct(half, jnp.float32),
            jax.ShapeDtypeStruct(half, jnp.bfloat16),
        ],
        compiler_params=params(),
    )(offsets, place, waves, spreads)


def on_device(obj_amp, obj_phase, forward_waves, exit_adjoint, offsets):
    sections = lax.axis_size("sec")
    section = lax.axis_index("sec")
    place = lax.axis_index("scan").astype(jnp.int32).reshape(1)
    position_count, _, window, _ = exit_adjoint.shape
    group = position_count
    group_count = sections // group
    swap = [(0, 1), (1, 0)]
    groups = [[first + i for i in range(group)] for first in range(0, sections, group)]

    trans_re = obj_amp[0] * jnp.cos(obj_phase[0])
    trans_im = obj_amp[0] * jnp.sin(obj_phase[0])
    mine = jnp.exp(code_gain * jnp.stack([trans_re, trans_im])).astype(jnp.bfloat16)
    other = lax.ppermute(mine, "scan", swap)
    cut = cut_windows(offsets, place, mine, other, window)
    windows = lax.all_to_all(cut, "sec", 0, 0, axis_index_groups=groups, tiled=True)

    at_end = (section >= sections - group).astype(jnp.int32)
    pick = jnp.stack([section % group, jnp.int32(1)])
    come = jnp.zeros((2, window, window), jnp.bfloat16)
    for stage in range(group_count):
        spreads, leave = through_group(pick, exit_adjoint, come, windows)
        if stage < group_count - 1:
            come = lax.ppermute(leave, "sec", [(s, s - group) for s in range(group, sections)])
            pick = jnp.stack([section % group, at_end])

    spreads = lax.all_to_all(spreads, "sec", 0, 0, axis_index_groups=groups, tiled=True)
    own, away = gradient(offsets, place, forward_waves[0], spreads, mine.shape)
    reduced = own + lax.ppermute(away, "scan", swap).astype(jnp.float32)
    return reduced[None]


def solution(mesh):
    in_specs = (
        P("sec", "scan", None),
        P("sec", "scan", None),
        P("sec", "scan", None, None, None),
        P("scan", None, None, None),
        P("scan", None),
    )
    out_specs = P("sec", None, "scan", None)
    return jax.shard_map(
        on_device, mesh=mesh, in_specs=in_specs, out_specs=out_specs, check_vma=False
    )
```

```python
import functools
import math

import jax
import jax.numpy as jnp
from jax import lax
from jax.experimental import pallas as pl
from jax.experimental.pallas import tpu as pltpu
from jax.sharding import PartitionSpec as P

SUBSTEPS = 2
damping = 0.0005
turning = 0.011
code_gain = 83.0
chunk_count = 2
f32 = jnp.float32
bf16 = jnp.bfloat16


def call(kernel, out_shape, prefetch=0, scratch=(), flops=0, transcendentals=0):
    def run(*args):
        moved = sum(a.size * a.dtype.itemsize for a in jax.tree.leaves((args, out_shape)))
        vmem = pl.BlockSpec(memory_space=pltpu.VMEM)
        return pl.pallas_call(
            kernel,
            grid_spec=pltpu.PrefetchScalarGridSpec(
                num_scalar_prefetch=prefetch,
                grid=(1,),
                in_specs=[vmem] * (len(args) - prefetch),
                out_specs=jax.tree.map(lambda _: vmem, out_shape),
                scratch_shapes=list(scratch),
            ),
            out_shape=out_shape,
            cost_estimate=pl.CostEstimate(flops=flops, bytes_accessed=moved, transcendentals=transcendentals),
            compiler_params=pltpu.CompilerParams(vmem_limit_bytes=32 * 2**20),
        )(*args)

    return run


def code_kernel(amp_ref, phase_ref, *code_refs):
    rows = code_refs[0].shape[1]
    for chunk, code_ref in enumerate(code_refs):
        amp = amp_ref[pl.ds(chunk * rows, rows), :]
        half = 0.5 * phase_ref[pl.ds(chunk * rows, rows), :]
        square = half * half
        sine = jnp.full_like(half, 1.0 / math.factorial(13))
        cosine = jnp.full_like(half, 1.0 / math.factorial(12))
        for power in (11, 9, 7, 5, 3, 1):
            sign = -1.0 if power % 4 == 3 else 1.0
            sine = sine * square + sign / math.factorial(power)
            cosine = cosine * square + sign / math.factorial(power - 1)
        sine = sine * half
        code_ref[0] = jnp.exp((code_gain * amp) * (1.0 - 2.0 * sine * sine)).astype(bf16)
        code_ref[1] = jnp.exp((code_gain * amp) * (2.0 * sine * cosine)).astype(bf16)


def first_masks(corner_ref, position, place, base, shape):
    row = lax.broadcasted_iota(jnp.int32, shape, 0) + base
    col = lax.broadcasted_iota(jnp.int32, shape, 1)
    at_first = (row >= corner_ref[position, 0]).astype(jnp.int32)
    return at_first != place, col >= corner_ref[position, 1]


def cut_kernel(base, corner_ref, place_ref, mine_ref, other_ref, win_ref):
    count, _, rows, window = win_ref.shape
    place = place_ref[0]

    def one(position, _):
        in_mine, in_left = first_masks(corner_ref, position, place, base, (rows, window))
        for part in range(2):
            left = jnp.where(in_mine, mine_ref[part, :, :window].astype(f32), other_ref[part, :, :window].astype(f32))
            right = jnp.where(in_mine, mine_ref[part, :, window:].astype(f32), other_ref[part, :, window:].astype(f32))
            win_ref[position, part] = jnp.where(in_left, left, right).astype(bf16)
        return 0

    lax.fori_loop(0, count, one, 0)


def turned(wave, row_at, col_at):
    window = wave.shape[-1]
    wave = pltpu.roll(wave.astype(f32), lax.rem(row_at, window), 0)
    return pltpu.roll(wave, lax.rem(col_at, window), 1).astype(bf16)


def second_difference(size, break_at):
    row = lax.broadcasted_iota(jnp.int32, (size, size), 0)
    col = lax.broadcasted_iota(jnp.int32, (size, size), 1)
    start = lax.rem(break_at, size)
    before = (lax.rem(row - col + size, size) == 1) & (row != start)
    after = (lax.rem(col - row + size, size) == 1) & (col != start)
    return jnp.where(row == col, -2.0, jnp.where(before | after, 1.0, 0.0)).astype(bf16)


def ready_kernel(corner_ref, pick_ref, exit_ref, start_ref, down_ref, across_ref):
    own = pick_ref[0]
    row_at = corner_ref[own, 0]
    col_at = corner_ref[own, 1]
    size = start_ref.shape[-1]
    for part in range(2):
        start_ref[part] = turned(exit_ref[own, part], row_at, col_at)
    down_ref[...] = second_difference(size, row_at)
    across_ref[...] = second_difference(size, col_at)


def turn_kernel(corner_ref, wave_ref, turned_ref):
    count = wave_ref.shape[0]

    def one(position, _):
        for part in range(2):
            turned_ref[position, part] = turned(
                wave_ref[position, part], corner_ref[position, 0], corner_ref[position, 1]
            )
        return 0

    lax.fori_loop(0, count, one, 0)


def back(down, across, chi_re, chi_im):
    def laplacian(field):
        rows = jnp.dot(down, field, preferred_element_type=f32)
        return rows + jnp.dot(field, across, preferred_element_type=f32)

    lap_re = laplacian(chi_re)
    lap_im = laplacian(chi_im)
    lap2_re = laplacian(lap_re.astype(bf16))
    lap2_im = laplacian(lap_im.astype(bf16))
    square_re = damping * damping - turning * turning
    square_im = 2.0 * damping * turning
    spread_re = chi_re.astype(f32) + (2.0 * damping) * lap_re + (2.0 * turning) * lap_im
    spread_im = chi_im.astype(f32) + (2.0 * damping) * lap_im - (2.0 * turning) * lap_re
    spread_re = spread_re + square_re * lap2_re + square_im * lap2_im
    spread_im = spread_im + square_re * lap2_im - square_im * lap2_re
    return spread_re, spread_im


def group_kernel(pick_ref, start_ref, come_ref, down_ref, across_ref, *refs):
    win_refs = refs[:chunk_count]
    spread_refs = refs[chunk_count : 2 * chunk_count]
    leave_ref = refs[2 * chunk_count]
    count, _, rows, _ = win_refs[0].shape
    down = down_ref[...]
    across = across_ref[...]
    at_end = jnp.full(start_ref.shape[1:], pick_ref[1], jnp.int32) == 1
    chi_re, chi_im = (
        jnp.where(at_end, start_ref[part].astype(f32), come_ref[part].astype(f32)).astype(bf16) for part in range(2)
    )
    for layer in range(count - 1, -1, -1):
        spread_re, spread_im = back(down, across, chi_re, chi_im)
        out_re, out_im = [], []
        for chunk in range(chunk_count):
            here = slice(chunk * rows, (chunk + 1) * rows)
            part_re, part_im = spread_re[here], spread_im[here]
            spread_refs[chunk][layer, 0] = part_re.astype(bf16)
            spread_refs[chunk][layer, 1] = part_im.astype(bf16)
            win_re = jnp.log(win_refs[chunk][layer, 0].astype(f32)) * (1.0 / code_gain)
            win_im = jnp.log(win_refs[chunk][layer, 1].astype(f32)) * (1.0 / code_gain)
            out_re.append((win_re * part_re + win_im * part_im).astype(bf16))
            out_im.append((win_re * part_im - win_im * part_re).astype(bf16))
        chi_re = jnp.concatenate(out_re, axis=0)
        chi_im = jnp.concatenate(out_im, axis=0)
    leave_ref[0] = chi_re
    leave_ref[1] = chi_im


def gradient_kernel(base, corner_ref, place_ref, wave_ref, spread_ref, own_ref, away_ref):
    count, _, rows, window = spread_ref.shape
    tall = 16
    place = place_ref[0]

    def one(block, _):
        at = pl.multiple_of(block * tall, tall)
        sums = [jnp.zeros((tall, window), f32) for _ in range(8)]
        for position in range(count):
            in_mine, in_left = first_masks(corner_ref, position, place, base + at, (tall, window))
            wave_re, wave_im = (wave_ref[position, part, pl.ds(base + at, tall), :].astype(f32) for part in range(2))
            spread_re, spread_im = (spread_ref[position, part, pl.ds(at, tall), :].astype(f32) for part in range(2))
            parts = (
                wave_re * spread_re + wave_im * spread_im,
                wave_re * spread_im - wave_im * spread_re,
            )
            for part in range(2):
                left = jnp.where(in_left, parts[part], 0.0)
                right = jnp.where(in_left, 0.0, parts[part])
                for side, value in enumerate((left, right)):
                    sums[4 * part + side] += jnp.where(in_mine, value, 0.0)
                    sums[4 * part + 2 + side] += jnp.where(in_mine, 0.0, value)
        for part in range(2):
            for side in range(2):
                cols = pl.ds(side * window, window)
                own_ref[part, pl.ds(at, tall), cols] = sums[4 * part + side]
                away_ref[part, pl.ds(at, tall), cols] = sums[4 * part + 2 + side].astype(bf16)
        return 0

    lax.fori_loop(0, rows // tall, one, 0)


def finish_kernel(*refs):
    out_ref = refs[-1]
    rows = refs[0].shape[1]
    for chunk in range(chunk_count):
        own_ref, come_ref = refs[2 * chunk : 2 * chunk + 2]
        out_ref[:, pl.ds(chunk * rows, rows), :] = own_ref[...] + come_ref[...].astype(f32)


def shape_of(dims, dtype):
    return jax.ShapeDtypeStruct(dims, dtype)


def on_device(obj_amp, obj_phase, forward_waves, exit_adjoint, offsets):
    sections = lax.axis_size("sec")
    section = lax.axis_index("sec")
    place = lax.axis_index("scan").astype(jnp.int32).reshape(1)
    count, _, window, _ = exit_adjoint.shape
    _, half, width = obj_amp.shape
    swap = [(0, 1), (1, 0)]
    groups = [[first + i for i in range(count)] for first in range(0, sections, count)]
    group_count = sections // count
    rows = half // chunk_count
    chunks = range(chunk_count)
    piece = (2, rows, width)
    part = (count, 2, rows, window)
    wave = (2, window, window)
    flops = 8 * 2 * window**3

    def all_to_all(value):
        return lax.all_to_all(value, "sec", 0, 0, axis_index_groups=groups, tiled=True)

    own = section % count
    pick = jnp.stack([own, jnp.int32(1)])
    mine = call(code_kernel, [shape_of(piece, bf16)] * chunk_count)(obj_amp[0], obj_phase[0])
    other = [lax.ppermute(mine[c], "scan", swap) for c in chunks]
    windows = []
    for c in chunks:
        cut = call(functools.partial(cut_kernel, c * rows), shape_of(part, bf16), prefetch=2)
        windows.append(all_to_all(cut(offsets, place, mine[c], other[c])))
    ready = call(ready_kernel, [shape_of(wave, bf16)] + [shape_of((window, window), bf16)] * 2, prefetch=2)
    start, down, across = ready(offsets, pick, exit_adjoint)
    waves = call(turn_kernel, shape_of(forward_waves.shape[1:], bf16), prefetch=1)(offsets, forward_waves[0])

    at_end = (section >= sections - count).astype(jnp.int32)
    come = start
    through = call(
        group_kernel,
        [shape_of(part, bf16)] * chunk_count + [shape_of(wave, bf16)],
        prefetch=1,
        flops=count * flops,
    )
    for stage in range(group_count):
        *spreads, leave = through(pick, start, come, down, across, *windows)
        if stage < group_count - 1:
            come = lax.ppermute(leave, "sec", [(s, s - count) for s in range(count, sections)])
            pick = jnp.stack([own, at_end])

    spreads = [all_to_all(spreads[c]) for c in chunks]
    sums = []
    for c in chunks:
        gradient = call(
            functools.partial(gradient_kernel, c * rows), [shape_of(piece, f32), shape_of(piece, bf16)], prefetch=2
        )
        keep, away = gradient(offsets, place, waves, spreads[c])
        sums += [keep, lax.ppermute(away, "scan", swap)]
    return call(finish_kernel, shape_of((2, half, width), f32))(*sums)[None]


def solution(mesh):
    in_specs = (
        P("sec", "scan", None),
        P("sec", "scan", None),
        P("sec", "scan", None, None, None),
        P("scan", None, None, None),
        P("scan", None),
    )
    out_specs = P("sec", None, "scan", None)
    return jax.shard_map(
        on_device, mesh=mesh, in_specs=in_specs, out_specs=out_specs, check_vma=False
    )
```

```python
import functools
import math

import jax
import jax.numpy as jnp
from jax import lax
from jax.experimental import pallas as pl
from jax.experimental.pallas import tpu as pltpu
from jax.sharding import PartitionSpec as P

SUBSTEPS = 2
damping = 0.0005
turning = 0.011
code_gain = 83.0
chunk_count = 2
f32 = jnp.float32
bf16 = jnp.bfloat16


def call(kernel, out_shape, prefetch=0, scratch=(), flops=0, transcendentals=0):
    def run(*args):
        moved = sum(a.size * a.dtype.itemsize for a in jax.tree.leaves((args, out_shape)))
        vmem = pl.BlockSpec(memory_space=pltpu.VMEM)
        return pl.pallas_call(
            kernel,
            grid_spec=pltpu.PrefetchScalarGridSpec(
                num_scalar_prefetch=prefetch,
                grid=(1,),
                in_specs=[vmem] * (len(args) - prefetch),
                out_specs=jax.tree.map(lambda _: vmem, out_shape),
                scratch_shapes=list(scratch),
            ),
            out_shape=out_shape,
            cost_estimate=pl.CostEstimate(flops=flops, bytes_accessed=moved, transcendentals=transcendentals),
            compiler_params=pltpu.CompilerParams(vmem_limit_bytes=32 * 2**20),
        )(*args)

    return run


def code_kernel(amp_ref, phase_ref, *code_refs):
    rows = code_refs[0].shape[1]
    for chunk, code_ref in enumerate(code_refs):
        amp = amp_ref[pl.ds(chunk * rows, rows), :]
        half = 0.5 * phase_ref[pl.ds(chunk * rows, rows), :]
        square = half * half
        sine = jnp.full_like(half, 1.0 / math.factorial(13))
        cosine = jnp.full_like(half, 1.0 / math.factorial(12))
        for power in (11, 9, 7, 5, 3, 1):
            sign = -1.0 if power % 4 == 3 else 1.0
            sine = sine * square + sign / math.factorial(power)
            cosine = cosine * square + sign / math.factorial(power - 1)
        sine = sine * half
        code_ref[0] = jnp.exp((code_gain * amp) * (1.0 - 2.0 * sine * sine)).astype(bf16)
        code_ref[1] = jnp.exp((code_gain * amp) * (2.0 * sine * cosine)).astype(bf16)


def first_masks(corner_ref, position, place, base, shape):
    row = lax.broadcasted_iota(jnp.int32, shape, 0) + base
    col = lax.broadcasted_iota(jnp.int32, shape, 1)
    at_first = (row >= corner_ref[position, 0]).astype(jnp.int32)
    return at_first != place, col >= corner_ref[position, 1]


def cut_kernel(base, corner_ref, place_ref, pick_ref, mine_ref, other_ref, *win_refs):
    _, rows, window = win_refs[0].shape
    place = place_ref[0]
    for apart, win_ref in enumerate(win_refs):
        in_mine, in_left = first_masks(corner_ref, pick_ref[0] ^ apart, place, base, (rows, window))
        for part in range(2):
            left = jnp.where(in_mine, mine_ref[part, :, :window].astype(f32), other_ref[part, :, :window].astype(f32))
            right = jnp.where(in_mine, mine_ref[part, :, window:].astype(f32), other_ref[part, :, window:].astype(f32))
            win_ref[part] = jnp.where(in_left, left, right).astype(bf16)


def turned(wave, row_at, col_at):
    window = wave.shape[-1]
    wave = pltpu.roll(wave.astype(f32), lax.rem(row_at, window), 0)
    return pltpu.roll(wave, lax.rem(col_at, window), 1).astype(bf16)


def second_difference(size, break_at):
    row = lax.broadcasted_iota(jnp.int32, (size, size), 0)
    col = lax.broadcasted_iota(jnp.int32, (size, size), 1)
    start = lax.rem(break_at, size)
    before = (lax.rem(row - col + size, size) == 1) & (row != start)
    after = (lax.rem(col - row + size, size) == 1) & (col != start)
    return jnp.where(row == col, -2.0, jnp.where(before | after, 1.0, 0.0)).astype(bf16)


def ready_kernel(corner_ref, pick_ref, exit_ref, start_ref, down_ref, across_ref):
    own = pick_ref[0]
    row_at = corner_ref[own, 0]
    col_at = corner_ref[own, 1]
    size = start_ref.shape[-1]
    for part in range(2):
        start_ref[part] = turned(exit_ref[own, part], row_at, col_at)
    down_ref[...] = second_difference(size, row_at)
    across_ref[...] = second_difference(size, col_at)


def turn_kernel(corner_ref, wave_ref, turned_ref):
    count = wave_ref.shape[0]

    def one(position, _):
        for part in range(2):
            turned_ref[position, part] = turned(
                wave_ref[position, part], corner_ref[position, 0], corner_ref[position, 1]
            )
        return 0

    lax.fori_loop(0, count, one, 0)


def back(down, across, chi_re, chi_im):
    def laplacian(field):
        rows = jnp.dot(down, field, preferred_element_type=f32)
        return rows + jnp.dot(field, across, preferred_element_type=f32)

    lap_re = laplacian(chi_re)
    lap_im = laplacian(chi_im)
    lap2_re = laplacian(lap_re.astype(bf16))
    lap2_im = laplacian(lap_im.astype(bf16))
    square_re = damping * damping - turning * turning
    square_im = 2.0 * damping * turning
    spread_re = chi_re.astype(f32) + (2.0 * damping) * lap_re + (2.0 * turning) * lap_im
    spread_im = chi_im.astype(f32) + (2.0 * damping) * lap_im - (2.0 * turning) * lap_re
    spread_re = spread_re + square_re * lap2_re + square_im * lap2_im
    spread_im = spread_im + square_re * lap2_im - square_im * lap2_re
    return spread_re, spread_im


def group_kernel(pick_ref, start_ref, come_ref, down_ref, across_ref, *refs):
    win_refs, refs = refs[: len(refs) // 2 - 1], refs[len(refs) // 2 - 1 :]
    *spread_refs, leave_ref, held_ref, kept_ref = refs
    count, _, window, _ = held_ref.shape
    rows = window // chunk_count
    own = pick_ref[0]
    for apart in range(count):
        for chunk in range(chunk_count):
            here = slice(chunk * rows, (chunk + 1) * rows)
            held_ref[own ^ apart, :, here] = win_refs[apart * chunk_count + chunk][...]
    down = down_ref[...]
    across = across_ref[...]
    at_end = jnp.full(start_ref.shape[1:], pick_ref[1], jnp.int32) == 1
    chi_re, chi_im = (
        jnp.where(at_end, start_ref[part].astype(f32), come_ref[part].astype(f32)).astype(bf16) for part in range(2)
    )
    for layer in range(count - 1, -1, -1):
        spread_re, spread_im = back(down, across, chi_re, chi_im)
        kept_ref[layer, 0] = spread_re.astype(bf16)
        kept_ref[layer, 1] = spread_im.astype(bf16)
        win_re = jnp.log(held_ref[layer, 0].astype(f32)) * (1.0 / code_gain)
        win_im = jnp.log(held_ref[layer, 1].astype(f32)) * (1.0 / code_gain)
        chi_re = (win_re * spread_re + win_im * spread_im).astype(bf16)
        chi_im = (win_re * spread_im - win_im * spread_re).astype(bf16)
    leave_ref[0] = chi_re
    leave_ref[1] = chi_im
    for apart in range(count):
        for chunk in range(chunk_count):
            here = slice(chunk * rows, (chunk + 1) * rows)
            spread_refs[apart * chunk_count + chunk][...] = kept_ref[own ^ apart, :, here]


def gradient_kernel(base, corner_ref, place_ref, pick_ref, wave_ref, *refs):
    *spread_refs, own_ref, away_ref = refs
    _, rows, window = spread_refs[0].shape
    tall = 16
    place = place_ref[0]
    own = pick_ref[0]

    def one(block, _):
        at = pl.multiple_of(block * tall, tall)
        sums = [jnp.zeros((tall, window), f32) for _ in range(8)]
        for apart, spread_ref in enumerate(spread_refs):
            position = own ^ apart
            in_mine, in_left = first_masks(corner_ref, position, place, base + at, (tall, window))
            wave_re, wave_im = (wave_ref[position, part, pl.ds(base + at, tall), :].astype(f32) for part in range(2))
            spread_re, spread_im = (spread_ref[part, pl.ds(at, tall), :].astype(f32) for part in range(2))
            parts = (
                wave_re * spread_re + wave_im * spread_im,
                wave_re * spread_im - wave_im * spread_re,
            )
            for part in range(2):
                left = jnp.where(in_left, parts[part], 0.0)
                right = jnp.where(in_left, 0.0, parts[part])
                for side, value in enumerate((left, right)):
                    sums[4 * part + side] += jnp.where(in_mine, value, 0.0)
                    sums[4 * part + 2 + side] += jnp.where(in_mine, 0.0, value)
        for part in range(2):
            for side in range(2):
                cols = pl.ds(side * window, window)
                own_ref[part, pl.ds(at, tall), cols] = sums[4 * part + side]
                away_ref[part, pl.ds(at, tall), cols] = sums[4 * part + 2 + side].astype(bf16)
        return 0

    lax.fori_loop(0, rows // tall, one, 0)


def finish_kernel(*refs):
    out_ref = refs[-1]
    rows = refs[0].shape[1]
    for chunk in range(chunk_count):
        own_ref, come_ref = refs[2 * chunk : 2 * chunk + 2]
        out_ref[:, pl.ds(chunk * rows, rows), :] = own_ref[...] + come_ref[...].astype(f32)


def shape_of(dims, dtype):
    return jax.ShapeDtypeStruct(dims, dtype)


def on_device(obj_amp, obj_phase, forward_waves, exit_adjoint, offsets):
    sections = lax.axis_size("sec")
    section = lax.axis_index("sec")
    place = lax.axis_index("scan").astype(jnp.int32).reshape(1)
    count, _, window, _ = exit_adjoint.shape
    _, half, width = obj_amp.shape
    swap = [(0, 1), (1, 0)]
    group_count = sections // count
    rows = half // chunk_count
    chunks = range(chunk_count)
    piece = (2, rows, width)
    part = (2, rows, window)
    wave = (2, window, window)
    flops = 8 * 2 * window**3

    def exchange(values):
        order = sorted(range(1, count), key=lambda apart: (apart == 1, apart % 2, apart))
        got = list(values)
        for apart in order:
            got[apart] = lax.ppermute(values[apart], "sec", [(s, s ^ apart) for s in range(sections)])
        return got

    own = section % count
    pick = jnp.stack([own, jnp.int32(1)])
    mine = call(code_kernel, [shape_of(piece, bf16)] * chunk_count)(obj_amp[0], obj_phase[0])
    other = [lax.ppermute(mine[c], "scan", swap) for c in chunks]
    windows = []
    for c in chunks:
        cut = call(functools.partial(cut_kernel, c * rows), [shape_of(part, bf16)] * count, prefetch=3)
        windows.append(exchange(cut(offsets, place, pick, mine[c], other[c])))
    ready = call(ready_kernel, [shape_of(wave, bf16)] + [shape_of((window, window), bf16)] * 2, prefetch=2)
    start, down, across = ready(offsets, pick, exit_adjoint)
    waves = call(turn_kernel, shape_of(forward_waves.shape[1:], bf16), prefetch=1)(offsets, forward_waves[0])

    at_end = (section >= sections - count).astype(jnp.int32)
    come = start
    through = call(
        group_kernel,
        [shape_of(part, bf16)] * (chunk_count * count) + [shape_of(wave, bf16)],
        prefetch=1,
        scratch=[pltpu.VMEM((count,) + wave, bf16)] * 2,
        flops=count * flops,
    )
    stage_windows = [windows[c][apart] for apart in range(count) for c in chunks]
    for stage in range(group_count):
        *spreads, leave = through(pick, start, come, down, across, *stage_windows)
        if stage < group_count - 1:
            come = lax.ppermute(leave, "sec", [(s, s - count) for s in range(count, sections)])
            pick = jnp.stack([own, at_end])

    spreads = [exchange(spreads[c::chunk_count]) for c in chunks]
    sums = []
    for c in chunks:
        gradient = call(
            functools.partial(gradient_kernel, c * rows), [shape_of(piece, f32), shape_of(piece, bf16)], prefetch=3
        )
        keep, away = gradient(offsets, place, pick, waves, *spreads[c])
        sums += [keep, lax.ppermute(away, "scan", swap)]
    return call(finish_kernel, shape_of((2, half, width), f32))(*sums)[None]


def solution(mesh):
    in_specs = (
        P("sec", "scan", None),
        P("sec", "scan", None),
        P("sec", "scan", None, None, None),
        P("scan", None, None, None),
        P("scan", None),
    )
    out_specs = P("sec", None, "scan", None)
    return jax.shard_map(
        on_device, mesh=mesh, in_specs=in_specs, out_specs=out_specs, check_vma=False
    )
```

```python
import functools
import math

import jax
import jax.numpy as jnp
from jax import lax
from jax.experimental import pallas as pl
from jax.experimental.pallas import tpu as pltpu
from jax.sharding import PartitionSpec as P

SUBSTEPS = 2
damping = 0.0005
turning = 0.011
code_gain = 83.0
chunk_count = 2
f32 = jnp.float32
bf16 = jnp.bfloat16


def call(kernel, out_shape, prefetch=0, scratch=(), flops=0, grant=12, space=pltpu.VMEM):
    def run(*args):
        moved = sum(a.size * a.dtype.itemsize for a in jax.tree.leaves((args, out_shape)))
        vmem = pl.BlockSpec(memory_space=pltpu.VMEM)
        return pl.pallas_call(
            kernel,
            grid_spec=pltpu.PrefetchScalarGridSpec(
                num_scalar_prefetch=prefetch,
                grid=(1,),
                in_specs=[pl.BlockSpec(memory_space=space)] * (len(args) - prefetch),
                out_specs=jax.tree.map(lambda _: vmem, out_shape),
                scratch_shapes=list(scratch),
            ),
            out_shape=out_shape,
            cost_estimate=pl.CostEstimate(flops=flops, bytes_accessed=moved, transcendentals=0),
            compiler_params=pltpu.CompilerParams(vmem_limit_bytes=grant * 2**20),
        )(*args)

    return run


def code_kernel(amp_hbm, phase_hbm, *refs):
    *code_refs, amp_ref, phase_ref, sems = refs
    rows = code_refs[0].shape[1]
    copies = []
    for piece in range(sems.shape[0]):
        tall = amp_ref.shape[0] // sems.shape[0]
        here = pl.ds(piece * tall, tall)
        for side, (source, target) in enumerate(((amp_hbm, amp_ref), (phase_hbm, phase_ref))):
            copies.append(pltpu.make_async_copy(source.at[here], target.at[here], sems.at[piece, side]))
            copies[-1].start()
    share = len(copies) // len(code_refs)
    for chunk, code_ref in enumerate(code_refs):
        for copy in copies[chunk * share : (chunk + 1) * share]:
            copy.wait()
        amp = amp_ref[pl.ds(chunk * rows, rows), :]
        half = 0.5 * phase_ref[pl.ds(chunk * rows, rows), :]
        square = half * half
        sine = jnp.full_like(half, 1.0 / math.factorial(13))
        cosine = jnp.full_like(half, 1.0 / math.factorial(12))
        for power in (11, 9, 7, 5, 3, 1):
            sign = -1.0 if power % 4 == 3 else 1.0
            sine = sine * square + sign / math.factorial(power)
            cosine = cosine * square + sign / math.factorial(power - 1)
        sine = sine * half
        code_ref[0] = jnp.exp((code_gain * amp) * (1.0 - 2.0 * sine * sine)).astype(bf16)
        code_ref[1] = jnp.exp((code_gain * amp) * (2.0 * sine * cosine)).astype(bf16)


def first_masks(corner_ref, position, place, base, shape):
    row = lax.broadcasted_iota(jnp.int32, shape, 0) + base
    col = lax.broadcasted_iota(jnp.int32, shape, 1)
    at_first = (row >= corner_ref[position, 0]).astype(jnp.int32)
    return at_first != place, col >= corner_ref[position, 1]


def cut_kernel(base, corner_ref, place_ref, pick_ref, *refs):
    slices = (refs[:2], refs[2:4])
    place = place_ref[0]
    for apart, win_ref in enumerate(refs[4:]):
        _, _, rows, window = win_ref.shape
        in_mine, in_left = first_masks(corner_ref, pick_ref[0] ^ (2 * apart), place, base, (rows, window))
        for core, (mine_ref, other_ref) in enumerate(slices):
            for part in range(2):
                left, right = (
                    jnp.where(in_mine, mine_ref[part, :, cols].astype(f32), other_ref[part, :, cols].astype(f32))
                    for cols in (slice(0, window), slice(window, 2 * window))
                )
                win_ref[core, part] = jnp.where(in_left, left, right).astype(bf16)


def turned(wave, row_at, col_at):
    window = wave.shape[-1]
    wave = pltpu.roll(wave.astype(f32), lax.rem(row_at, window), 0)
    return pltpu.roll(wave, lax.rem(col_at, window), 1).astype(bf16)


def second_difference(size, break_at):
    row = lax.broadcasted_iota(jnp.int32, (size, size), 0)
    col = lax.broadcasted_iota(jnp.int32, (size, size), 1)
    start = lax.rem(break_at, size)
    before = (lax.rem(row - col + size, size) == 1) & (row != start)
    after = (lax.rem(col - row + size, size) == 1) & (col != start)
    return jnp.where(row == col, -2.0, jnp.where(before | after, 1.0, 0.0)).astype(bf16)


def ready_kernel(corner_ref, pick_ref, exit_ref, start_ref, down_ref, across_ref):
    own = pick_ref[0]
    row_at = corner_ref[own, 0]
    col_at = corner_ref[own, 1]
    size = start_ref.shape[-1]
    for part in range(2):
        start_ref[part] = turned(exit_ref[own, part], row_at, col_at)
    down_ref[...] = second_difference(size, row_at)
    across_ref[...] = second_difference(size, col_at)


def turn_kernel(corner_ref, wave_ref, turned_ref):
    count = wave_ref.shape[0]

    def one(position, _):
        for part in range(2):
            turned_ref[position, part] = turned(
                wave_ref[position, part], corner_ref[position, 0], corner_ref[position, 1]
            )
        return 0

    lax.fori_loop(0, count, one, 0)


def back(down, across, chi_re, chi_im):
    def laplacian(field):
        rows = jnp.dot(down, field, preferred_element_type=f32)
        return rows + jnp.dot(field, across, preferred_element_type=f32)

    lap_re = laplacian(chi_re)
    lap_im = laplacian(chi_im)
    lap2_re = laplacian(lap_re.astype(bf16))
    lap2_im = laplacian(lap_im.astype(bf16))
    square_re = damping * damping - turning * turning
    square_im = 2.0 * damping * turning
    spread_re = chi_re.astype(f32) + (2.0 * damping) * lap_re + (2.0 * turning) * lap_im
    spread_im = chi_im.astype(f32) + (2.0 * damping) * lap_im - (2.0 * turning) * lap_re
    spread_re = spread_re + square_re * lap2_re + square_im * lap2_im
    spread_im = spread_im + square_re * lap2_im - square_im * lap2_re
    return spread_re, spread_im


def group_kernel(pick_ref, start_ref, come_ref, down_ref, across_ref, *refs):
    win_refs, refs = refs[: len(refs) // 2 - 1], refs[len(refs) // 2 - 1 :]
    *spread_refs, leave_ref, held_ref, kept_ref = refs
    count, _, window, _ = held_ref.shape
    rows = window // chunk_count
    own = pick_ref[0]
    for apart in range(count):
        for chunk in range(chunk_count):
            here = slice(chunk * rows, (chunk + 1) * rows)
            held_ref[own ^ apart, :, here] = win_refs[apart // 2 * chunk_count + chunk][apart % 2]
    down = down_ref[...]
    across = across_ref[...]
    at_end = jnp.full(start_ref.shape[1:], pick_ref[1], jnp.int32) == 1
    chi_re, chi_im = (
        jnp.where(at_end, start_ref[part].astype(f32), come_ref[part].astype(f32)).astype(bf16) for part in range(2)
    )
    for layer in range(count - 1, -1, -1):
        spread_re, spread_im = back(down, across, chi_re, chi_im)
        kept_ref[layer, 0] = spread_re.astype(bf16)
        kept_ref[layer, 1] = spread_im.astype(bf16)
        win_re = jnp.log(held_ref[layer, 0].astype(f32)) * (1.0 / code_gain)
        win_im = jnp.log(held_ref[layer, 1].astype(f32)) * (1.0 / code_gain)
        chi_re = (win_re * spread_re + win_im * spread_im).astype(bf16)
        chi_im = (win_re * spread_im - win_im * spread_re).astype(bf16)
    leave_ref[0] = chi_re
    leave_ref[1] = chi_im
    for apart in range(count):
        for chunk in range(chunk_count):
            here = slice(chunk * rows, (chunk + 1) * rows)
            spread_refs[apart // 2 * chunk_count + chunk][apart % 2] = kept_ref[own ^ apart, :, here]


def pass_kernel(*refs):
    *spread_refs, pass_ref = refs
    for apart, spread_ref in enumerate(spread_refs):
        pass_ref[apart] = spread_ref[1]


def gradient_kernel(base, corner_ref, place_ref, pick_ref, wave_ref, *refs):
    *came_refs, passed_ref, own_ref, away_ref = refs
    _, _, rows, window = passed_ref.shape
    tall = 16
    place = place_ref[0]
    own = pick_ref[0]

    def one(block, _):
        at = pl.multiple_of(block * tall, tall)
        sums = [jnp.zeros((tall, window), f32) for _ in range(8)]
        for apart in range(2 * len(came_refs)):
            spread_ref = passed_ref.at[apart // 2] if apart % 2 else came_refs[apart // 2].at[0]
            position = own ^ apart
            in_mine, in_left = first_masks(corner_ref, position, place, base + at, (tall, window))
            wave_re, wave_im = (wave_ref[position, part, pl.ds(base + at, tall), :].astype(f32) for part in range(2))
            spread_re, spread_im = (spread_ref[part, pl.ds(at, tall), :].astype(f32) for part in range(2))
            parts = (
                wave_re * spread_re + wave_im * spread_im,
                wave_re * spread_im - wave_im * spread_re,
            )
            for part in range(2):
                left = jnp.where(in_left, parts[part], 0.0)
                right = jnp.where(in_left, 0.0, parts[part])
                for side, value in enumerate((left, right)):
                    sums[4 * part + side] += jnp.where(in_mine, value, 0.0)
                    sums[4 * part + 2 + side] += jnp.where(in_mine, 0.0, value)
        for part in range(2):
            for side in range(2):
                cols = pl.ds(side * window, window)
                own_ref[part, pl.ds(at, tall), cols] = sums[4 * part + side]
                away_ref[part, pl.ds(at, tall), cols] = sums[4 * part + 2 + side].astype(bf16)
        return 0

    lax.fori_loop(0, rows // tall, one, 0)


def finish_kernel(*refs):
    out_ref = refs[-1]
    rows = refs[0].shape[1]
    for chunk in range(chunk_count):
        own_ref, come_ref = refs[2 * chunk : 2 * chunk + 2]
        out_ref[:, pl.ds(chunk * rows, rows), :] = own_ref[...] + come_ref[...].astype(f32)


def shape_of(dims, dtype):
    return jax.ShapeDtypeStruct(dims, dtype)


def on_device(obj_amp, obj_phase, forward_waves, exit_adjoint, offsets):
    sections = lax.axis_size("sec")
    section = lax.axis_index("sec")
    place = lax.axis_index("scan").astype(jnp.int32).reshape(1)
    count, _, window, _ = exit_adjoint.shape
    _, half, width = obj_amp.shape
    swap = [(0, 1), (1, 0)]
    group_count = sections // count
    rows = half // chunk_count
    chunks = range(chunk_count)
    piece = (2, rows, width)
    part = (2, 2, rows, window)
    wave = (2, window, window)
    chips = range(count // 2)

    def to_partner(value, distance):
        return lax.ppermute(value, "sec", [(s, s ^ distance) for s in range(sections)])

    def exchange(values):
        return [to_partner(values[d], 2 * d) if d else values[0] for d in chips]

    own = section % count
    pick = jnp.stack([own, jnp.int32(1)])
    code = call(
        code_kernel,
        [shape_of(piece, bf16)] * chunk_count,
        scratch=[pltpu.VMEM((half, width), f32)] * 2 + [pltpu.SemaphoreType.DMA((8, 2))],
        space=pltpu.HBM,
    )
    mine = code(obj_amp[0], obj_phase[0])
    windows = []
    for c in chunks:
        other = lax.ppermute(mine[c], "scan", swap)
        slices = [mine[c], other, to_partner(mine[c], 1), to_partner(other, 1)]
        cut = call(functools.partial(cut_kernel, c * rows), [shape_of(part, bf16)] * len(chips), prefetch=3)
        windows.append(exchange(cut(offsets, place, pick, *slices)))
    ready = call(ready_kernel, [shape_of(wave, bf16)] + [shape_of((window, window), bf16)] * 2, prefetch=2)
    start, down, across = ready(offsets, pick, exit_adjoint)
    waves = call(turn_kernel, shape_of(forward_waves.shape[1:], bf16), prefetch=1)(offsets, forward_waves[0])

    at_end = (section >= sections - count).astype(jnp.int32)
    come = start
    through = call(
        group_kernel,
        [shape_of(part, bf16)] * (chunk_count * len(chips)) + [shape_of(wave, bf16)],
        prefetch=1,
        scratch=[pltpu.VMEM((count,) + wave, bf16)] * 2,
        flops=count * 8 * 2 * window**3,
        grant=20,
    )
    stage_windows = [windows[c][d] for d in chips for c in chunks]
    for stage in range(group_count):
        *spreads, leave = through(pick, start, come, down, across, *stage_windows)
        if stage < group_count - 1:
            come = lax.ppermute(leave, "sec", [(s, s - count) for s in range(count, sections)])
            come, waves = lax.optimization_barrier((come, waves))
            pick = jnp.stack([own, at_end])

    came = [exchange(spreads[c::chunk_count]) for c in chunks]
    sums = []
    for c in chunks:
        passed = to_partner(call(pass_kernel, shape_of((len(chips), 2, rows, window), bf16))(*came[c]), 1)
        gradient = call(
            functools.partial(gradient_kernel, c * rows), [shape_of(piece, f32), shape_of(piece, bf16)], prefetch=3
        )
        keep, away = gradient(offsets, place, pick, waves, *came[c], passed)
        sums += [keep, lax.ppermute(away, "scan", swap)]
    return call(finish_kernel, shape_of((2, half, width), f32))(*sums)[None]


def solution(mesh):
    in_specs = (
        P("sec", "scan", None),
        P("sec", "scan", None),
        P("sec", "scan", None, None, None),
        P("scan", None, None, None),
        P("scan", None),
    )
    out_specs = P("sec", None, "scan", None)
    return jax.shard_map(
        on_device, mesh=mesh, in_specs=in_specs, out_specs=out_specs, check_vma=False
    )
```

```python
import functools
import math

import jax
import jax.numpy as jnp
from jax import lax
from jax.experimental import pallas as pl
from jax.experimental.pallas import tpu as pltpu
from jax.sharding import PartitionSpec as P

SUBSTEPS = 2
damping = 0.0005
turning = 0.011
code_gain = 83.0
chunk_count = 2
f32 = jnp.float32
bf16 = jnp.bfloat16


def call(kernel, out_shape, prefetch=0, scratch=(), cost=1, grant=12):
    def run(*args):
        vmem = pl.BlockSpec(memory_space=pltpu.VMEM)
        return pl.pallas_call(
            kernel,
            grid_spec=pltpu.PrefetchScalarGridSpec(
                num_scalar_prefetch=prefetch,
                grid=(1,),
                in_specs=[vmem] * (len(args) - prefetch),
                out_specs=jax.tree.map(lambda _: vmem, out_shape),
                scratch_shapes=list(scratch),
            ),
            out_shape=out_shape,
            cost_estimate=pl.CostEstimate(flops=cost, bytes_accessed=cost, transcendentals=0),
            compiler_params=pltpu.CompilerParams(vmem_limit_bytes=grant * 2**20),
        )(*args)

    return run


def code_kernel(amp_ref, phase_ref, *code_refs):
    rows = code_refs[0].shape[1]
    for chunk, code_ref in enumerate(code_refs):
        amp = amp_ref[pl.ds(chunk * rows, rows), :]
        half = 0.5 * phase_ref[pl.ds(chunk * rows, rows), :]
        square = half * half
        sine = jnp.full_like(half, 1.0 / math.factorial(13))
        cosine = jnp.full_like(half, 1.0 / math.factorial(12))
        for power in (11, 9, 7, 5, 3, 1):
            sign = -1.0 if power % 4 == 3 else 1.0
            sine = sine * square + sign / math.factorial(power)
            cosine = cosine * square + sign / math.factorial(power - 1)
        sine = sine * half
        code_ref[0] = jnp.exp((code_gain * amp) * (1.0 - 2.0 * sine * sine)).astype(bf16)
        code_ref[1] = jnp.exp((code_gain * amp) * (2.0 * sine * cosine)).astype(bf16)


def first_masks(corner_ref, position, place, base, shape):
    row = lax.broadcasted_iota(jnp.int32, shape, 0) + base
    col = lax.broadcasted_iota(jnp.int32, shape, 1)
    at_first = (row >= corner_ref[position, 0]).astype(jnp.int32)
    return at_first != place, col >= corner_ref[position, 1]


def cut_kernel(base, corner_ref, place_ref, pick_ref, *refs):
    slices = (refs[:2], refs[2:4])
    place = place_ref[0]
    for apart, win_ref in enumerate(refs[4:]):
        _, _, rows, window = win_ref.shape
        in_mine, in_left = first_masks(corner_ref, pick_ref[0] ^ (2 * apart), place, base, (rows, window))
        for core, (mine_ref, other_ref) in enumerate(slices):
            for part in range(2):
                left, right = (
                    jnp.where(in_mine, mine_ref[part, :, cols].astype(f32), other_ref[part, :, cols].astype(f32))
                    for cols in (slice(0, window), slice(window, 2 * window))
                )
                win_ref[core, part] = jnp.where(in_left, left, right).astype(bf16)


def turned(wave, row_at, col_at):
    window = wave.shape[-1]
    wave = pltpu.roll(wave.astype(f32), lax.rem(row_at, window), 0)
    return pltpu.roll(wave, lax.rem(col_at, window), 1).astype(bf16)


def second_difference(size, break_at):
    row = lax.broadcasted_iota(jnp.int32, (size, size), 0)
    col = lax.broadcasted_iota(jnp.int32, (size, size), 1)
    start = lax.rem(break_at, size)
    before = (lax.rem(row - col + size, size) == 1) & (row != start)
    after = (lax.rem(col - row + size, size) == 1) & (col != start)
    return jnp.where(row == col, -2.0, jnp.where(before | after, 1.0, 0.0)).astype(bf16)


def ready_kernel(corner_ref, pick_ref, exit_ref, start_ref, down_ref, across_ref):
    own = pick_ref[0]
    row_at = corner_ref[own, 0]
    col_at = corner_ref[own, 1]
    size = start_ref.shape[-1]
    for part in range(2):
        start_ref[part] = turned(exit_ref[own, part], row_at, col_at)
    down_ref[...] = second_difference(size, row_at)
    across_ref[...] = second_difference(size, col_at)


def turn_kernel(corner_ref, wave_ref, turned_ref):
    count = wave_ref.shape[0]

    def one(position, _):
        for part in range(2):
            turned_ref[position, part] = turned(
                wave_ref[position, part], corner_ref[position, 0], corner_ref[position, 1]
            )
        return 0

    lax.fori_loop(0, count, one, 0)


def back(down, across, chi_re, chi_im):
    def laplacian(field):
        rows = jnp.dot(down, field, preferred_element_type=f32)
        return rows + jnp.dot(field, across, preferred_element_type=f32)

    lap_re = laplacian(chi_re)
    lap_im = laplacian(chi_im)
    lap2_re = laplacian(lap_re.astype(bf16))
    lap2_im = laplacian(lap_im.astype(bf16))
    square_re = damping * damping - turning * turning
    square_im = 2.0 * damping * turning
    spread_re = chi_re.astype(f32) + (2.0 * damping) * lap_re + (2.0 * turning) * lap_im
    spread_im = chi_im.astype(f32) + (2.0 * damping) * lap_im - (2.0 * turning) * lap_re
    spread_re = spread_re + square_re * lap2_re + square_im * lap2_im
    spread_im = spread_im + square_re * lap2_im - square_im * lap2_re
    return spread_re, spread_im


def group_kernel(pick_ref, start_ref, come_ref, down_ref, across_ref, token_ref, *refs):
    *refs, leave_ref, held_ref, kept_ref = refs
    count, _, window, _ = held_ref.shape
    rows = window // chunk_count
    here_refs = refs[:chunk_count]
    far = (count // 2 - 1) * chunk_count
    spread_refs = refs[chunk_count + 2 * far :]
    own = pick_ref[0]

    def hold(apart, chunk, ref):
        held_ref[own ^ apart, :, pl.ds(chunk * rows, rows)] = ref[apart % 2]

    for apart in range(2):
        for chunk in range(chunk_count):
            hold(apart, chunk, here_refs[chunk])
    for core in range(2):

        @pl.when(lax.rem(own, 2) == core)
        def _(core=core):
            came_refs = refs[chunk_count + core * far : chunk_count + (core + 1) * far]
            for apart in range(2, count):
                for chunk in range(chunk_count):
                    hold(apart, chunk, came_refs[(apart // 2 - 1) * chunk_count + chunk])

    down = down_ref[...]
    across = across_ref[...]
    at_end = jnp.full(start_ref.shape[1:], pick_ref[1], jnp.int32) == 1
    chi_re, chi_im = (
        jnp.where(at_end, start_ref[part].astype(f32), come_ref[part].astype(f32)).astype(bf16) for part in range(2)
    )
    for layer in range(count - 1, -1, -1):
        spread_re, spread_im = back(down, across, chi_re, chi_im)
        kept_ref[layer, 0] = spread_re.astype(bf16)
        kept_ref[layer, 1] = spread_im.astype(bf16)
        win_re = jnp.log(held_ref[layer, 0].astype(f32)) * (1.0 / code_gain)
        win_im = jnp.log(held_ref[layer, 1].astype(f32)) * (1.0 / code_gain)
        chi_re = (win_re * spread_re + win_im * spread_im).astype(bf16)
        chi_im = (win_re * spread_im - win_im * spread_re).astype(bf16)
    leave_ref[0] = chi_re
    leave_ref[1] = chi_im
    for apart in range(count):
        for chunk in range(chunk_count):
            here = slice(chunk * rows, (chunk + 1) * rows)
            spread_refs[apart // 2 * chunk_count + chunk][apart % 2] = kept_ref[own ^ apart, :, here]


def pass_kernel(*refs):
    *spread_refs, pass_ref = refs
    for apart, spread_ref in enumerate(spread_refs):
        pass_ref[apart] = spread_ref[1]


def gradient_kernel(base, corner_ref, place_ref, pick_ref, wave_ref, *refs):
    *came_refs, passed_ref, own_ref, away_ref = refs
    _, _, rows, window = passed_ref.shape
    tall = 16
    place = place_ref[0]
    own = pick_ref[0]

    def one(block, _):
        at = pl.multiple_of(block * tall, tall)
        sums = [jnp.zeros((tall, window), f32) for _ in range(8)]
        for apart in range(2 * len(came_refs)):
            spread_ref = passed_ref.at[apart // 2] if apart % 2 else came_refs[apart // 2].at[0]
            position = own ^ apart
            in_mine, in_left = first_masks(corner_ref, position, place, base + at, (tall, window))
            wave_re, wave_im = (wave_ref[position, part, pl.ds(base + at, tall), :].astype(f32) for part in range(2))
            spread_re, spread_im = (spread_ref[part, pl.ds(at, tall), :].astype(f32) for part in range(2))
            parts = (
                wave_re * spread_re + wave_im * spread_im,
                wave_re * spread_im - wave_im * spread_re,
            )
            for part in range(2):
                left = jnp.where(in_left, parts[part], 0.0)
                right = jnp.where(in_left, 0.0, parts[part])
                for side, value in enumerate((left, right)):
                    sums[4 * part + side] += jnp.where(in_mine, value, 0.0)
                    sums[4 * part + 2 + side] += jnp.where(in_mine, 0.0, value)
        for part in range(2):
            for side in range(2):
                cols = pl.ds(side * window, window)
                own_ref[part, pl.ds(at, tall), cols] = sums[4 * part + side]
                away_ref[part, pl.ds(at, tall), cols] = sums[4 * part + 2 + side].astype(bf16)
        return 0

    lax.fori_loop(0, rows // tall, one, 0)


def finish_kernel(*refs):
    out_ref = refs[-1]
    rows = refs[0].shape[1]
    for chunk in range(chunk_count):
        own_ref, come_ref = refs[2 * chunk : 2 * chunk + 2]
        out_ref[:, pl.ds(chunk * rows, rows), :] = own_ref[...] + come_ref[...].astype(f32)


def shape_of(dims, dtype):
    return jax.ShapeDtypeStruct(dims, dtype)


def on_device(obj_amp, obj_phase, forward_waves, exit_adjoint, offsets):
    sections = lax.axis_size("sec")
    section = lax.axis_index("sec")
    place = lax.axis_index("scan").astype(jnp.int32).reshape(1)
    count, _, window, _ = exit_adjoint.shape
    _, half, width = obj_amp.shape
    swap = [(0, 1), (1, 0)]
    group_count = sections // count
    rows = half // chunk_count
    chunks = range(chunk_count)
    piece = (2, rows, width)
    part = (2, 2, rows, window)
    wave = (2, window, window)
    chips = range(count // 2)

    def to_partner(value, distance, core=None):
        senders = [s for s in range(sections) if core is None or s % 2 == core]
        return lax.ppermute(value, "sec", [(s, s ^ distance) for s in senders])

    def exchange(values):
        return [to_partner(values[d], 2 * d) if d else values[0] for d in chips]

    own = section % count
    pick = jnp.stack([own, jnp.int32(1)])
    mine = call(code_kernel, [shape_of(piece, bf16)] * chunk_count)(obj_amp[0], obj_phase[0])
    others = [lax.ppermute(mine[c], "scan", swap) for c in chunks]
    beside = [to_partner(mine[c], 1) for c in chunks]
    cuts = []
    for c in chunks:
        slices = [mine[c], others[c], beside[c], to_partner(others[c], 1)]
        cut = call(functools.partial(cut_kernel, c * rows), [shape_of(part, bf16)] * len(chips), prefetch=3)
        cuts.append(cut(offsets, place, pick, *slices))
        if c < chunk_count - 1:
            others[c + 1], cuts[c] = lax.optimization_barrier((others[c + 1], cuts[c]))

    windows = [[[to_partner(cuts[c][d], 2 * d, 0) for c in chunks] for d in chips[1:]]]
    *most, last = jax.tree.leaves(windows)
    most = lax.optimization_barrier(most)
    windows = [most + [last]]
    token = lax.slice(most[0], (0, 0, 0, 0), (1, 1, 16, 128))
    token = lax.ppermute(token, "sec", [(s, s + 1) for s in range(0, sections, 2)])
    cuts, token = lax.optimization_barrier((cuts, token))
    windows.append([[to_partner(cuts[c][d], 2 * d, 1) for c in chunks] for d in chips[1:]])
    stage_windows = [cuts[c][0] for c in chunks] + jax.tree.leaves(windows)
    ready = call(ready_kernel, [shape_of(wave, bf16)] + [shape_of((window, window), bf16)] * 2, prefetch=2)
    start, down, across = ready(offsets, pick, exit_adjoint)
    waves = call(turn_kernel, shape_of(forward_waves.shape[1:], bf16), prefetch=1)(offsets, forward_waves[0])

    at_end = (section >= sections - count).astype(jnp.int32)
    come = start
    through = call(
        group_kernel,
        [shape_of(part, bf16)] * (chunk_count * len(chips)) + [shape_of(wave, bf16)],
        prefetch=1,
        scratch=[pltpu.VMEM((count,) + wave, bf16)] * 2,
        grant=20,
    )
    for stage in range(group_count):
        *spreads, leave = through(pick, start, come, down, across, token, *stage_windows)
        if stage < group_count - 1:
            come = lax.ppermute(leave, "sec", [(s, s - count) for s in range(count, sections)])
            come, waves = lax.optimization_barrier((come, waves))
            pick = jnp.stack([own, at_end])

    came = [exchange(spreads[c::chunk_count]) for c in chunks]
    sums = []
    for c in chunks:
        if c > 0:
            came[c], sums = lax.optimization_barrier((came[c], sums))
        passed = to_partner(call(pass_kernel, shape_of((len(chips), 2, rows, window), bf16))(*came[c]), 1)
        gradient = call(
            functools.partial(gradient_kernel, c * rows), [shape_of(piece, f32), shape_of(piece, bf16)], prefetch=3
        )
        keep, away = gradient(offsets, place, pick, waves, *came[c], passed)
        sums += [keep, away]
    sums[1::2] = [lax.ppermute(away, "scan", swap) for away in sums[1::2]]
    return call(finish_kernel, shape_of((2, half, width), f32))(*sums)[None]


def solution(mesh):
    in_specs = (
        P("sec", "scan", None),
        P("sec", "scan", None),
        P("sec", "scan", None, None, None),
        P("scan", None, None, None),
        P("scan", None),
    )
    out_specs = P("sec", None, "scan", None)
    return jax.shard_map(
        on_device, mesh=mesh, in_specs=in_specs, out_specs=out_specs, check_vma=False
    )
```

```python
import functools
import math

import jax
import jax.numpy as jnp
from jax import lax
from jax.experimental import pallas as pl
from jax.experimental.pallas import tpu as pltpu
from jax.sharding import PartitionSpec as P

SUBSTEPS = 2
damping = 0.0005
turning = 0.011
code_gain = 83.0
chunk_count = 2
f32 = jnp.float32
bf16 = jnp.bfloat16


def call(kernel, out_shape, prefetch=0, scratch=(), flops=0, grant=12):
    def run(*args):
        moved = sum(a.size * a.dtype.itemsize for a in jax.tree.leaves((args, out_shape)))
        vmem = pl.BlockSpec(memory_space=pltpu.VMEM)
        return pl.pallas_call(
            kernel,
            grid_spec=pltpu.PrefetchScalarGridSpec(
                num_scalar_prefetch=prefetch,
                grid=(1,),
                in_specs=[vmem] * (len(args) - prefetch),
                out_specs=jax.tree.map(lambda _: vmem, out_shape),
                scratch_shapes=list(scratch),
            ),
            out_shape=out_shape,
            cost_estimate=pl.CostEstimate(flops=flops, bytes_accessed=moved, transcendentals=0),
            compiler_params=pltpu.CompilerParams(vmem_limit_bytes=grant * 2**20),
        )(*args)

    return run


def code_kernel(amp_ref, phase_ref, *code_refs):
    rows = code_refs[0].shape[1]
    for chunk, code_ref in enumerate(code_refs):
        amp = amp_ref[pl.ds(chunk * rows, rows), :]
        half = 0.5 * phase_ref[pl.ds(chunk * rows, rows), :]
        square = half * half
        sine = jnp.full_like(half, 1.0 / math.factorial(13))
        cosine = jnp.full_like(half, 1.0 / math.factorial(12))
        for power in (11, 9, 7, 5, 3, 1):
            sign = -1.0 if power % 4 == 3 else 1.0
            sine = sine * square + sign / math.factorial(power)
            cosine = cosine * square + sign / math.factorial(power - 1)
        sine = sine * half
        code_ref[0] = jnp.exp((code_gain * amp) * (1.0 - 2.0 * sine * sine)).astype(bf16)
        code_ref[1] = jnp.exp((code_gain * amp) * (2.0 * sine * cosine)).astype(bf16)


def first_masks(corner_ref, position, place, base, shape):
    row = lax.broadcasted_iota(jnp.int32, shape, 0) + base
    col = lax.broadcasted_iota(jnp.int32, shape, 1)
    at_first = (row >= corner_ref[position, 0]).astype(jnp.int32)
    return at_first != place, col >= corner_ref[position, 1]


def cut_kernel(base, corner_ref, place_ref, pick_ref, *refs):
    slices = (refs[:2], refs[2:4])
    place = place_ref[0]
    for apart, win_ref in enumerate(refs[4:]):
        _, _, rows, window = win_ref.shape
        in_mine, in_left = first_masks(corner_ref, pick_ref[0] ^ (2 * apart), place, base, (rows, window))
        for core, (mine_ref, other_ref) in enumerate(slices):
            for part in range(2):
                left, right = (
                    jnp.where(in_mine, mine_ref[part, :, cols].astype(f32), other_ref[part, :, cols].astype(f32))
                    for cols in (slice(0, window), slice(window, 2 * window))
                )
                win_ref[core, part] = jnp.where(in_left, left, right).astype(bf16)


def turned(wave, row_at, col_at):
    window = wave.shape[-1]
    wave = pltpu.roll(wave.astype(f32), lax.rem(row_at, window), 0)
    return pltpu.roll(wave, lax.rem(col_at, window), 1).astype(bf16)


def second_difference(size, break_at):
    row = lax.broadcasted_iota(jnp.int32, (size, size), 0)
    col = lax.broadcasted_iota(jnp.int32, (size, size), 1)
    start = lax.rem(break_at, size)
    before = (lax.rem(row - col + size, size) == 1) & (row != start)
    after = (lax.rem(col - row + size, size) == 1) & (col != start)
    return jnp.where(row == col, -2.0, jnp.where(before | after, 1.0, 0.0)).astype(bf16)


def ready_kernel(corner_ref, pick_ref, exit_ref, start_ref, down_ref, across_ref):
    own = pick_ref[0]
    row_at = corner_ref[own, 0]
    col_at = corner_ref[own, 1]
    size = start_ref.shape[-1]
    for part in range(2):
        start_ref[part] = turned(exit_ref[own, part], row_at, col_at)
    down_ref[...] = second_difference(size, row_at)
    across_ref[...] = second_difference(size, col_at)


def turn_kernel(corner_ref, wave_ref, turned_ref):
    count = wave_ref.shape[0]

    def one(position, _):
        for part in range(2):
            turned_ref[position, part] = turned(
                wave_ref[position, part], corner_ref[position, 0], corner_ref[position, 1]
            )
        return 0

    lax.fori_loop(0, count, one, 0)


def back(down, across, chi_re, chi_im):
    def laplacian(field):
        rows = jnp.dot(down, field, preferred_element_type=f32)
        return rows + jnp.dot(field, across, preferred_element_type=f32)

    lap_re = laplacian(chi_re)
    lap_im = laplacian(chi_im)
    lap2_re = laplacian(lap_re.astype(bf16))
    lap2_im = laplacian(lap_im.astype(bf16))
    more_re = 2.0 * lap_re + (damping * lap2_re + turning * lap2_im)
    more_im = 2.0 * lap_im + (damping * lap2_im - turning * lap2_re)
    spread_re = chi_re.astype(f32) + (damping * more_re + turning * more_im)
    spread_im = chi_im.astype(f32) + (damping * more_im - turning * more_re)
    return spread_re, spread_im


def pass_group(down, across, chi_re, chi_im, count, window_of, keep):
    for layer in range(count - 1, -1, -1):
        spread_re, spread_im = back(down, across, chi_re, chi_im)
        keep(layer, spread_re, spread_im)
        win_re, win_im = window_of(layer)
        chi_re = (win_re * spread_re + win_im * spread_im).astype(bf16)
        chi_im = (win_re * spread_im - win_im * spread_re).astype(bf16)
    return chi_re, chi_im


def first_kernel(pick_ref, start_ref, down_ref, across_ref, *refs):
    *win_refs, leave_ref, clear_ref, held_ref = refs
    count, _, window, _ = held_ref.shape
    rows = window // chunk_count
    own = pick_ref[0]
    for apart in range(count):
        for chunk in range(chunk_count):
            here = slice(chunk * rows, (chunk + 1) * rows)
            held_ref[own ^ apart, :, here] = win_refs[apart // 2 * chunk_count + chunk][apart % 2]

    def window_of(layer):
        window = [jnp.log(held_ref[layer, part].astype(f32)) * (1.0 / code_gain) for part in range(2)]
        for part in range(2):
            clear_ref[layer, part] = window[part]
        return window

    chi = pass_group(
        down_ref[...], across_ref[...], start_ref[0], start_ref[1], count, window_of, lambda *_: None
    )
    leave_ref[0], leave_ref[1] = chi


def next_kernel(is_last, pick_ref, start_ref, come_ref, down_ref, across_ref, clear_ref, *refs):
    count, _, window, _ = clear_ref.shape
    rows = window // chunk_count
    own = pick_ref[0]
    at_end = jnp.full((window, window), pick_ref[1], jnp.int32) == 1
    chi_re, chi_im = (
        jnp.where(at_end, start_ref[part].astype(f32), come_ref[part].astype(f32)).astype(bf16) for part in range(2)
    )

    def window_of(layer):
        return clear_ref[layer, 0], clear_ref[layer, 1]

    def keep(layer, spread_re, spread_im):
        if is_last:
            refs[-1][layer, 0] = spread_re.astype(bf16)
            refs[-1][layer, 1] = spread_im.astype(bf16)

    chi = pass_group(down_ref[...], across_ref[...], chi_re, chi_im, count, window_of, keep)
    if not is_last:
        refs[0][0], refs[0][1] = chi
        return
    *spread_refs, kept_ref = refs
    for apart in range(count):
        for chunk in range(chunk_count):
            here = slice(chunk * rows, (chunk + 1) * rows)
            spread_refs[apart // 2 * chunk_count + chunk][apart % 2] = kept_ref[own ^ apart, :, here]


def pass_kernel(*refs):
    *spread_refs, pass_ref = refs
    for apart, spread_ref in enumerate(spread_refs):
        pass_ref[apart] = spread_ref[1]


def gradient_kernel(base, corner_ref, place_ref, pick_ref, wave_ref, *refs):
    *came_refs, passed_ref, own_ref, away_ref = refs
    _, _, rows, window = passed_ref.shape
    tall = 16
    place = place_ref[0]
    own = pick_ref[0]

    def one(block, _):
        at = pl.multiple_of(block * tall, tall)
        sums = [jnp.zeros((tall, window), f32) for _ in range(8)]
        for apart in range(2 * len(came_refs)):
            spread_ref = passed_ref.at[apart // 2] if apart % 2 else came_refs[apart // 2].at[0]
            position = own ^ apart
            in_mine, in_left = first_masks(corner_ref, position, place, base + at, (tall, window))
            wave_re, wave_im = (wave_ref[position, part, pl.ds(base + at, tall), :].astype(f32) for part in range(2))
            spread_re, spread_im = (spread_ref[part, pl.ds(at, tall), :].astype(f32) for part in range(2))
            parts = (
                wave_re * spread_re + wave_im * spread_im,
                wave_re * spread_im - wave_im * spread_re,
            )
            for part in range(2):
                left = jnp.where(in_left, parts[part], 0.0)
                right = jnp.where(in_left, 0.0, parts[part])
                for side, value in enumerate((left, right)):
                    sums[4 * part + side] += jnp.where(in_mine, value, 0.0)
                    sums[4 * part + 2 + side] += jnp.where(in_mine, 0.0, value)
        for part in range(2):
            for side in range(2):
                cols = pl.ds(side * window, window)
                own_ref[part, pl.ds(at, tall), cols] = sums[4 * part + side]
                away_ref[part, pl.ds(at, tall), cols] = sums[4 * part + 2 + side].astype(bf16)
        return 0

    lax.fori_loop(0, rows // tall, one, 0)


def finish_kernel(*refs):
    out_ref = refs[-1]
    rows = refs[0].shape[1]
    for chunk in range(chunk_count):
        own_ref, come_ref = refs[2 * chunk : 2 * chunk + 2]
        out_ref[:, pl.ds(chunk * rows, rows), :] = own_ref[...] + come_ref[...].astype(f32)


def shape_of(dims, dtype):
    return jax.ShapeDtypeStruct(dims, dtype)


def on_device(obj_amp, obj_phase, forward_waves, exit_adjoint, offsets):
    sections = lax.axis_size("sec")
    section = lax.axis_index("sec")
    place = lax.axis_index("scan").astype(jnp.int32).reshape(1)
    count, _, window, _ = exit_adjoint.shape
    _, half, width = obj_amp.shape
    swap = [(0, 1), (1, 0)]
    group_count = sections // count
    rows = half // chunk_count
    chunks = range(chunk_count)
    piece = (2, rows, width)
    part = (2, 2, rows, window)
    wave = (2, window, window)
    chips = range(count // 2)

    def to_partner(value, distance):
        return lax.ppermute(value, "sec", [(s, s ^ distance) for s in range(sections)])

    def exchange(values):
        return [to_partner(values[d], 2 * d) if d else values[0] for d in chips]

    own = section % count
    pick = jnp.stack([own, jnp.int32(1)])
    code = call(code_kernel, [shape_of(piece, bf16)] * chunk_count)
    mine = list(code(obj_amp[0], obj_phase[0]))
    beside = [to_partner(mine[c], 1) for c in chunks]
    windows = []
    for c in chunks:
        other = lax.ppermute(mine[c], "scan", swap)
        if c > 0:
            other, windows[-1] = lax.optimization_barrier((other, windows[-1]))
        slices = [mine[c], other, beside[c], to_partner(other, 1)]
        if c < chunk_count - 1:
            slices[3], mine[c + 1] = lax.optimization_barrier((slices[3], mine[c + 1]))
        cut = call(functools.partial(cut_kernel, c * rows), [shape_of(part, bf16)] * len(chips), prefetch=3)
        windows.append(cut(offsets, place, pick, *slices))
    windows = [exchange(cuts) for cuts in windows]
    ready = call(ready_kernel, [shape_of(wave, bf16)] + [shape_of((window, window), bf16)] * 2, prefetch=2)
    start, down, across = ready(offsets, pick, exit_adjoint)
    waves = call(turn_kernel, shape_of(forward_waves.shape[1:], bf16), prefetch=1)(offsets, forward_waves[0])

    at_end = (section >= sections - count).astype(jnp.int32)
    stage_windows = [windows[c][d] for d in chips for c in chunks]
    flops = count * 8 * 2 * window**3
    first = call(
        first_kernel,
        [shape_of(wave, bf16), shape_of((count,) + wave, f32)],
        prefetch=1,
        scratch=[pltpu.VMEM((count,) + wave, bf16)],
        flops=flops,
        grant=20,
    )
    leave, clear = first(pick, start, down, across, *stage_windows)
    pick = jnp.stack([own, at_end])
    for stage in range(1, group_count):
        come = lax.ppermute(leave, "sec", [(s, s - count) for s in range(count, sections)])
        come, waves = lax.optimization_barrier((come, waves))
        is_last = stage == group_count - 1
        through = call(
            functools.partial(next_kernel, is_last),
            [shape_of(part, bf16)] * (chunk_count * len(chips)) if is_last else shape_of(wave, bf16),
            prefetch=1,
            scratch=[pltpu.VMEM((count,) + wave, bf16)] if is_last else [],
            flops=flops,
            grant=20,
        )
        leave = through(pick, start, come, down, across, clear)
    spreads = leave

    came = [exchange(spreads[c::chunk_count]) for c in chunks]
    sums = []
    for c in chunks:
        if c > 0:
            came[c], sums[-2:] = lax.optimization_barrier((came[c], sums[-2:]))
        passed = to_partner(call(pass_kernel, shape_of((len(chips), 2, rows, window), bf16))(*came[c]), 1)
        if c > 0:
            sums[-1] = lax.ppermute(sums[-1], "scan", swap)
            passed, sums[-1] = lax.optimization_barrier((passed, sums[-1]))
        gradient = call(
            functools.partial(gradient_kernel, c * rows), [shape_of(piece, f32), shape_of(piece, bf16)], prefetch=3
        )
        sums += gradient(offsets, place, pick, waves, *came[c], passed)
    sums[-1] = lax.ppermute(sums[-1], "scan", swap)
    return call(finish_kernel, shape_of((2, half, width), f32))(*sums)[None]


def solution(mesh):
    in_specs = (
        P("sec", "scan", None),
        P("sec", "scan", None),
        P("sec", "scan", None, None, None),
        P("scan", None, None, None),
        P("scan", None),
    )
    out_specs = P("sec", None, "scan", None)
    return jax.shard_map(
        on_device, mesh=mesh, in_specs=in_specs, out_specs=out_specs, check_vma=False
    )
```

```python
import functools
import math

import jax
import jax.numpy as jnp
from jax import lax
from jax.experimental import pallas as pl
from jax.experimental.pallas import tpu as pltpu
from jax.sharding import PartitionSpec as P

SUBSTEPS = 2
damping = 0.0005
turning = 0.011
code_gain = 83.0
chunk_count = 2
f32 = jnp.float32
bf16 = jnp.bfloat16


def call(kernel, out_shape, prefetch=0, scratch=(), cost=(0, 0), grant=6, aliases=None):
    flops, transcendentals = cost

    def run(*args):
        moved = sum(a.size * a.dtype.itemsize for a in jax.tree.leaves((args, out_shape)))
        vmem = pl.BlockSpec(memory_space=pltpu.VMEM)
        return pl.pallas_call(
            kernel,
            grid_spec=pltpu.PrefetchScalarGridSpec(
                num_scalar_prefetch=prefetch,
                grid=(1,),
                in_specs=[vmem] * (len(args) - prefetch),
                out_specs=jax.tree.map(lambda _: vmem, out_shape),
                scratch_shapes=list(scratch),
            ),
            out_shape=out_shape,
            input_output_aliases=aliases or {},
            cost_estimate=pl.CostEstimate(flops=flops, bytes_accessed=moved, transcendentals=transcendentals),
            compiler_params=pltpu.CompilerParams(vmem_limit_bytes=grant * 2**20),
        )(*args)

    return run


def place_in_group(count):
    return lax.rem(lax.axis_index("sec").astype(jnp.int32), count)


def code_kernel(amp_ref, phase_ref, *code_refs):
    rows = code_refs[0].shape[1]
    for chunk, code_ref in enumerate(code_refs):
        amp = amp_ref[pl.ds(chunk * rows, rows), :]
        half = 0.5 * phase_ref[pl.ds(chunk * rows, rows), :]
        square = half * half
        sine = jnp.full_like(half, 1.0 / math.factorial(13))
        cosine = jnp.full_like(half, 1.0 / math.factorial(12))
        for power in (11, 9, 7, 5, 3, 1):
            sign = -1.0 if power % 4 == 3 else 1.0
            sine = sine * square + sign / math.factorial(power)
            cosine = cosine * square + sign / math.factorial(power - 1)
        sine = sine * half
        code_ref[0] = jnp.exp((code_gain * amp) * (1.0 - 2.0 * sine * sine)).astype(bf16)
        code_ref[1] = jnp.exp((code_gain * amp) * (2.0 * sine * cosine)).astype(bf16)


def first_masks(corner_ref, position, base, shape):
    place = lax.axis_index("scan").astype(jnp.int32)
    row = lax.broadcasted_iota(jnp.int32, shape, 0) + base
    col = lax.broadcasted_iota(jnp.int32, shape, 1)
    at_first = (row >= corner_ref[0, position]).astype(jnp.int32)
    return at_first != place, col >= corner_ref[1, position]


def cut_kernel(base, count, corner_ref, mine_ref, other_ref, *refs):
    own = place_in_group(count)
    for apart, win_ref in enumerate(refs[-count:]):
        _, rows, width = mine_ref.shape
        window = width // 2
        if base:
            win_ref[:, :base] = refs[apart][:, :base]
        in_mine, in_left = first_masks(corner_ref, own ^ apart, base, (rows, window))
        for part in range(2):
            left, right = (
                jnp.where(in_mine, mine_ref[part, :, cols].astype(f32), other_ref[part, :, cols].astype(f32))
                for cols in (slice(0, window), slice(window, 2 * window))
            )
            win_ref[part, pl.ds(base, rows), :] = jnp.where(in_left, left, right).astype(bf16)


def turned(wave, row_at, col_at):
    window = wave.shape[-1]
    wave = pltpu.roll(wave.astype(f32), lax.rem(row_at, window), 0)
    return pltpu.roll(wave, lax.rem(col_at, window), 1).astype(bf16)


def second_difference(size, break_at):
    row = lax.broadcasted_iota(jnp.int32, (size, size), 0)
    col = lax.broadcasted_iota(jnp.int32, (size, size), 1)
    start = lax.rem(break_at, size)
    before = (lax.rem(row - col + size, size) == 1) & (row != start)
    after = (lax.rem(col - row + size, size) == 1) & (col != start)
    return jnp.where(row == col, -2.0, jnp.where(before | after, 1.0, 0.0)).astype(bf16)


def ready_kernel(corner_ref, exit_ref, start_ref, down_ref, across_ref):
    own = place_in_group(exit_ref.shape[0])
    row_at = corner_ref[0, own]
    col_at = corner_ref[1, own]
    size = start_ref.shape[-1]
    for part in range(2):
        start_ref[part] = turned(exit_ref[own, part], row_at, col_at)
    down_ref[...] = second_difference(size, row_at)
    across_ref[...] = second_difference(size, col_at)


def turn_kernel(corner_ref, wave_ref, turned_ref):
    count = wave_ref.shape[0]

    def one(position, _):
        for part in range(2):
            turned_ref[position, part] = turned(
                wave_ref[position, part], corner_ref[0, position], corner_ref[1, position]
            )
        return 0

    lax.fori_loop(0, count, one, 0)


def back(down, across, chi_re, chi_im):
    def laplacian(field):
        rows = jnp.dot(down, field, preferred_element_type=f32)
        return rows + jnp.dot(field, across, preferred_element_type=f32)

    lap_re = laplacian(chi_re)
    lap_im = laplacian(chi_im)
    lap2_re = laplacian(lap_re.astype(bf16))
    lap2_im = laplacian(lap_im.astype(bf16))
    more_re = 2.0 * lap_re + (damping * lap2_re + turning * lap2_im)
    more_im = 2.0 * lap_im + (damping * lap2_im - turning * lap2_re)
    spread_re = chi_re.astype(f32) + (damping * more_re + turning * more_im)
    spread_im = chi_im.astype(f32) + (damping * more_im - turning * more_re)
    return spread_re, spread_im


def pass_group(down, across, chi_re, chi_im, count, window_of, keep):
    for layer in range(count - 1, -1, -1):
        spread_re, spread_im = back(down, across, chi_re, chi_im)
        keep(layer, spread_re, spread_im)
        win_re, win_im = window_of(layer)
        chi_re = (win_re * spread_re + win_im * spread_im).astype(bf16)
        chi_im = (win_re * spread_im - win_im * spread_re).astype(bf16)
    return chi_re, chi_im


def decoded(held_ref, layer):
    return [jnp.log(held_ref[layer, part].astype(f32)) * (1.0 / code_gain) for part in range(2)]


def first_kernel(start_ref, down_ref, across_ref, *refs):
    *win_refs, leave_ref, held_ref = refs
    count = len(win_refs)
    own = place_in_group(count)
    for apart in range(count):
        held_ref[own ^ apart] = win_refs[apart][...]
    leave_ref[0], leave_ref[1] = pass_group(
        down_ref[...],
        across_ref[...],
        start_ref[0],
        start_ref[1],
        count,
        functools.partial(decoded, held_ref),
        lambda *_: None,
    )


def next_kernel(is_last, start_ref, come_ref, down_ref, across_ref, held_ref, *refs):
    count, _, window, _ = held_ref.shape
    own = place_in_group(count)
    behind = (lax.axis_index("sec") + count).astype(jnp.int32)
    at_end = jnp.full((window, window), behind, jnp.int32) >= lax.axis_size("sec")
    chi_re, chi_im = (
        jnp.where(at_end, start_ref[part].astype(f32), come_ref[part].astype(f32)).astype(bf16) for part in range(2)
    )

    def keep(layer, spread_re, spread_im):
        if is_last:
            refs[-1][layer, 0] = spread_re.astype(bf16)
            refs[-1][layer, 1] = spread_im.astype(bf16)

    chi = pass_group(
        down_ref[...], across_ref[...], chi_re, chi_im, count, functools.partial(decoded, held_ref), keep
    )
    if not is_last:
        refs[0][0], refs[0][1] = chi
        return
    for apart in range(count):
        refs[apart][...] = refs[-1][own ^ apart]


def gradient_kernel(base, corner_ref, wave_ref, *refs):
    *spread_refs, own_ref, away_ref = refs
    rows = own_ref.shape[1]
    window = wave_ref.shape[-1]
    tall = 16
    own = place_in_group(wave_ref.shape[0])

    def one(block, _):
        at = pl.multiple_of(block * tall, tall)
        sums = [jnp.zeros((tall, window), f32) for _ in range(8)]
        here = pl.ds(base + at, tall)
        for apart, spread_ref in enumerate(spread_refs):
            position = own ^ apart
            in_mine, in_left = first_masks(corner_ref, position, base + at, (tall, window))
            wave_re, wave_im = (wave_ref[position, part, here, :].astype(f32) for part in range(2))
            spread_re, spread_im = (spread_ref[part, here, :].astype(f32) for part in range(2))
            parts = (
                wave_re * spread_re + wave_im * spread_im,
                wave_re * spread_im - wave_im * spread_re,
            )
            for part in range(2):
                left = jnp.where(in_left, parts[part], 0.0)
                right = jnp.where(in_left, 0.0, parts[part])
                for side, value in enumerate((left, right)):
                    sums[4 * part + side] += jnp.where(in_mine, value, 0.0)
                    sums[4 * part + 2 + side] += jnp.where(in_mine, 0.0, value)
        for part in range(2):
            for side in range(2):
                cols = pl.ds(side * window, window)
                own_ref[part, pl.ds(at, tall), cols] = sums[4 * part + side]
                away_ref[part, pl.ds(at, tall), cols] = sums[4 * part + 2 + side].astype(bf16)
        return 0

    lax.fori_loop(0, rows // tall, one, 0)


def finish_kernel(*refs):
    out_ref = refs[-1]
    rows = refs[0].shape[1]
    for chunk in range(chunk_count):
        own_ref, come_ref = refs[2 * chunk : 2 * chunk + 2]
        out_ref[:, pl.ds(chunk * rows, rows), :] = own_ref[...] + come_ref[...].astype(f32)


def shape_of(dims, dtype):
    return jax.ShapeDtypeStruct(dims, dtype)


def on_device(obj_amp, obj_phase, forward_waves, exit_adjoint, offsets):
    sections = lax.axis_size("sec")
    count, _, window, _ = exit_adjoint.shape
    _, half, width = obj_amp.shape
    group_count = sections // count
    chunks = range(chunk_count)
    rows = half // chunk_count
    piece = (2, rows, width)
    wave = (2, window, window)
    corners = offsets.T

    def to_other_half(value):
        return lax.ppermute(value, "scan", [(0, 1), (1, 0)])

    def exchange(values):
        return [values[0]] + [
            lax.ppermute(values[d], "sec", [(s, s ^ d) for s in range(sections)]) for d in range(1, count)
        ]

    mine = call(code_kernel, [shape_of(piece, bf16)] * chunk_count)(obj_amp[0], obj_phase[0])
    windows = []
    for c in chunks:
        cut = call(
            functools.partial(cut_kernel, c * rows, count),
            [shape_of(wave, bf16)] * count,
            prefetch=1,
            aliases={3 + i: i for i in range(len(windows))},
        )
        windows = cut(corners, mine[c], to_other_half(mine[c]), *windows)
    windows = exchange(windows)
    ready = call(ready_kernel, [shape_of(wave, bf16)] + [shape_of((window, window), bf16)] * 2, prefetch=1)
    start, down, across = ready(corners, exit_adjoint)
    waves = call(turn_kernel, shape_of(forward_waves.shape[1:], bf16), prefetch=1)(corners, forward_waves[0])

    cost = (count * 16 * window**3, count * 2 * window**2)
    first = call(first_kernel, [shape_of(wave, bf16), shape_of((count,) + wave, bf16)], cost=cost, grant=12)
    leave, held = first(start, down, across, *windows)
    for stage in range(1, group_count):
        come = lax.ppermute(leave, "sec", [(s, s - count) for s in range(count, sections)])
        come, waves = lax.optimization_barrier((come, waves))
        is_last = stage == group_count - 1
        through = call(
            functools.partial(next_kernel, is_last),
            [shape_of(wave, bf16)] * count if is_last else shape_of(wave, bf16),
            scratch=[pltpu.VMEM((count,) + wave, bf16)] if is_last else [],
            cost=cost,
            grant=12,
        )
        leave = through(start, come, down, across, held)

    came = exchange(leave)
    sums = []
    for c in chunks:
        gradient = call(
            functools.partial(gradient_kernel, c * rows), [shape_of(piece, f32), shape_of(piece, bf16)], prefetch=1
        )
        keep, away = gradient(corners, waves, *came)
        sums += [keep, to_other_half(away)]
    return call(finish_kernel, shape_of((2, half, width), f32))(*sums)[None]


def solution(mesh):
    in_specs = (
        P("sec", "scan", None),
        P("sec", "scan", None),
        P("sec", "scan", None, None, None),
        P("scan", None, None, None),
        P("scan", None),
    )
    out_specs = P("sec", None, "scan", None)
    return jax.shard_map(
        on_device, mesh=mesh, in_specs=in_specs, out_specs=out_specs, check_vma=False
    )
```

```python
import functools
import math

import jax
import jax.numpy as jnp
from jax import lax
from jax.experimental import pallas as pl
from jax.experimental.pallas import tpu as pltpu
from jax.sharding import PartitionSpec as P

SUBSTEPS = 2
damping = 0.0005
turning = 0.011
code_gain = 83.0
chunk_count = 2
far = 2
f32 = jnp.float32
bf16 = jnp.bfloat16


def call(kernel, out_shape, prefetch=0, scratch=(), cost=(0, 0), grant=6, aliases=None):
    flops, transcendentals = cost

    def run(*args):
        moved = sum(a.size * a.dtype.itemsize for a in jax.tree.leaves((args, out_shape)))
        vmem = pl.BlockSpec(memory_space=pltpu.VMEM)
        return pl.pallas_call(
            kernel,
            grid_spec=pltpu.PrefetchScalarGridSpec(
                num_scalar_prefetch=prefetch,
                grid=(1,),
                in_specs=[vmem] * (len(args) - prefetch),
                out_specs=jax.tree.map(lambda _: vmem, out_shape),
                scratch_shapes=list(scratch),
            ),
            out_shape=out_shape,
            input_output_aliases=aliases or {},
            cost_estimate=pl.CostEstimate(flops=flops, bytes_accessed=moved, transcendentals=transcendentals),
            compiler_params=pltpu.CompilerParams(vmem_limit_bytes=grant * 2**20),
        )(*args)

    return run


def place_in_group(count):
    return lax.rem(lax.axis_index("sec").astype(jnp.int32), count)


def coded(amp, phase):
    half = 0.5 * phase
    square = half * half
    sine = jnp.full_like(half, 1.0 / math.factorial(13))
    cosine = jnp.full_like(half, 1.0 / math.factorial(12))
    for power in (11, 9, 7, 5, 3, 1):
        sign = -1.0 if power % 4 == 3 else 1.0
        sine = sine * square + sign / math.factorial(power)
        cosine = cosine * square + sign / math.factorial(power - 1)
    sine = sine * half
    trans_re = amp * (1.0 - 2.0 * sine * sine)
    trans_im = amp * (2.0 * sine * cosine)
    return jnp.stack([jnp.exp(code_gain * trans_re).astype(bf16), jnp.exp(code_gain * trans_im).astype(bf16)])


def first_masks(corner_ref, position, base, shape):
    place = lax.axis_index("scan").astype(jnp.int32)
    row = lax.broadcasted_iota(jnp.int32, shape, 0) + base
    col = lax.broadcasted_iota(jnp.int32, shape, 1)
    at_first = (row >= corner_ref[0, position]).astype(jnp.int32)
    return at_first != place, col >= corner_ref[1, position]


def distances(count):
    return sorted(range(count), key=lambda d: (d >= count - far, d > 0, d == 1, d % 2, d))


def cut_kernel(base, count, corner_ref, mine_ref, other_ref, *refs):
    own = place_in_group(count)
    _, rows, width = mine_ref.shape
    window = width // 2
    for i, (apart, win_ref) in enumerate(zip(distances(count), refs[-count:])):
        here = pl.ds(0 if i >= count - far else base, rows)
        if base and i < count - far:
            win_ref[:, :base] = refs[i][:, :base]
        in_mine, in_left = first_masks(corner_ref, own ^ apart, base, (rows, window))
        for part in range(2):
            left, right = (
                jnp.where(in_mine, mine_ref[part, :, cols].astype(f32), other_ref[part, :, cols].astype(f32))
                for cols in (slice(0, window), slice(window, 2 * window))
            )
            win_ref[part, here, :] = jnp.where(in_left, left, right).astype(bf16)


def turned(wave, row_at, col_at):
    window = wave.shape[-1]
    wave = pltpu.roll(wave.astype(f32), lax.rem(row_at, window), 0)
    return pltpu.roll(wave, lax.rem(col_at, window), 1).astype(bf16)


def second_difference(size, break_at):
    row = lax.broadcasted_iota(jnp.int32, (size, size), 0)
    col = lax.broadcasted_iota(jnp.int32, (size, size), 1)
    start = lax.rem(break_at, size)
    before = (lax.rem(row - col + size, size) == 1) & (row != start)
    after = (lax.rem(col - row + size, size) == 1) & (col != start)
    return jnp.where(row == col, -2.0, jnp.where(before | after, 1.0, 0.0)).astype(bf16)


def ready_kernel(corner_ref, exit_ref, start_ref, down_ref, across_ref):
    own = place_in_group(exit_ref.shape[0])
    row_at = corner_ref[0, own]
    col_at = corner_ref[1, own]
    size = start_ref.shape[-1]
    for part in range(2):
        start_ref[part] = turned(exit_ref[own, part], row_at, col_at)
    down_ref[...] = second_difference(size, row_at)
    across_ref[...] = second_difference(size, col_at)


def turn_kernel(corner_ref, wave_ref, turned_ref):
    count = wave_ref.shape[0]

    def one(position, _):
        for part in range(2):
            turned_ref[position, part] = turned(
                wave_ref[position, part], corner_ref[0, position], corner_ref[1, position]
            )
        return 0

    lax.fori_loop(0, count, one, 0)


def back(down, across, chi_re, chi_im):
    def laplacian(field):
        rows = jnp.dot(down, field, preferred_element_type=f32)
        return rows + jnp.dot(field, across, preferred_element_type=f32)

    lap_re = laplacian(chi_re)
    lap_im = laplacian(chi_im)
    lap2_re = laplacian(lap_re.astype(bf16))
    lap2_im = laplacian(lap_im.astype(bf16))
    more_re = 2.0 * lap_re + (damping * lap2_re + turning * lap2_im)
    more_im = 2.0 * lap_im + (damping * lap2_im - turning * lap2_re)
    spread_re = chi_re.astype(f32) + (damping * more_re + turning * more_im)
    spread_im = chi_im.astype(f32) + (damping * more_im - turning * more_re)
    return spread_re, spread_im


def pass_group(down, across, chi_re, chi_im, count, window_of, keep):
    for layer in range(count - 1, -1, -1):
        spread_re, spread_im = back(down, across, chi_re, chi_im)
        keep(layer, spread_re, spread_im)
        win_re, win_im = window_of(layer)
        chi_re = (win_re * spread_re + win_im * spread_im).astype(bf16)
        chi_im = (win_re * spread_im - win_im * spread_re).astype(bf16)
    return chi_re, chi_im


def in_pieces(count, window):
    rows = window // chunk_count
    near = [(apart, slice(0, window)) for apart in distances(count)[:-far]]
    cut = [(count - far + i, slice(c * rows, (c + 1) * rows)) for c in range(chunk_count) for i in range(far)]
    return list(zip(*near, *cut))


def decoded(held_ref, layer):
    return [jnp.log(held_ref[layer, part].astype(f32)) * (1.0 / code_gain) for part in range(2)]


def first_kernel(start_ref, down_ref, across_ref, *refs):
    *win_refs, leave_ref, held_ref = refs
    count, _, window, _ = held_ref.shape
    own = place_in_group(count)
    for win_ref, apart, here in zip(win_refs, *in_pieces(count, window)):
        held_ref[own ^ apart, :, here] = win_ref[...]
    leave_ref[0], leave_ref[1] = pass_group(
        down_ref[...],
        across_ref[...],
        start_ref[0],
        start_ref[1],
        count,
        functools.partial(decoded, held_ref),
        lambda *_: None,
    )


def next_kernel(is_last, start_ref, come_ref, down_ref, across_ref, held_ref, *refs):
    count, _, window, _ = held_ref.shape
    own = place_in_group(count)
    behind = (lax.axis_index("sec") + count).astype(jnp.int32)
    at_end = jnp.full((window, window), behind, jnp.int32) >= lax.axis_size("sec")
    chi_re, chi_im = (
        jnp.where(at_end, start_ref[part].astype(f32), come_ref[part].astype(f32)).astype(bf16) for part in range(2)
    )

    def keep(layer, spread_re, spread_im):
        if is_last:
            refs[-1][layer, 0] = spread_re.astype(bf16)
            refs[-1][layer, 1] = spread_im.astype(bf16)

    chi = pass_group(
        down_ref[...], across_ref[...], chi_re, chi_im, count, functools.partial(decoded, held_ref), keep
    )
    if not is_last:
        refs[0][0], refs[0][1] = chi
        return
    for spread_ref, apart, here in zip(refs, *in_pieces(count, window)):
        spread_ref[...] = refs[-1][own ^ apart, :, here]


def gradient_kernel(base, corner_ref, wave_ref, *refs):
    *spread_refs, own_ref, away_ref = refs
    rows = own_ref.shape[1]
    window = wave_ref.shape[-1]
    tall = 16
    own = place_in_group(wave_ref.shape[0])

    def one(block, _):
        at = pl.multiple_of(block * tall, tall)
        sums = [jnp.zeros((tall, window), f32) for _ in range(8)]
        here = pl.ds(base + at, tall)
        for apart, spread_ref in zip(distances(len(spread_refs)), spread_refs):
            position = own ^ apart
            there = pl.ds(at, tall) if apart >= len(spread_refs) - far else here
            in_mine, in_left = first_masks(corner_ref, position, base + at, (tall, window))
            wave_re, wave_im = (wave_ref[position, part, here, :].astype(f32) for part in range(2))
            spread_re, spread_im = (spread_ref[part, there, :].astype(f32) for part in range(2))
            parts = (
                wave_re * spread_re + wave_im * spread_im,
                wave_re * spread_im - wave_im * spread_re,
            )
            for part in range(2):
                left = jnp.where(in_left, parts[part], 0.0)
                right = jnp.where(in_left, 0.0, parts[part])
                for side, value in enumerate((left, right)):
                    sums[4 * part + side] += jnp.where(in_mine, value, 0.0)
                    sums[4 * part + 2 + side] += jnp.where(in_mine, 0.0, value)
        for part in range(2):
            for side in range(2):
                cols = pl.ds(side * window, window)
                own_ref[part, pl.ds(at, tall), cols] = sums[4 * part + side]
                away_ref[part, pl.ds(at, tall), cols] = sums[4 * part + 2 + side].astype(bf16)
        return 0

    lax.fori_loop(0, rows // tall, one, 0)


def finish_kernel(*refs):
    out_ref = refs[-1]
    rows = refs[0].shape[1]
    for chunk in range(chunk_count):
        own_ref, come_ref = refs[2 * chunk : 2 * chunk + 2]
        out_ref[:, pl.ds(chunk * rows, rows), :] = own_ref[...] + come_ref[...].astype(f32)


def shape_of(dims, dtype):
    return jax.ShapeDtypeStruct(dims, dtype)


def on_device(obj_amp, obj_phase, forward_waves, exit_adjoint, offsets):
    sections = lax.axis_size("sec")
    count, _, window, _ = exit_adjoint.shape
    _, half, width = obj_amp.shape
    group_count = sections // count
    chunks = range(chunk_count)
    rows = half // chunk_count
    piece = (2, rows, width)
    wave = (2, window, window)
    corners = offsets.T

    def to_other_half(value):
        return lax.ppermute(value, "scan", [(0, 1), (1, 0)])

    def to_distance(value, d):
        return lax.ppermute(value, "sec", [(s, s ^ d) for s in range(sections)])

    def exchange(near):
        return [to_distance(value, d) if d else value for d, value in zip(distances(count), near)]

    def exchange_far(values):
        return [to_distance(value, count - far + i) for i, value in enumerate(values)]

    mine = [coded(obj_amp[0, c * rows : (c + 1) * rows], obj_phase[0, c * rows : (c + 1) * rows]) for c in chunks]
    other = [to_other_half(value) for value in mine]
    ready = call(ready_kernel, [shape_of(wave, bf16)] + [shape_of((window, window), bf16)] * 2, prefetch=1)
    start, down, across = ready(corners, exit_adjoint)
    other[0], start, down, across = lax.optimization_barrier((other[0], start, down, across))
    near, distant = [], []
    for c in chunks:
        cut = call(
            functools.partial(cut_kernel, c * rows, count),
            [shape_of(wave, bf16)] * (count - far) + [shape_of((2, rows, window), bf16)] * far,
            prefetch=1,
            aliases={3 + i: i for i in range(len(near))},
        )
        if distant:
            other[c], distant[-far] = lax.optimization_barrier((other[c], distant[-far]))
        cuts = cut(corners, mine[c], other[c], *near)
        near = cuts[: count - far]
        distant += exchange_far(cuts[count - far :])
    windows = exchange(near) + distant
    waves = call(turn_kernel, shape_of(forward_waves.shape[1:], bf16), prefetch=1)(corners, forward_waves[0])

    pieces = [shape_of(wave, bf16)] * (count - far) + [shape_of((2, rows, window), bf16)] * (far * chunk_count)
    cost = (count * 16 * window**3, count * 2 * window**2)
    first = call(first_kernel, [shape_of(wave, bf16), shape_of((count,) + wave, bf16)], cost=cost, grant=12)
    leave, held = first(start, down, across, *windows)
    for stage in range(1, group_count):
        come = lax.ppermute(leave, "sec", [(s, s - count) for s in range(count, sections)])
        come, waves = lax.optimization_barrier((come, waves))
        is_last = stage == group_count - 1
        through = call(
            functools.partial(next_kernel, is_last),
            pieces if is_last else shape_of(wave, bf16),
            scratch=[pltpu.VMEM((count,) + wave, bf16)] if is_last else [],
            cost=cost,
            grant=12,
        )
        leave = through(start, come, down, across, held)

    near, distant = leave[: count - far], leave[count - far :]
    came_far = [exchange_far(distant[:far])]
    came = exchange(near)
    came_far += [exchange_far(distant[c * far : (c + 1) * far]) for c in chunks[1:]]
    sums = []
    for c in chunks:
        gradient = call(
            functools.partial(gradient_kernel, c * rows), [shape_of(piece, f32), shape_of(piece, bf16)], prefetch=1
        )
        keep, away = gradient(corners, waves, *came, *came_far[c])
        sums += [keep, to_other_half(away)]
    return call(finish_kernel, shape_of((2, half, width), f32))(*sums)[None]


def solution(mesh):
    in_specs = (
        P("sec", "scan", None),
        P("sec", "scan", None),
        P("sec", "scan", None, None, None),
        P("scan", None, None, None),
        P("scan", None),
    )
    out_specs = P("sec", None, "scan", None)
    return jax.shard_map(
        on_device, mesh=mesh, in_specs=in_specs, out_specs=out_specs, check_vma=False
    )
```

```python
import functools
import math

import jax
import jax.numpy as jnp
from jax import lax
from jax.experimental import pallas as pl
from jax.experimental.pallas import tpu as pltpu
from jax.sharding import PartitionSpec as P

SUBSTEPS = 2
damping = 0.0005
turning = 0.011
code_gain = 83.0
chunk_count = 2
far = 2
f32 = jnp.float32
bf16 = jnp.bfloat16


def call(kernel, out_shape, prefetch=0, scratch=(), cost=(0, 0), grant=6, aliases=None):
    flops, transcendentals = cost

    def run(*args):
        moved = sum(a.size * a.dtype.itemsize for a in jax.tree.leaves((args, out_shape)))
        vmem = pl.BlockSpec(memory_space=pltpu.VMEM)
        return pl.pallas_call(
            kernel,
            grid_spec=pltpu.PrefetchScalarGridSpec(
                num_scalar_prefetch=prefetch,
                grid=(1,),
                in_specs=[vmem] * (len(args) - prefetch),
                out_specs=jax.tree.map(lambda _: vmem, out_shape),
                scratch_shapes=list(scratch),
            ),
            out_shape=out_shape,
            input_output_aliases=aliases or {},
            cost_estimate=pl.CostEstimate(flops=flops, bytes_accessed=moved, transcendentals=transcendentals),
            compiler_params=pltpu.CompilerParams(vmem_limit_bytes=grant * 2**20),
        )(*args)

    return run


def place_in_group(count):
    return lax.rem(lax.axis_index("sec").astype(jnp.int32), count)


def position_at(place, count):
    hops = lax.axis_size("sec") // count - 1 - lax.axis_index("sec").astype(jnp.int32) // count
    return place ^ (count // 2 * lax.rem(hops, 2) * lax.rem(place, 2))


def coded(amp, phase):
    half = 0.5 * phase
    square = half * half
    sine = jnp.full_like(half, 1.0 / math.factorial(13))
    cosine = jnp.full_like(half, 1.0 / math.factorial(12))
    for power in (11, 9, 7, 5, 3, 1):
        sign = -1.0 if power % 4 == 3 else 1.0
        sine = sine * square + sign / math.factorial(power)
        cosine = cosine * square + sign / math.factorial(power - 1)
    sine = sine * half
    trans_re = amp * (1.0 - 2.0 * sine * sine)
    trans_im = amp * (2.0 * sine * cosine)
    return jnp.stack([jnp.exp(code_gain * trans_re).astype(bf16), jnp.exp(code_gain * trans_im).astype(bf16)])


def first_masks(corner_ref, position, base, shape):
    place = lax.axis_index("scan").astype(jnp.int32)
    row = lax.broadcasted_iota(jnp.int32, shape, 0) + base
    col = lax.broadcasted_iota(jnp.int32, shape, 1)
    at_first = (row >= corner_ref[0, position]).astype(jnp.int32)
    return at_first != place, col >= corner_ref[1, position]


def distances(count):
    return sorted(range(count), key=lambda d: (d >= count - far, d > 0, d == 1, d % 2, d))


def cut_kernel(base, count, corner_ref, mine_ref, other_ref, *refs):
    own = place_in_group(count)
    _, rows, width = mine_ref.shape
    window = width // 2
    for i, (apart, win_ref) in enumerate(zip(distances(count), refs[-count:])):
        here = pl.ds(0 if i >= count - far else base, rows)
        if base and i < count - far:
            win_ref[:, :base] = refs[i][:, :base]
        in_mine, in_left = first_masks(corner_ref, position_at(own ^ apart, count), base, (rows, window))
        for part in range(2):
            left, right = (
                jnp.where(in_mine, mine_ref[part, :, cols].astype(f32), other_ref[part, :, cols].astype(f32))
                for cols in (slice(0, window), slice(window, 2 * window))
            )
            win_ref[part, here, :] = jnp.where(in_left, left, right).astype(bf16)


def turned(wave, row_at, col_at):
    window = wave.shape[-1]
    wave = pltpu.roll(wave.astype(f32), lax.rem(row_at, window), 0)
    return pltpu.roll(wave, lax.rem(col_at, window), 1).astype(bf16)


def second_difference(size, break_at):
    row = lax.broadcasted_iota(jnp.int32, (size, size), 0)
    col = lax.broadcasted_iota(jnp.int32, (size, size), 1)
    start = lax.rem(break_at, size)
    before = (lax.rem(row - col + size, size) == 1) & (row != start)
    after = (lax.rem(col - row + size, size) == 1) & (col != start)
    return jnp.where(row == col, -2.0, jnp.where(before | after, 1.0, 0.0)).astype(bf16)


def ready_kernel(corner_ref, exit_ref, start_ref, down_ref, across_ref):
    count = exit_ref.shape[0]
    own = position_at(place_in_group(count), count)
    row_at = corner_ref[0, own]
    col_at = corner_ref[1, own]
    size = start_ref.shape[-1]
    for part in range(2):
        start_ref[part] = turned(exit_ref[own, part], row_at, col_at)
    down_ref[...] = second_difference(size, row_at)
    across_ref[...] = second_difference(size, col_at)


def turn_kernel(corner_ref, wave_ref, turned_ref):
    count = wave_ref.shape[0]

    def one(position, _):
        for part in range(2):
            turned_ref[position, part] = turned(
                wave_ref[position, part], corner_ref[0, position], corner_ref[1, position]
            )
        return 0

    lax.fori_loop(0, count, one, 0)


def back(down, across, chi):
    half = chi.shape[0] // 2

    def laplacian(field):
        columns = jnp.dot(field, across, preferred_element_type=f32)
        return [
            jnp.dot(down, field[here], preferred_element_type=f32) + columns[here]
            for here in (slice(0, half), slice(half, 2 * half))
        ]

    lap_re, lap_im = laplacian(chi)
    lap2_re, lap2_im = laplacian(jnp.concatenate([lap_re.astype(bf16), lap_im.astype(bf16)], axis=0))
    more_re = 2.0 * lap_re + (damping * lap2_re + turning * lap2_im)
    more_im = 2.0 * lap_im + (damping * lap2_im - turning * lap2_re)
    spread_re = chi[:half].astype(f32) + (damping * more_re + turning * more_im)
    spread_im = chi[half:].astype(f32) + (damping * more_im - turning * more_re)
    return spread_re, spread_im


def pass_group(down, across, chi, count, window_of, keep):
    half = chi.shape[0] // 2
    for layer in range(count - 1, -1, -1):
        spread_re, spread_im = back(down, across, chi)
        keep(layer, spread_re, spread_im)
        win_re, win_im = window_of(layer)
        chi_re = (win_re * spread_re + win_im * spread_im).astype(bf16)
        chi_im = (win_re * spread_im - win_im * spread_re).astype(bf16)
        chi = jnp.concatenate([chi_re, chi_im], axis=0)
    return chi[:half], chi[half:]


def in_pieces(count, window):
    rows = window // chunk_count
    near = [(apart, slice(0, window)) for apart in distances(count)[:-far]]
    cut = [(count - far + i, slice(c * rows, (c + 1) * rows)) for c in range(chunk_count) for i in range(far)]
    return list(zip(*near, *cut))


def decoded(held_ref, layer):
    return [jnp.log(held_ref[layer, part].astype(f32)) * (1.0 / code_gain) for part in range(2)]


def first_kernel(start_ref, down_ref, across_ref, *refs):
    *win_refs, leave_ref, held_ref = refs
    count, _, window, _ = held_ref.shape
    own = place_in_group(count)
    for win_ref, apart, here in zip(win_refs, *in_pieces(count, window)):
        held_ref[own ^ apart, :, here] = win_ref[...]
    leave_ref[0], leave_ref[1] = pass_group(
        down_ref[...],
        across_ref[...],
        jnp.concatenate([start_ref[0], start_ref[1]], axis=0),
        count,
        functools.partial(decoded, held_ref),
        lambda *_: None,
    )


def next_kernel(is_last, start_ref, come_ref, down_ref, across_ref, held_ref, *refs):
    count, _, window, _ = held_ref.shape
    own = place_in_group(count)
    behind = (lax.axis_index("sec") + count).astype(jnp.int32)
    at_end = jnp.full((window, window), behind, jnp.int32) >= lax.axis_size("sec")
    chi_re, chi_im = (
        jnp.where(at_end, start_ref[part].astype(f32), come_ref[part].astype(f32)).astype(bf16) for part in range(2)
    )

    def keep(layer, spread_re, spread_im):
        if is_last:
            refs[-1][layer, 0] = spread_re.astype(bf16)
            refs[-1][layer, 1] = spread_im.astype(bf16)

    chi = jnp.concatenate([chi_re, chi_im], axis=0)
    chi = pass_group(down_ref[...], across_ref[...], chi, count, functools.partial(decoded, held_ref), keep)
    if not is_last:
        refs[0][0], refs[0][1] = chi
        return
    for spread_ref, apart, here in zip(refs, *in_pieces(count, window)):
        spread_ref[...] = refs[-1][own ^ apart, :, here]


def gradient_kernel(base, corner_ref, wave_ref, *refs):
    *spread_refs, own_ref, away_ref = refs
    rows = own_ref.shape[1]
    window = wave_ref.shape[-1]
    tall = 16
    own = place_in_group(wave_ref.shape[0])

    def one(block, _):
        at = pl.multiple_of(block * tall, tall)
        sums = [jnp.zeros((tall, window), f32) for _ in range(8)]
        here = pl.ds(base + at, tall)
        for apart, spread_ref in zip(distances(len(spread_refs)), spread_refs):
            position = position_at(own ^ apart, len(spread_refs))
            there = pl.ds(at, tall) if apart >= len(spread_refs) - far else here
            in_mine, in_left = first_masks(corner_ref, position, base + at, (tall, window))
            wave_re, wave_im = (wave_ref[position, part, here, :].astype(f32) for part in range(2))
            spread_re, spread_im = (spread_ref[part, there, :].astype(f32) for part in range(2))
            parts = (
                wave_re * spread_re + wave_im * spread_im,
                wave_re * spread_im - wave_im * spread_re,
            )
            for part in range(2):
                own_part = jnp.where(in_mine, parts[part], 0.0)
                sums[4 * part] += parts[part]
                sums[4 * part + 1] += own_part
                sums[4 * part + 2] += jnp.where(in_left, parts[part], 0.0)
                sums[4 * part + 3] += jnp.where(in_left, own_part, 0.0)
        left, right = pl.ds(0, window), pl.ds(window, window)
        for part in range(2):
            every, mine, at_left, mine_left = sums[4 * part : 4 * part + 4]
            own_ref[part, pl.ds(at, tall), left] = mine_left
            own_ref[part, pl.ds(at, tall), right] = mine - mine_left
            away_ref[part, pl.ds(at, tall), left] = (at_left - mine_left).astype(bf16)
            away_ref[part, pl.ds(at, tall), right] = ((every - mine) - (at_left - mine_left)).astype(bf16)
        return 0

    lax.fori_loop(0, rows // tall, one, 0)


def finish_kernel(*refs):
    out_ref = refs[-1]
    rows = refs[0].shape[1]
    for chunk in range(chunk_count):
        own_ref, come_ref = refs[2 * chunk : 2 * chunk + 2]
        out_ref[:, pl.ds(chunk * rows, rows), :] = own_ref[...] + come_ref[...].astype(f32)


def shape_of(dims, dtype):
    return jax.ShapeDtypeStruct(dims, dtype)


def on_device(obj_amp, obj_phase, forward_waves, exit_adjoint, offsets):
    sections = lax.axis_size("sec")
    count, _, window, _ = exit_adjoint.shape
    _, half, width = obj_amp.shape
    group_count = sections // count
    chunks = range(chunk_count)
    rows = half // chunk_count
    piece = (2, rows, width)
    wave = (2, window, window)
    corners = offsets.T

    def to_other_half(value):
        return lax.ppermute(value, "scan", [(0, 1), (1, 0)])

    def to_distance(value, d):
        return lax.ppermute(value, "sec", [(s, s ^ d) for s in range(sections)])

    def exchange(near):
        return [to_distance(value, d) if d else value for d, value in zip(distances(count), near)]

    def exchange_far(values):
        return [to_distance(value, count - far + i) for i, value in enumerate(values)]

    mine = [coded(obj_amp[0, c * rows : (c + 1) * rows], obj_phase[0, c * rows : (c + 1) * rows]) for c in chunks]
    other = [to_other_half(value) for value in mine]
    ready = call(ready_kernel, [shape_of(wave, bf16)] + [shape_of((window, window), bf16)] * 2, prefetch=1)
    start, down, across = ready(corners, exit_adjoint)
    other[0], start, down, across = lax.optimization_barrier((other[0], start, down, across))
    near, distant = [], []
    for c in chunks:
        cut = call(
            functools.partial(cut_kernel, c * rows, count),
            [shape_of(wave, bf16)] * (count - far) + [shape_of((2, rows, window), bf16)] * far,
            prefetch=1,
            aliases={3 + i: i for i in range(len(near))},
        )
        if distant:
            other[c], distant[-far] = lax.optimization_barrier((other[c], distant[-far]))
        cuts = cut(corners, mine[c], other[c], *near)
        near = cuts[: count - far]
        distant += exchange_far(cuts[count - far :])
    windows = exchange(near) + distant
    waves = call(turn_kernel, shape_of(forward_waves.shape[1:], bf16), prefetch=1)(corners, forward_waves[0])

    pieces = [shape_of(wave, bf16)] * (count - far) + [shape_of((2, rows, window), bf16)] * (far * chunk_count)
    cost = (count * 16 * window**3, count * 2 * window**2)
    first = call(first_kernel, [shape_of(wave, bf16), shape_of((count,) + wave, bf16)], cost=cost, grant=12)
    leave, held = first(start, down, across, *windows)
    for stage in range(1, group_count):
        come = lax.ppermute(
            leave, "sec", [(s, (s - count) ^ (s % 2 * count // 2)) for s in range(count, sections)]
        )
        come, waves = lax.optimization_barrier((come, waves))
        is_last = stage == group_count - 1
        through = call(
            functools.partial(next_kernel, is_last),
            pieces if is_last else shape_of(wave, bf16),
            scratch=[pltpu.VMEM((count,) + wave, bf16)] if is_last else [],
            cost=cost,
            grant=12,
        )
        leave = through(start, come, down, across, held)

    near, distant = leave[: count - far], leave[count - far :]
    came_far = [exchange_far(distant[:far])]
    came = exchange(near)
    came_far += [exchange_far(distant[c * far : (c + 1) * far]) for c in chunks[1:]]
    sums = []
    for c in chunks:
        gradient = call(
            functools.partial(gradient_kernel, c * rows), [shape_of(piece, f32), shape_of(piece, bf16)], prefetch=1
        )
        keep, away = gradient(corners, waves, *came, *came_far[c])
        sums += [keep, to_other_half(away)]
    return call(finish_kernel, shape_of((2, half, width), f32))(*sums)[None]


def solution(mesh):
    in_specs = (
        P("sec", "scan", None),
        P("sec", "scan", None),
        P("sec", "scan", None, None, None),
        P("scan", None, None, None),
        P("scan", None),
    )
    out_specs = P("sec", None, "scan", None)
    return jax.shard_map(
        on_device, mesh=mesh, in_specs=in_specs, out_specs=out_specs, check_vma=False
    )
```

```python
import functools
import math

import jax
import jax.numpy as jnp
from jax import lax
from jax.experimental import pallas as pl
from jax.experimental.pallas import tpu as pltpu
from jax.sharding import PartitionSpec as P

SUBSTEPS = 2
damping = 0.0005
turning = 0.011
code_gain = 83.0
chunk_count = 2
far = 2
f32 = jnp.float32
bf16 = jnp.bfloat16


def call(kernel, out_shape, prefetch=0, scratch=(), cost=(0, 0), grant=6, aliases=None):
    flops, transcendentals = cost

    def run(*args):
        moved = sum(a.size * a.dtype.itemsize for a in jax.tree.leaves((args, out_shape)))
        vmem = pl.BlockSpec(memory_space=pltpu.VMEM)
        return pl.pallas_call(
            kernel,
            grid_spec=pltpu.PrefetchScalarGridSpec(
                num_scalar_prefetch=prefetch,
                grid=(1,),
                in_specs=[vmem] * (len(args) - prefetch),
                out_specs=jax.tree.map(lambda _: vmem, out_shape),
                scratch_shapes=list(scratch),
            ),
            out_shape=out_shape,
            input_output_aliases=aliases or {},
            cost_estimate=pl.CostEstimate(flops=flops, bytes_accessed=moved, transcendentals=transcendentals),
            compiler_params=pltpu.CompilerParams(vmem_limit_bytes=grant * 2**20),
        )(*args)

    return run


def place_in_group(count):
    return lax.rem(lax.axis_index("sec").astype(jnp.int32), count)


def position_at(place, count):
    hops = lax.axis_size("sec") // count - 1 - lax.axis_index("sec").astype(jnp.int32) // count
    return place ^ (count // 2 * lax.rem(hops, 2))


def coded(amp, phase):
    half = 0.5 * phase
    square = half * half
    sine = jnp.full_like(half, 1.0 / math.factorial(13))
    cosine = jnp.full_like(half, 1.0 / math.factorial(12))
    for power in (11, 9, 7, 5, 3, 1):
        sign = -1.0 if power % 4 == 3 else 1.0
        sine = sine * square + sign / math.factorial(power)
        cosine = cosine * square + sign / math.factorial(power - 1)
    sine = sine * half
    trans_re = amp * (1.0 - 2.0 * sine * sine)
    trans_im = amp * (2.0 * sine * cosine)
    return jnp.stack([jnp.exp(code_gain * trans_re).astype(bf16), jnp.exp(code_gain * trans_im).astype(bf16)])


def first_masks(corner_ref, position, base, shape):
    place = lax.axis_index("scan").astype(jnp.int32)
    row = lax.broadcasted_iota(jnp.int32, shape, 0) + base
    col = lax.broadcasted_iota(jnp.int32, shape, 1)
    at_first = (row >= corner_ref[0, position]).astype(jnp.int32)
    return at_first != place, col >= corner_ref[1, position]


def distances(count):
    return sorted(range(count), key=lambda d: (d >= count - far, d > 0, d == 1, d % 2, d))


def cut_kernel(base, count, corner_ref, mine_ref, other_ref, *refs):
    own = place_in_group(count)
    _, rows, width = mine_ref.shape
    window = width // 2
    for i, (apart, win_ref) in enumerate(zip(distances(count), refs[-count:])):
        here = pl.ds(0 if i >= count - far else base, rows)
        if base and i < count - far:
            win_ref[:, :base] = refs[i][:, :base]
        in_mine, in_left = first_masks(corner_ref, position_at(own ^ apart, count), base, (rows, window))
        for part in range(2):
            left, right = (
                jnp.where(in_mine, mine_ref[part, :, cols].astype(f32), other_ref[part, :, cols].astype(f32))
                for cols in (slice(0, window), slice(window, 2 * window))
            )
            win_ref[part, here, :] = jnp.where(in_left, left, right).astype(bf16)


def turned(wave, row_at, col_at):
    window = wave.shape[-1]
    wave = pltpu.roll(wave.astype(f32), lax.rem(row_at, window), 0)
    return pltpu.roll(wave, lax.rem(col_at, window), 1).astype(bf16)


def second_difference(size, break_at):
    row = lax.broadcasted_iota(jnp.int32, (size, size), 0)
    col = lax.broadcasted_iota(jnp.int32, (size, size), 1)
    start = lax.rem(break_at, size)
    before = (lax.rem(row - col + size, size) == 1) & (row != start)
    after = (lax.rem(col - row + size, size) == 1) & (col != start)
    return jnp.where(row == col, -2.0, jnp.where(before | after, 1.0, 0.0)).astype(bf16)


def ready_kernel(corner_ref, exit_ref, start_ref, down_ref, across_ref):
    count = exit_ref.shape[0]
    own = position_at(place_in_group(count), count)
    row_at = corner_ref[0, own]
    col_at = corner_ref[1, own]
    size = start_ref.shape[-1]
    for part in range(2):
        start_ref[part] = turned(exit_ref[own, part], row_at, col_at)
    down_ref[...] = second_difference(size, row_at)
    across_ref[...] = second_difference(size, col_at)


def turn_kernel(corner_ref, wave_ref, turned_ref):
    count = wave_ref.shape[0]

    def one(position, _):
        for part in range(2):
            turned_ref[position, part] = turned(
                wave_ref[position, part], corner_ref[0, position], corner_ref[1, position]
            )
        return 0

    lax.fori_loop(0, count, one, 0)


def back(down, across, chi_re, chi_im):
    def laplacian(field):
        rows = jnp.dot(down, field, preferred_element_type=f32)
        return rows + jnp.dot(field, across, preferred_element_type=f32)

    lap_re = laplacian(chi_re)
    lap_im = laplacian(chi_im)
    lap2_re = laplacian(lap_re.astype(bf16))
    lap2_im = laplacian(lap_im.astype(bf16))
    more_re = 2.0 * lap_re + (damping * lap2_re + turning * lap2_im)
    more_im = 2.0 * lap_im + (damping * lap2_im - turning * lap2_re)
    spread_re = chi_re.astype(f32) + (damping * more_re + turning * more_im)
    spread_im = chi_im.astype(f32) + (damping * more_im - turning * more_re)
    return spread_re, spread_im


def pass_group(down, across, chi_re, chi_im, count, window_of, keep):
    for layer in range(count - 1, -1, -1):
        spread_re, spread_im = back(down, across, chi_re, chi_im)
        keep(layer, spread_re, spread_im)
        win_re, win_im = window_of(layer)
        chi_re = (win_re * spread_re + win_im * spread_im).astype(bf16)
        chi_im = (win_re * spread_im - win_im * spread_re).astype(bf16)
    return chi_re, chi_im


def in_pieces(count, window):
    rows = window // chunk_count
    near = [(apart, slice(0, window)) for apart in distances(count)[:-far]]
    cut = [(count - far + i, slice(c * rows, (c + 1) * rows)) for c in range(chunk_count) for i in range(far)]
    return list(zip(*near, *cut))


def decoded(held_ref, layer):
    return [jnp.log(held_ref[layer, part].astype(f32)) * (1.0 / code_gain) for part in range(2)]


def first_kernel(start_ref, down_ref, across_ref, *refs):
    *win_refs, leave_ref, held_ref = refs
    count, _, window, _ = held_ref.shape
    own = place_in_group(count)
    for win_ref, apart, here in zip(win_refs, *in_pieces(count, window)):
        held_ref[own ^ apart, :, here] = win_ref[...]
    leave_ref[0], leave_ref[1] = pass_group(
        down_ref[...],
        across_ref[...],
        start_ref[0],
        start_ref[1],
        count,
        functools.partial(decoded, held_ref),
        lambda *_: None,
    )


def next_kernel(is_last, start_ref, come_ref, down_ref, across_ref, held_ref, *refs):
    count, _, window, _ = held_ref.shape
    own = place_in_group(count)
    behind = (lax.axis_index("sec") + count).astype(jnp.int32)
    at_end = jnp.full((window, window), behind, jnp.int32) >= lax.axis_size("sec")
    chi_re, chi_im = (
        jnp.where(at_end, start_ref[part].astype(f32), come_ref[part].astype(f32)).astype(bf16) for part in range(2)
    )

    def keep(layer, spread_re, spread_im):
        if is_last:
            refs[-1][layer, 0] = spread_re.astype(bf16)
            refs[-1][layer, 1] = spread_im.astype(bf16)

    chi = pass_group(
        down_ref[...], across_ref[...], chi_re, chi_im, count, functools.partial(decoded, held_ref), keep
    )
    if not is_last:
        refs[0][0], refs[0][1] = chi
        return
    for spread_ref, apart, here in zip(refs, *in_pieces(count, window)):
        spread_ref[...] = refs[-1][own ^ apart, :, here]


def gradient_kernel(base, corner_ref, wave_ref, *refs):
    *spread_refs, own_ref, away_ref = refs
    rows = own_ref.shape[1]
    window = wave_ref.shape[-1]
    tall = 16
    own = place_in_group(wave_ref.shape[0])

    def one(block, _):
        at = pl.multiple_of(block * tall, tall)
        sums = [jnp.zeros((tall, window), f32) for _ in range(8)]
        here = pl.ds(base + at, tall)
        for apart, spread_ref in zip(distances(len(spread_refs)), spread_refs):
            position = position_at(own ^ apart, len(spread_refs))
            there = pl.ds(at, tall) if apart >= len(spread_refs) - far else here
            in_mine, in_left = first_masks(corner_ref, position, base + at, (tall, window))
            wave_re, wave_im = (wave_ref[position, part, here, :].astype(f32) for part in range(2))
            spread_re, spread_im = (spread_ref[part, there, :].astype(f32) for part in range(2))
            parts = (
                wave_re * spread_re + wave_im * spread_im,
                wave_re * spread_im - wave_im * spread_re,
            )
            for part in range(2):
                own_part = jnp.where(in_mine, parts[part], 0.0)
                sums[4 * part] += parts[part]
                sums[4 * part + 1] += own_part
                sums[4 * part + 2] += jnp.where(in_left, parts[part], 0.0)
                sums[4 * part + 3] += jnp.where(in_left, own_part, 0.0)
        left, right = pl.ds(0, window), pl.ds(window, window)
        for part in range(2):
            every, mine, at_left, mine_left = sums[4 * part : 4 * part + 4]
            own_ref[part, pl.ds(at, tall), left] = mine_left
            own_ref[part, pl.ds(at, tall), right] = mine - mine_left
            away_ref[part, pl.ds(at, tall), left] = (at_left - mine_left).astype(bf16)
            away_ref[part, pl.ds(at, tall), right] = ((every - mine) - (at_left - mine_left)).astype(bf16)
        return 0

    lax.fori_loop(0, rows // tall, one, 0)


def finish_kernel(*refs):
    out_ref = refs[-1]
    rows = refs[0].shape[1]
    for chunk in range(chunk_count):
        own_ref, come_ref = refs[2 * chunk : 2 * chunk + 2]
        out_ref[:, pl.ds(chunk * rows, rows), :] = own_ref[...] + come_ref[...].astype(f32)


def shape_of(dims, dtype):
    return jax.ShapeDtypeStruct(dims, dtype)


def on_device(obj_amp, obj_phase, forward_waves, exit_adjoint, offsets):
    sections = lax.axis_size("sec")
    count, _, window, _ = exit_adjoint.shape
    _, half, width = obj_amp.shape
    group_count = sections // count
    chunks = range(chunk_count)
    rows = half // chunk_count
    piece = (2, rows, width)
    wave = (2, window, window)
    corners = offsets.T

    def to_other_half(value):
        return lax.ppermute(value, "scan", [(0, 1), (1, 0)])

    def to_distance(value, d):
        return lax.ppermute(value, "sec", [(s, s ^ d) for s in range(sections)])

    def exchange(near):
        return [to_distance(value, d) if d else value for d, value in zip(distances(count), near)]

    def exchange_far(values):
        return [to_distance(value, count - far + i) for i, value in enumerate(values)]

    mine = [coded(obj_amp[0, c * rows : (c + 1) * rows], obj_phase[0, c * rows : (c + 1) * rows]) for c in chunks]
    other = [to_other_half(value) for value in mine]
    ready = call(ready_kernel, [shape_of(wave, bf16)] + [shape_of((window, window), bf16)] * 2, prefetch=1)
    start, down, across = ready(corners, exit_adjoint)
    other[0], start, down, across = lax.optimization_barrier((other[0], start, down, across))
    near, distant = [], []
    for c in chunks:
        cut = call(
            functools.partial(cut_kernel, c * rows, count),
            [shape_of(wave, bf16)] * (count - far) + [shape_of((2, rows, window), bf16)] * far,
            prefetch=1,
            aliases={3 + i: i for i in range(len(near))},
        )
        if distant:
            other[c], distant[-far] = lax.optimization_barrier((other[c], distant[-far]))
        cuts = cut(corners, mine[c], other[c], *near)
        near = cuts[: count - far]
        distant += exchange_far(cuts[count - far :])
    windows = exchange(near) + distant
    waves = call(turn_kernel, shape_of(forward_waves.shape[1:], bf16), prefetch=1)(corners, forward_waves[0])

    pieces = [shape_of(wave, bf16)] * (count - far) + [shape_of((2, rows, window), bf16)] * (far * chunk_count)
    cost = (count * 16 * window**3, count * 2 * window**2)
    first = call(first_kernel, [shape_of(wave, bf16), shape_of((count,) + wave, bf16)], cost=cost, grant=12)
    leave, held = first(start, down, across, *windows)
    for stage in range(1, group_count):
        come = lax.ppermute(
            leave, "sec", [(s, (s - count) ^ (count // 2)) for s in range(count, sections)]
        )
        come, waves = lax.optimization_barrier((come, waves))
        is_last = stage == group_count - 1
        through = call(
            functools.partial(next_kernel, is_last),
            pieces if is_last else shape_of(wave, bf16),
            scratch=[pltpu.VMEM((count,) + wave, bf16)] if is_last else [],
            cost=cost,
            grant=12,
        )
        leave = through(start, come, down, across, held)

    near, distant = leave[: count - far], leave[count - far :]
    came_far = [exchange_far(distant[:far])]
    came = exchange(near)
    came_far += [exchange_far(distant[c * far : (c + 1) * far]) for c in chunks[1:]]
    sums = []
    for c in chunks:
        gradient = call(
            functools.partial(gradient_kernel, c * rows), [shape_of(piece, f32), shape_of(piece, bf16)], prefetch=1
        )
        keep, away = gradient(corners, waves, *came, *came_far[c])
        sums += [keep, to_other_half(away)]
    return call(finish_kernel, shape_of((2, half, width), f32))(*sums)[None]


def solution(mesh):
    in_specs = (
        P("sec", "scan", None),
        P("sec", "scan", None),
        P("sec", "scan", None, None, None),
        P("scan", None, None, None),
        P("scan", None),
    )
    out_specs = P("sec", None, "scan", None)
    return jax.shard_map(
        on_device, mesh=mesh, in_specs=in_specs, out_specs=out_specs, check_vma=False
    )
```

```python
import functools
import math

import jax
import jax.numpy as jnp
from jax import lax
from jax.experimental import pallas as pl
from jax.experimental.pallas import tpu as pltpu
from jax.sharding import PartitionSpec as P

SUBSTEPS = 2
damping = 0.0005
turning = 0.011
code_gain = 83.0
chunk_count = 2
far = 2
f32 = jnp.float32
bf16 = jnp.bfloat16


def call(kernel, out_shape, prefetch=0, scratch=(), cost=(0, 0), grant=6, aliases=None):
    flops, transcendentals = cost

    def run(*args):
        moved = sum(a.size * a.dtype.itemsize for a in jax.tree.leaves((args, out_shape)))
        vmem = pl.BlockSpec(memory_space=pltpu.VMEM)
        return pl.pallas_call(
            kernel,
            grid_spec=pltpu.PrefetchScalarGridSpec(
                num_scalar_prefetch=prefetch,
                grid=(1,),
                in_specs=[vmem] * (len(args) - prefetch),
                out_specs=jax.tree.map(lambda _: vmem, out_shape),
                scratch_shapes=list(scratch),
            ),
            out_shape=out_shape,
            input_output_aliases=aliases or {},
            cost_estimate=pl.CostEstimate(flops=flops, bytes_accessed=moved, transcendentals=transcendentals),
            compiler_params=pltpu.CompilerParams(vmem_limit_bytes=grant * 2**20),
        )(*args)

    return run


def place_in_group(count):
    return lax.rem(lax.axis_index("sec").astype(jnp.int32), count)


def position_at(place, count):
    hops = lax.axis_size("sec") // count - 1 - lax.axis_index("sec").astype(jnp.int32) // count
    return place ^ (count // 2 * lax.rem(hops, 2))


def coded(amp, phase):
    half = 0.5 * phase
    square = half * half
    sine = jnp.full_like(half, 1.0 / math.factorial(13))
    cosine = jnp.full_like(half, 1.0 / math.factorial(12))
    for power in (11, 9, 7, 5, 3, 1):
        sign = -1.0 if power % 4 == 3 else 1.0
        sine = sine * square + sign / math.factorial(power)
        cosine = cosine * square + sign / math.factorial(power - 1)
    sine = sine * half
    trans_re = amp * (1.0 - 2.0 * sine * sine)
    trans_im = amp * (2.0 * sine * cosine)
    return jnp.stack([jnp.exp(code_gain * trans_re).astype(bf16), jnp.exp(code_gain * trans_im).astype(bf16)])


def first_masks(corner_ref, position, base, shape):
    place = lax.axis_index("scan").astype(jnp.int32)
    row = lax.broadcasted_iota(jnp.int32, shape, 0) + base
    col = lax.broadcasted_iota(jnp.int32, shape, 1)
    at_first = (row >= corner_ref[0, position]).astype(jnp.int32)
    return at_first != place, col >= corner_ref[1, position]


def distances(count):
    return sorted(range(count), key=lambda d: (d >= count - far, d > 0, d == 1, d % 2, d))


def cut_kernel(base, count, corner_ref, mine_ref, other_ref, *refs):
    own = place_in_group(count)
    _, rows, width = mine_ref.shape
    window = width // 2
    for i, (apart, win_ref) in enumerate(zip(distances(count), refs[-count:])):
        here = pl.ds(0 if i >= count - far else base, rows)
        if base and i < count - far:
            win_ref[:, :base] = refs[i][:, :base]
        in_mine, in_left = first_masks(corner_ref, position_at(own ^ apart, count), base, (rows, window))
        for part in range(2):
            left, right = (
                jnp.where(in_mine, mine_ref[part, :, cols].astype(f32), other_ref[part, :, cols].astype(f32))
                for cols in (slice(0, window), slice(window, 2 * window))
            )
            win_ref[part, here, :] = jnp.where(in_left, left, right).astype(bf16)


def turned(wave, row_at, col_at):
    window = wave.shape[-1]
    wave = pltpu.roll(wave.astype(f32), lax.rem(row_at, window), 0)
    return pltpu.roll(wave, lax.rem(col_at, window), 1).astype(bf16)


def second_difference(size, break_at):
    row = lax.broadcasted_iota(jnp.int32, (size, size), 0)
    col = lax.broadcasted_iota(jnp.int32, (size, size), 1)
    start = lax.rem(break_at, size)
    before = (lax.rem(row - col + size, size) == 1) & (row != start)
    after = (lax.rem(col - row + size, size) == 1) & (col != start)
    return jnp.where(row == col, -2.0, jnp.where(before | after, 1.0, 0.0)).astype(bf16)


def ready_kernel(corner_ref, exit_ref, start_ref, down_ref, across_ref):
    count = exit_ref.shape[0]
    own = position_at(place_in_group(count), count)
    row_at = corner_ref[0, own]
    col_at = corner_ref[1, own]
    size = start_ref.shape[-1]
    for part in range(2):
        start_ref[part] = turned(exit_ref[own, part], row_at, col_at)
    down_ref[...] = second_difference(size, row_at)
    across_ref[...] = second_difference(size, col_at)


def turn_kernel(corner_ref, wave_ref, turned_ref):
    count = wave_ref.shape[0]

    def one(position, _):
        for part in range(2):
            turned_ref[position, part] = turned(
                wave_ref[position, part], corner_ref[0, position], corner_ref[1, position]
            )
        return 0

    lax.fori_loop(0, count, one, 0)


def back(down, across, chi_re, chi_im):
    def laplacian(field):
        rows = jnp.dot(down, field, preferred_element_type=f32)
        return rows + jnp.dot(field, across, preferred_element_type=f32)

    lap_re = laplacian(chi_re)
    lap_im = laplacian(chi_im)
    lap2_re = laplacian(lap_re.astype(bf16))
    lap2_im = laplacian(lap_im.astype(bf16))
    more_re = 2.0 * lap_re + (damping * lap2_re + turning * lap2_im)
    more_im = 2.0 * lap_im + (damping * lap2_im - turning * lap2_re)
    spread_re = chi_re.astype(f32) + (damping * more_re + turning * more_im)
    spread_im = chi_im.astype(f32) + (damping * more_im - turning * more_re)
    return spread_re, spread_im


def pass_group(down, across, chi_re, chi_im, count, window_of, keep):
    for layer in range(count - 1, -1, -1):
        spread_re, spread_im = back(down, across, chi_re, chi_im)
        keep(layer, spread_re, spread_im)
        win_re, win_im = window_of(layer)
        chi_re = (win_re * spread_re + win_im * spread_im).astype(bf16)
        chi_im = (win_re * spread_im - win_im * spread_re).astype(bf16)
    return chi_re, chi_im


def in_pieces(count, window):
    rows = window // chunk_count
    near = [(apart, slice(0, window)) for apart in distances(count)[:-far]]
    cut = [(count - far + i, slice(c * rows, (c + 1) * rows)) for c in range(chunk_count) for i in range(far)]
    return list(zip(*near, *cut))


def decoded(held_ref, layer):
    return [jnp.log(held_ref[layer, part].astype(f32)) * (1.0 / code_gain) for part in range(2)]


def first_kernel(start_ref, down_ref, across_ref, *refs):
    *win_refs, leave_ref, held_ref = refs
    count, _, window, _ = held_ref.shape
    own = place_in_group(count)
    for win_ref, apart, here in zip(win_refs, *in_pieces(count, window)):
        held_ref[own ^ apart, :, here] = win_ref[...]
    leave_ref[0], leave_ref[1] = pass_group(
        down_ref[...],
        across_ref[...],
        start_ref[0],
        start_ref[1],
        count,
        functools.partial(decoded, held_ref),
        lambda *_: None,
    )


def next_kernel(is_last, start_ref, come_ref, down_ref, across_ref, held_ref, *refs):
    count, _, window, _ = held_ref.shape
    own = place_in_group(count)
    behind = (lax.axis_index("sec") + count).astype(jnp.int32)
    at_end = jnp.full((window, window), behind, jnp.int32) >= lax.axis_size("sec")
    chi_re, chi_im = (
        jnp.where(at_end, start_ref[part].astype(f32), come_ref[part].astype(f32)).astype(bf16) for part in range(2)
    )

    def keep(layer, spread_re, spread_im):
        if is_last:
            refs[-1][layer, 0] = spread_re.astype(bf16)
            refs[-1][layer, 1] = spread_im.astype(bf16)

    chi = pass_group(
        down_ref[...], across_ref[...], chi_re, chi_im, count, functools.partial(decoded, held_ref), keep
    )
    if not is_last:
        refs[0][0], refs[0][1] = chi
        return
    for spread_ref, apart, here in zip(refs, *in_pieces(count, window)):
        spread_ref[...] = refs[-1][own ^ apart, :, here]


def add_kernel(base, picks, begun, ends, corner_ref, wave_ref, *refs):
    spread_refs, refs = refs[: len(picks)], refs[len(picks) :]
    count, _, window, _ = wave_ref.shape
    rows = window // chunk_count
    tall = 16
    own = place_in_group(count)

    def one(block, _):
        at = pl.multiple_of(block * tall, tall)
        rows_at = pl.ds(at, tall)
        here = pl.ds(base + at, tall)
        sums = [refs[0][i, rows_at, :] if begun else jnp.zeros((tall, window), f32) for i in range(8)]
        for apart, spread_ref in zip(picks, spread_refs):
            position = position_at(own ^ apart, count)
            there = rows_at if apart >= count - far else here
            in_mine, in_left = first_masks(corner_ref, position, base + at, (tall, window))
            wave_re, wave_im = (wave_ref[position, part, here, :].astype(f32) for part in range(2))
            spread_re, spread_im = (spread_ref[part, there, :].astype(f32) for part in range(2))
            parts = (
                wave_re * spread_re + wave_im * spread_im,
                wave_re * spread_im - wave_im * spread_re,
            )
            for part in range(2):
                own_part = jnp.where(in_mine, parts[part], 0.0)
                sums[4 * part] += parts[part]
                sums[4 * part + 1] += own_part
                sums[4 * part + 2] += jnp.where(in_left, parts[part], 0.0)
                sums[4 * part + 3] += jnp.where(in_left, own_part, 0.0)
        if not ends:
            for i in range(8):
                refs[-1][i, rows_at, :] = sums[i]
            return 0
        own_ref, away_ref = refs[-2:]
        left, right = pl.ds(0, window), pl.ds(window, window)
        for part in range(2):
            every, mine, at_left, mine_left = sums[4 * part : 4 * part + 4]
            own_ref[part, rows_at, left] = mine_left
            own_ref[part, rows_at, right] = mine - mine_left
            away_ref[part, rows_at, left] = (at_left - mine_left).astype(bf16)
            away_ref[part, rows_at, right] = ((every - mine) - (at_left - mine_left)).astype(bf16)
        return 0

    lax.fori_loop(0, rows // tall, one, 0)


def finish(chunk, own, come, shape, before):
    def kernel(own_ref, come_ref, *refs):
        refs[-1][...] = own_ref[...] + come_ref[...].astype(f32)

    vmem = pl.BlockSpec(memory_space=pltpu.VMEM)
    return pl.pallas_call(
        kernel,
        grid=(1,),
        in_specs=[vmem, vmem] + [pl.BlockSpec(memory_space=pl.ANY)] * len(before),
        out_specs=pl.BlockSpec(own.shape, lambda _: (0, chunk, 0)),
        out_shape=shape_of(shape, f32),
        input_output_aliases={2: 0} if before else {},
        compiler_params=pltpu.CompilerParams(vmem_limit_bytes=6 * 2**20),
    )(own, come, *before)


def shape_of(dims, dtype):
    return jax.ShapeDtypeStruct(dims, dtype)


def on_device(obj_amp, obj_phase, forward_waves, exit_adjoint, offsets):
    sections = lax.axis_size("sec")
    count, _, window, _ = exit_adjoint.shape
    _, half, width = obj_amp.shape
    group_count = sections // count
    chunks = range(chunk_count)
    rows = half // chunk_count
    piece = (2, rows, width)
    wave = (2, window, window)
    corners = offsets.T

    def to_other_half(value):
        return lax.ppermute(value, "scan", [(0, 1), (1, 0)])

    def to_distance(value, d):
        return lax.ppermute(value, "sec", [(s, s ^ d) for s in range(sections)])

    def exchange(near):
        return [to_distance(value, d) if d else value for d, value in zip(distances(count), near)]

    def exchange_far(values):
        return [to_distance(value, count - far + i) for i, value in enumerate(values)]

    mine, other = [], []
    for c in chunks:
        source = [array[0, c * rows : (c + 1) * rows] for array in (obj_amp, obj_phase)]
        if c > 0:
            source, mine[-1] = lax.optimization_barrier((source, mine[-1]))
        mine.append(coded(*source))
        other.append(to_other_half(mine[-1]))
    ready = call(ready_kernel, [shape_of(wave, bf16)] + [shape_of((window, window), bf16)] * 2, prefetch=1)
    start, down, across = ready(corners, exit_adjoint)
    other[0], start, down, across = lax.optimization_barrier((other[0], start, down, across))
    near, distant = [], []
    for c in chunks:
        cut = call(
            functools.partial(cut_kernel, c * rows, count),
            [shape_of(wave, bf16)] * (count - far) + [shape_of((2, rows, window), bf16)] * far,
            prefetch=1,
            aliases={3 + i: i for i in range(len(near))},
        )
        if distant:
            other[c], distant[-far] = lax.optimization_barrier((other[c], distant[-far]))
        cuts = cut(corners, mine[c], other[c], *near)
        near = cuts[: count - far]
        distant += exchange_far(cuts[count - far :])
    windows = exchange(near) + distant
    waves = call(turn_kernel, shape_of(forward_waves.shape[1:], bf16), prefetch=1)(corners, forward_waves[0])

    pieces = [shape_of(wave, bf16)] * (count - far) + [shape_of((2, rows, window), bf16)] * (far * chunk_count)
    cost = (count * 16 * window**3, count * 2 * window**2)
    first = call(first_kernel, [shape_of(wave, bf16), shape_of((count,) + wave, bf16)], cost=cost, grant=12)
    leave, held = first(start, down, across, *windows)
    for stage in range(1, group_count):
        come = lax.ppermute(
            leave, "sec", [(s, (s - count) ^ (count // 2)) for s in range(count, sections)]
        )
        come, waves = lax.optimization_barrier((come, waves))
        is_last = stage == group_count - 1
        through = call(
            functools.partial(next_kernel, is_last),
            pieces if is_last else shape_of(wave, bf16),
            scratch=[pltpu.VMEM((count,) + wave, bf16)] if is_last else [],
            cost=cost,
            grant=12,
        )
        leave = through(start, come, down, across, held)

    near, distant = leave[: count - far], leave[count - far :]
    came_far = [exchange_far(distant[:far])]
    came = exchange(near)
    came_far += [exchange_far(distant[c * far : (c + 1) * far]) for c in chunks[1:]]
    order = distances(count)
    early, late = order[: count // 2 - 1], order[count // 2 - 1 : count - far]
    spread_at = dict(zip(order, came))

    def add(c, picks, sums, ends):
        spreads = [came_far[c][d - count + far] if d >= count - far else spread_at[d] for d in picks]
        kernel = functools.partial(add_kernel, c * rows, picks, bool(sums), ends)
        given = [shape_of(piece, f32), shape_of(piece, bf16)] if ends else shape_of((8, rows, window), f32)
        return call(kernel, given, prefetch=1)(corners, waves, *spreads, *sums)

    done = []
    for c in chunks:
        if c == 0:
            sums = add(c, early + order[-far:], [], False)
            keep, away = add(c, late, [sums], True)
        else:
            sums = add(c, early, [], False)
            sums, away = lax.optimization_barrier((sums, away))
            sums = add(c, late, [sums], False)
            done.append((keep, to_other_half(away)))
            keep, away = add(c, order[-far:], [sums], True)
    done.append((keep, to_other_half(away)))
    result = []
    for c in chunks:
        result = [finish(c, *done[c], (2, half, width), result)]
    return result[0][None]


def solution(mesh):
    in_specs = (
        P("sec", "scan", None),
        P("sec", "scan", None),
        P("sec", "scan", None, None, None),
        P("scan", None, None, None),
        P("scan", None),
    )
    out_specs = P("sec", None, "scan", None)
    return jax.shard_map(
        on_device, mesh=mesh, in_specs=in_specs, out_specs=out_specs, check_vma=False
    )
```

```python
import functools
import math

import jax
import jax.numpy as jnp
from jax import lax
from jax.experimental import pallas as pl
from jax.experimental.pallas import tpu as pltpu
from jax.sharding import PartitionSpec as P

SUBSTEPS = 2
damping = 0.0005
turning = 0.011
code_gain = 83.0
chunk_count = 2
far = 2
f32 = jnp.float32
bf16 = jnp.bfloat16


def call(kernel, out_shape, prefetch=0, scratch=(), cost=(0, 0), grant=6, aliases=None):
    flops, transcendentals = cost

    def run(*args):
        moved = sum(a.size * a.dtype.itemsize for a in jax.tree.leaves((args, out_shape)))
        vmem = pl.BlockSpec(memory_space=pltpu.VMEM)
        return pl.pallas_call(
            kernel,
            grid_spec=pltpu.PrefetchScalarGridSpec(
                num_scalar_prefetch=prefetch,
                grid=(1,),
                in_specs=[vmem] * (len(args) - prefetch),
                out_specs=jax.tree.map(lambda _: vmem, out_shape),
                scratch_shapes=list(scratch),
            ),
            out_shape=out_shape,
            input_output_aliases=aliases or {},
            cost_estimate=pl.CostEstimate(flops=flops, bytes_accessed=moved, transcendentals=transcendentals),
            compiler_params=pltpu.CompilerParams(vmem_limit_bytes=grant * 2**20),
        )(*args)

    return run


def place_in_group(count):
    return lax.rem(lax.axis_index("sec").astype(jnp.int32), count)


def position_at(place, count):
    hops = lax.axis_size("sec") // count - 1 - lax.axis_index("sec").astype(jnp.int32) // count
    return place ^ (count // 2 * lax.rem(hops, 2))


def coded(amp, phase):
    half = 0.5 * phase
    square = half * half
    sine = jnp.full_like(half, 1.0 / math.factorial(13))
    cosine = jnp.full_like(half, 1.0 / math.factorial(12))
    for power in (11, 9, 7, 5, 3, 1):
        sign = -1.0 if power % 4 == 3 else 1.0
        sine = sine * square + sign / math.factorial(power)
        cosine = cosine * square + sign / math.factorial(power - 1)
    sine = sine * half
    trans_re = amp * (1.0 - 2.0 * sine * sine)
    trans_im = amp * (2.0 * sine * cosine)
    return jnp.stack([jnp.exp(code_gain * trans_re).astype(bf16), jnp.exp(code_gain * trans_im).astype(bf16)])


def first_masks(corner_ref, position, base, shape):
    place = lax.axis_index("scan").astype(jnp.int32)
    row = lax.broadcasted_iota(jnp.int32, shape, 0) + base
    col = lax.broadcasted_iota(jnp.int32, shape, 1)
    at_first = (row >= corner_ref[0, position]).astype(jnp.int32)
    return at_first != place, col >= corner_ref[1, position]


def distances(count):
    return sorted(range(count), key=lambda d: (d >= count - far, d > 0, d == 1, d % 2, d))


def select_window(corner_ref, position, base, mine_ref, other_ref):
    _, rows, width = mine_ref.shape
    window = width // 2
    in_mine, in_left = first_masks(corner_ref, position, base, (rows, window))
    for part in range(2):
        left, right = (
            jnp.where(in_mine, mine_ref[part, :, cols].astype(f32), other_ref[part, :, cols].astype(f32))
            for cols in (slice(0, window), slice(window, 2 * window))
        )
        yield jnp.where(in_left, left, right).astype(bf16)


def cut_kernel(base, count, corner_ref, mine_ref, other_ref, *refs):
    own = place_in_group(count)
    here = pl.ds(base, mine_ref.shape[1])
    near = distances(count)[:-far]
    for i, (apart, win_ref) in enumerate(zip(near, refs[-len(near) :])):
        if base:
            win_ref[:, :base] = refs[i][:, :base]
        position = position_at(own ^ apart, count)
        for part, value in enumerate(select_window(corner_ref, position, base, mine_ref, other_ref)):
            win_ref[part, here, :] = value


def cut_far_kernel(base, count, corner_ref, mine_ref, other_ref, *win_refs):
    own = place_in_group(count)
    for apart, win_ref in enumerate(win_refs):
        position = position_at(own ^ apart, count)
        for part, value in enumerate(select_window(corner_ref, position, base, mine_ref, other_ref)):
            win_ref[part] = value


def turned(wave, row_at, col_at):
    window = wave.shape[-1]
    wave = pltpu.roll(wave.astype(f32), lax.rem(row_at, window), 0)
    return pltpu.roll(wave, lax.rem(col_at, window), 1).astype(bf16)


def second_difference(size, break_at):
    row = lax.broadcasted_iota(jnp.int32, (size, size), 0)
    col = lax.broadcasted_iota(jnp.int32, (size, size), 1)
    start = lax.rem(break_at, size)
    before = (lax.rem(row - col + size, size) == 1) & (row != start)
    after = (lax.rem(col - row + size, size) == 1) & (col != start)
    return jnp.where(row == col, -2.0, jnp.where(before | after, 1.0, 0.0)).astype(bf16)


def ready_kernel(corner_ref, exit_ref, start_ref, down_ref, across_ref):
    count = exit_ref.shape[0]
    own = position_at(place_in_group(count), count)
    row_at = corner_ref[0, own]
    col_at = corner_ref[1, own]
    size = start_ref.shape[-1]
    for part in range(2):
        start_ref[part] = turned(exit_ref[own, part], row_at, col_at)
    down_ref[...] = second_difference(size, row_at)
    across_ref[...] = second_difference(size, col_at)


def turn_kernel(corner_ref, wave_ref, turned_ref):
    count = wave_ref.shape[0]

    def one(position, _):
        for part in range(2):
            turned_ref[position, part] = turned(
                wave_ref[position, part], corner_ref[0, position], corner_ref[1, position]
            )
        return 0

    lax.fori_loop(0, count, one, 0)


def back(down, across, chi_re, chi_im):
    def laplacian(field):
        rows = jnp.dot(down, field, preferred_element_type=f32)
        return rows + jnp.dot(field, across, preferred_element_type=f32)

    lap_re = laplacian(chi_re)
    lap_im = laplacian(chi_im)
    lap2_re = laplacian(lap_re.astype(bf16))
    lap2_im = laplacian(lap_im.astype(bf16))
    more_re = 2.0 * lap_re + (damping * lap2_re + turning * lap2_im)
    more_im = 2.0 * lap_im + (damping * lap2_im - turning * lap2_re)
    spread_re = chi_re.astype(f32) + (damping * more_re + turning * more_im)
    spread_im = chi_im.astype(f32) + (damping * more_im - turning * more_re)
    return spread_re, spread_im


def pass_group(down, across, chi_re, chi_im, count, window_of, keep):
    for layer in range(count - 1, -1, -1):
        spread_re, spread_im = back(down, across, chi_re, chi_im)
        keep(layer, spread_re, spread_im)
        win_re, win_im = window_of(layer)
        chi_re = (win_re * spread_re + win_im * spread_im).astype(bf16)
        chi_im = (win_re * spread_im - win_im * spread_re).astype(bf16)
    return chi_re, chi_im


def in_pieces(count, window):
    rows = window // chunk_count
    near = [(apart, slice(0, window)) for apart in distances(count)[:-far]]
    cut = [(count - far + i, slice(c * rows, (c + 1) * rows)) for c in range(chunk_count) for i in range(far)]
    return list(zip(*near, *cut))


def decoded(held_ref, layer):
    return [jnp.log(held_ref[layer, part].astype(f32)) * (1.0 / code_gain) for part in range(2)]


def first_kernel(start_ref, down_ref, across_ref, *refs):
    *win_refs, leave_ref, held_ref = refs
    count, _, window, _ = held_ref.shape
    own = place_in_group(count)
    for win_ref, apart, here in zip(win_refs, *in_pieces(count, window)):
        held_ref[own ^ apart, :, here] = win_ref[...]
    leave_ref[0], leave_ref[1] = pass_group(
        down_ref[...],
        across_ref[...],
        start_ref[0],
        start_ref[1],
        count,
        functools.partial(decoded, held_ref),
        lambda *_: None,
    )


def next_kernel(is_last, start_ref, come_ref, down_ref, across_ref, held_ref, *refs):
    count, _, window, _ = held_ref.shape
    own = place_in_group(count)
    behind = (lax.axis_index("sec") + count).astype(jnp.int32)
    at_end = jnp.full((window, window), behind, jnp.int32) >= lax.axis_size("sec")
    chi_re, chi_im = (
        jnp.where(at_end, start_ref[part].astype(f32), come_ref[part].astype(f32)).astype(bf16) for part in range(2)
    )

    def keep(layer, spread_re, spread_im):
        if is_last:
            refs[-1][layer, 0] = spread_re.astype(bf16)
            refs[-1][layer, 1] = spread_im.astype(bf16)

    chi = pass_group(
        down_ref[...], across_ref[...], chi_re, chi_im, count, functools.partial(decoded, held_ref), keep
    )
    if not is_last:
        refs[0][0], refs[0][1] = chi
        return
    for spread_ref, apart, here in zip(refs, *in_pieces(count, window)):
        spread_ref[...] = refs[-1][own ^ apart, :, here]


def add_kernel(base, picks, begun, ends, corner_ref, wave_ref, *refs):
    spread_refs, refs = refs[: len(picks)], refs[len(picks) :]
    count, _, window, _ = wave_ref.shape
    rows = window // chunk_count
    tall = 16
    own = place_in_group(count)

    def one(block, _):
        at = pl.multiple_of(block * tall, tall)
        rows_at = pl.ds(at, tall)
        here = pl.ds(base + at, tall)
        sums = [refs[0][i, rows_at, :] if begun else jnp.zeros((tall, window), f32) for i in range(8)]
        for apart, spread_ref in zip(picks, spread_refs):
            position = position_at(own ^ apart, count)
            there = rows_at if apart >= count - far else here
            in_mine, in_left = first_masks(corner_ref, position, base + at, (tall, window))
            wave_re, wave_im = (wave_ref[position, part, here, :].astype(f32) for part in range(2))
            spread_re, spread_im = (spread_ref[part, there, :].astype(f32) for part in range(2))
            parts = (
                wave_re * spread_re + wave_im * spread_im,
                wave_re * spread_im - wave_im * spread_re,
            )
            for part in range(2):
                own_part = jnp.where(in_mine, parts[part], 0.0)
                sums[4 * part] += parts[part]
                sums[4 * part + 1] += own_part
                sums[4 * part + 2] += jnp.where(in_left, parts[part], 0.0)
                sums[4 * part + 3] += jnp.where(in_left, own_part, 0.0)
        if not ends:
            for i in range(8):
                refs[-1][i, rows_at, :] = sums[i]
            return 0
        own_ref, away_ref = refs[-2:]
        left, right = pl.ds(0, window), pl.ds(window, window)
        for part in range(2):
            every, mine, at_left, mine_left = sums[4 * part : 4 * part + 4]
            own_ref[part, rows_at, left] = mine_left
            own_ref[part, rows_at, right] = mine - mine_left
            away_ref[part, rows_at, left] = (at_left - mine_left).astype(bf16)
            away_ref[part, rows_at, right] = ((every - mine) - (at_left - mine_left)).astype(bf16)
        return 0

    lax.fori_loop(0, rows // tall, one, 0)


def finish(chunk, own, come, shape, before):
    def kernel(own_ref, come_ref, *refs):
        refs[-1][...] = own_ref[...] + come_ref[...].astype(f32)

    vmem = pl.BlockSpec(memory_space=pltpu.VMEM)
    return pl.pallas_call(
        kernel,
        grid=(1,),
        in_specs=[vmem, vmem] + [pl.BlockSpec(memory_space=pl.ANY)] * len(before),
        out_specs=pl.BlockSpec(own.shape, lambda _: (0, chunk, 0)),
        out_shape=shape_of(shape, f32),
        input_output_aliases={2: 0} if before else {},
        compiler_params=pltpu.CompilerParams(vmem_limit_bytes=6 * 2**20),
    )(own, come, *before)


def shape_of(dims, dtype):
    return jax.ShapeDtypeStruct(dims, dtype)


def on_device(obj_amp, obj_phase, forward_waves, exit_adjoint, offsets):
    sections = lax.axis_size("sec")
    count, _, window, _ = exit_adjoint.shape
    _, half, width = obj_amp.shape
    group_count = sections // count
    chunks = range(chunk_count)
    rows = half // chunk_count
    piece = (2, rows, width)
    wave = (2, window, window)
    corners = offsets.T

    def to_other_half(value):
        return lax.ppermute(value, "scan", [(0, 1), (1, 0)])

    def to_distance(value, d):
        return lax.ppermute(value, "sec", [(s, s ^ d) for s in range(sections)])

    def exchange(near):
        return [to_distance(value, d) if d else value for d, value in zip(distances(count), near)]

    def exchange_far(values):
        return [to_distance(value, count - far + i) for i, value in enumerate(values)]

    mine, other, far_mine = [], [], []
    source = (obj_amp, obj_phase)
    for c in chunks:
        if c > 0:
            source, mine[-1] = lax.optimization_barrier((source, mine[-1]))
        mine.append(coded(*(array[0, c * rows : (c + 1) * rows] for array in source)))
        other.append(to_other_half(mine[-1]))
        far_mine.append(to_distance(mine[-1], count - far))
    ready = call(ready_kernel, [shape_of(wave, bf16)] + [shape_of((window, window), bf16)] * 2, prefetch=1)
    start, down, across = ready(corners, exit_adjoint)
    other[0], start, down, across = lax.optimization_barrier((other[0], start, down, across))
    near, distant = [], []
    for c in chunks:
        cut = call(
            functools.partial(cut_kernel, c * rows, count),
            [shape_of(wave, bf16)] * (count - far),
            prefetch=1,
            aliases={3 + i: i for i in range(len(near))},
        )
        near = cut(corners, mine[c], other[c], *near)
    far_mine[-1], near = lax.optimization_barrier((far_mine[-1], near))
    for c in chunks:
        cut_far = call(
            functools.partial(cut_far_kernel, c * rows, count), [shape_of((2, rows, window), bf16)] * far, prefetch=1
        )
        kept, given = cut_far(corners, far_mine[c], to_other_half(far_mine[c]))
        distant += [kept, to_distance(given, 1)]
    windows = exchange(near) + distant
    waves = call(turn_kernel, shape_of(forward_waves.shape[1:], bf16), prefetch=1)(corners, forward_waves[0])

    pieces = [shape_of(wave, bf16)] * (count - far) + [shape_of((2, rows, window), bf16)] * (far * chunk_count)
    cost = (count * 16 * window**3, count * 2 * window**2)
    first = call(first_kernel, [shape_of(wave, bf16), shape_of((count,) + wave, bf16)], cost=cost, grant=12)
    leave, held = first(start, down, across, *windows)
    for stage in range(1, group_count):
        come = lax.ppermute(
            leave, "sec", [(s, (s - count) ^ (count // 2)) for s in range(count, sections)]
        )
        come, waves = lax.optimization_barrier((come, waves))
        is_last = stage == group_count - 1
        through = call(
            functools.partial(next_kernel, is_last),
            pieces if is_last else shape_of(wave, bf16),
            scratch=[pltpu.VMEM((count,) + wave, bf16)] if is_last else [],
            cost=cost,
            grant=12,
        )
        leave = through(start, come, down, across, held)

    near, distant = leave[: count - far], leave[count - far :]
    came_far = [exchange_far(distant[:far])]
    came = exchange(near)
    came_far += [exchange_far(distant[c * far : (c + 1) * far]) for c in chunks[1:]]
    order = distances(count)
    early, late = order[: count // 2 - 1], order[count // 2 - 1 : count - far]
    spread_at = dict(zip(order, came))

    def add(c, picks, sums, ends):
        spreads = [came_far[c][d - count + far] if d >= count - far else spread_at[d] for d in picks]
        kernel = functools.partial(add_kernel, c * rows, picks, bool(sums), ends)
        given = [shape_of(piece, f32), shape_of(piece, bf16)] if ends else shape_of((8, rows, window), f32)
        return call(kernel, given, prefetch=1)(corners, waves, *spreads, *sums)

    done = []
    for c in chunks:
        if c == 0:
            sums = add(c, early + order[-far:], [], False)
            keep, away = add(c, late, [sums], True)
        else:
            sums = add(c, early, [], False)
            sums, away = lax.optimization_barrier((sums, away))
            sums = add(c, late, [sums], False)
            done.append((keep, to_other_half(away)))
            keep, away = add(c, order[-far:], [sums], True)
    done.append((keep, to_other_half(away)))
    result = []
    for c in chunks:
        result = [finish(c, *done[c], (2, half, width), result)]
    return result[0][None]


def solution(mesh):
    in_specs = (
        P("sec", "scan", None),
        P("sec", "scan", None),
        P("sec", "scan", None, None, None),
        P("scan", None, None, None),
        P("scan", None),
    )
    out_specs = P("sec", None, "scan", None)
    return jax.shard_map(
        on_device, mesh=mesh, in_specs=in_specs, out_specs=out_specs, check_vma=False
    )
```

```python
import functools
import math

import jax
import jax.numpy as jnp
from jax import lax
from jax.experimental import pallas as pl
from jax.experimental.pallas import tpu as pltpu
from jax.sharding import PartitionSpec as P

SUBSTEPS = 2
damping = 0.0005
turning = 0.011
code_gain = 83.0
chunk_count = 2
far = 2
f32 = jnp.float32
bf16 = jnp.bfloat16


def call(kernel, out_shape, prefetch=0, scratch=(), cost=(0, 0), grant=6, aliases=None):
    flops, transcendentals = cost

    def run(*args):
        moved = sum(a.size * a.dtype.itemsize for a in jax.tree.leaves((args, out_shape)))
        vmem = pl.BlockSpec(memory_space=pltpu.VMEM)
        return pl.pallas_call(
            kernel,
            grid_spec=pltpu.PrefetchScalarGridSpec(
                num_scalar_prefetch=prefetch,
                grid=(1,),
                in_specs=[vmem] * (len(args) - prefetch),
                out_specs=jax.tree.map(lambda _: vmem, out_shape),
                scratch_shapes=list(scratch),
            ),
            out_shape=out_shape,
            input_output_aliases=aliases or {},
            cost_estimate=pl.CostEstimate(flops=flops, bytes_accessed=moved, transcendentals=transcendentals),
            compiler_params=pltpu.CompilerParams(vmem_limit_bytes=grant * 2**20),
        )(*args)

    return run


def place_in_group(count):
    return lax.rem(lax.axis_index("sec").astype(jnp.int32), count)


def position_at(place, count):
    hops = lax.axis_size("sec") // count - 1 - lax.axis_index("sec").astype(jnp.int32) // count
    return place ^ (count // 2 * lax.rem(hops, 2))


def coded(amp, phase):
    half = 0.5 * phase
    square = half * half
    sine = jnp.full_like(half, 1.0 / math.factorial(13))
    cosine = jnp.full_like(half, 1.0 / math.factorial(12))
    for power in (11, 9, 7, 5, 3, 1):
        sign = -1.0 if power % 4 == 3 else 1.0
        sine = sine * square + sign / math.factorial(power)
        cosine = cosine * square + sign / math.factorial(power - 1)
    sine = sine * half
    trans_re = amp * (1.0 - 2.0 * sine * sine)
    trans_im = amp * (2.0 * sine * cosine)
    return jnp.stack([jnp.exp(code_gain * trans_re).astype(bf16), jnp.exp(code_gain * trans_im).astype(bf16)])


def first_masks(corner_ref, position, base, shape):
    place = lax.axis_index("scan").astype(jnp.int32)
    row = lax.broadcasted_iota(jnp.int32, shape, 0) + base
    col = lax.broadcasted_iota(jnp.int32, shape, 1)
    at_first = (row >= corner_ref[0, position]).astype(jnp.int32)
    return at_first != place, col >= corner_ref[1, position]


def distances(count):
    return sorted(range(count), key=lambda d: (d >= count - far, d > 0, d == 1, d % 2, d))


def select_window(corner_ref, position, base, mine_ref, other_ref):
    _, rows, width = mine_ref.shape
    window = width // 2
    in_mine, in_left = first_masks(corner_ref, position, base, (rows, window))
    for part in range(2):
        left, right = (
            jnp.where(in_mine, mine_ref[part, :, cols].astype(f32), other_ref[part, :, cols].astype(f32))
            for cols in (slice(0, window), slice(window, 2 * window))
        )
        yield jnp.where(in_left, left, right).astype(bf16)


def cut_kernel(base, count, corner_ref, mine_ref, other_ref, *refs):
    own = place_in_group(count)
    here = pl.ds(base, mine_ref.shape[1])
    near = distances(count)[:-far]
    for i, (apart, win_ref) in enumerate(zip(near, refs[-len(near) :])):
        if base:
            win_ref[:, :base] = refs[i][:, :base]
        position = position_at(own ^ apart, count)
        for part, value in enumerate(select_window(corner_ref, position, base, mine_ref, other_ref)):
            win_ref[part, here, :] = value


def cut_far_kernel(base, count, corner_ref, mine_ref, other_ref, *win_refs):
    own = place_in_group(count)
    for apart, win_ref in enumerate(win_refs):
        position = position_at(own ^ apart, count)
        for part, value in enumerate(select_window(corner_ref, position, base, mine_ref, other_ref)):
            win_ref[part] = value


def turned(wave, row_at, col_at):
    window = wave.shape[-1]
    wave = pltpu.roll(wave.astype(f32), lax.rem(row_at, window), 0)
    return pltpu.roll(wave, lax.rem(col_at, window), 1).astype(bf16)


def second_difference(size, break_at):
    row = lax.broadcasted_iota(jnp.int32, (size, size), 0)
    col = lax.broadcasted_iota(jnp.int32, (size, size), 1)
    start = lax.rem(break_at, size)
    before = (lax.rem(row - col + size, size) == 1) & (row != start)
    after = (lax.rem(col - row + size, size) == 1) & (col != start)
    return jnp.where(row == col, -2.0, jnp.where(before | after, 1.0, 0.0)).astype(bf16)


def ready_kernel(corner_ref, exit_ref, start_ref, down_ref, across_ref):
    count = exit_ref.shape[0]
    own = position_at(place_in_group(count), count)
    row_at = corner_ref[0, own]
    col_at = corner_ref[1, own]
    size = start_ref.shape[-1]
    for part in range(2):
        start_ref[part] = turned(exit_ref[own, part], row_at, col_at)
    down_ref[...] = second_difference(size, row_at)
    across_ref[...] = second_difference(size, col_at)


def turn_kernel(corner_ref, wave_ref, turned_ref, given_ref):
    count = wave_ref.shape[0]

    def one(position, _):
        for part in range(2):
            turned_ref[position, part] = turned(
                wave_ref[position, part], corner_ref[0, position], corner_ref[1, position]
            )
        return 0

    lax.fori_loop(0, count, one, 0)
    own = place_in_group(count)
    for i in range(far):
        given_ref[i] = turned_ref[position_at(own ^ (count - far + i), count)]


def back(down, across, chi_re, chi_im):
    def laplacian(field):
        rows = jnp.dot(down, field, preferred_element_type=f32)
        return rows + jnp.dot(field, across, preferred_element_type=f32)

    lap_re = laplacian(chi_re)
    lap_im = laplacian(chi_im)
    lap2_re = laplacian(lap_re.astype(bf16))
    lap2_im = laplacian(lap_im.astype(bf16))
    more_re = 2.0 * lap_re + (damping * lap2_re + turning * lap2_im)
    more_im = 2.0 * lap_im + (damping * lap2_im - turning * lap2_re)
    spread_re = chi_re.astype(f32) + (damping * more_re + turning * more_im)
    spread_im = chi_im.astype(f32) + (damping * more_im - turning * more_re)
    return spread_re, spread_im


def pass_group(down, across, chi_re, chi_im, count, window_of, keep):
    for layer in range(count - 1, -1, -1):
        spread_re, spread_im = back(down, across, chi_re, chi_im)
        keep(layer, spread_re, spread_im)
        win_re, win_im = window_of(layer)
        chi_re = (win_re * spread_re + win_im * spread_im).astype(bf16)
        chi_im = (win_re * spread_im - win_im * spread_re).astype(bf16)
    return chi_re, chi_im


def in_pieces(count, window):
    rows = window // chunk_count
    near = [(apart, slice(0, window)) for apart in distances(count)[:-far]]
    cut = [(count - far + i, slice(c * rows, (c + 1) * rows)) for c in range(chunk_count) for i in range(far)]
    return list(zip(*near, *cut))


def decoded(held_ref, layer):
    return [jnp.log(held_ref[layer, part].astype(f32)) * (1.0 / code_gain) for part in range(2)]


def first_kernel(start_ref, down_ref, across_ref, *refs):
    *win_refs, leave_ref, held_ref = refs
    count, _, window, _ = held_ref.shape
    own = place_in_group(count)
    for win_ref, apart, here in zip(win_refs, *in_pieces(count, window)):
        held_ref[own ^ apart, :, here] = win_ref[...]
    leave_ref[0], leave_ref[1] = pass_group(
        down_ref[...],
        across_ref[...],
        start_ref[0],
        start_ref[1],
        count,
        functools.partial(decoded, held_ref),
        lambda *_: None,
    )


def next_kernel(is_last, start_ref, come_ref, down_ref, across_ref, held_ref, *refs):
    count, _, window, _ = held_ref.shape
    own = place_in_group(count)
    behind = (lax.axis_index("sec") + count).astype(jnp.int32)
    at_end = jnp.full((window, window), behind, jnp.int32) >= lax.axis_size("sec")
    chi_re, chi_im = (
        jnp.where(at_end, start_ref[part].astype(f32), come_ref[part].astype(f32)).astype(bf16) for part in range(2)
    )

    def keep(layer, spread_re, spread_im):
        if is_last:
            refs[-1][layer, 0] = spread_re.astype(bf16)
            refs[-1][layer, 1] = spread_im.astype(bf16)

    chi = pass_group(
        down_ref[...], across_ref[...], chi_re, chi_im, count, functools.partial(decoded, held_ref), keep
    )
    if not is_last:
        refs[0][0], refs[0][1] = chi
        return
    for spread_ref, apart in zip(refs, distances(count)):
        spread_ref[...] = refs[-1][own ^ apart]


def add_kernel(base, count, picks, begun, ends, corner_ref, wave_ref, *refs):
    spread_refs, refs = refs[: len(picks)], refs[len(picks) :]
    window = wave_ref.shape[-1]
    rows = window // chunk_count
    tall = 16
    own = place_in_group(count)

    def one(block, _):
        at = pl.multiple_of(block * tall, tall)
        rows_at = pl.ds(at, tall)
        here = pl.ds(base + at, tall)
        sums = [refs[0][i, rows_at, :] if begun else jnp.zeros((tall, window), f32) for i in range(8)]
        for apart, spread_ref in zip(picks, spread_refs):
            position = position_at(own ^ apart, count)
            slot = position if wave_ref.shape[0] == count else apart
            in_mine, in_left = first_masks(corner_ref, position, base + at, (tall, window))
            wave_re, wave_im = (wave_ref[slot, part, here, :].astype(f32) for part in range(2))
            spread_re, spread_im = (spread_ref[part, here, :].astype(f32) for part in range(2))
            parts = (
                wave_re * spread_re + wave_im * spread_im,
                wave_re * spread_im - wave_im * spread_re,
            )
            for part in range(2):
                own_part = jnp.where(in_mine, parts[part], 0.0)
                sums[4 * part] += parts[part]
                sums[4 * part + 1] += own_part
                sums[4 * part + 2] += jnp.where(in_left, parts[part], 0.0)
                sums[4 * part + 3] += jnp.where(in_left, own_part, 0.0)
        if not ends:
            for i in range(8):
                refs[-1][i, rows_at, :] = sums[i]
            return 0
        own_ref, away_ref = refs[-2:]
        left, right = pl.ds(0, window), pl.ds(window, window)
        for part in range(2):
            every, mine, at_left, mine_left = sums[4 * part : 4 * part + 4]
            own_ref[part, rows_at, left] = mine_left
            own_ref[part, rows_at, right] = mine - mine_left
            away_ref[part, rows_at, left] = (at_left - mine_left).astype(bf16)
            away_ref[part, rows_at, right] = ((every - mine) - (at_left - mine_left)).astype(bf16)
        return 0

    lax.fori_loop(0, rows // tall, one, 0)


def finish(chunk, own, come, far_come, shape, before):
    def kernel(own_ref, come_ref, far_ref, *refs):
        refs[-1][...] = own_ref[...] + (come_ref[...].astype(f32) + far_ref[...].astype(f32))

    vmem = pl.BlockSpec(memory_space=pltpu.VMEM)
    return pl.pallas_call(
        kernel,
        grid=(1,),
        in_specs=[vmem] * 3 + [pl.BlockSpec(memory_space=pl.ANY)] * len(before),
        out_specs=pl.BlockSpec(own.shape, lambda _: (0, chunk, 0)),
        out_shape=shape_of(shape, f32),
        input_output_aliases={3: 0} if before else {},
        compiler_params=pltpu.CompilerParams(vmem_limit_bytes=6 * 2**20),
    )(own, come, far_come, *before)


def shape_of(dims, dtype):
    return jax.ShapeDtypeStruct(dims, dtype)


def on_device(obj_amp, obj_phase, forward_waves, exit_adjoint, offsets):
    sections = lax.axis_size("sec")
    count, _, window, _ = exit_adjoint.shape
    _, half, width = obj_amp.shape
    group_count = sections // count
    chunks = range(chunk_count)
    rows = half // chunk_count
    piece = (2, rows, width)
    wave = (2, window, window)
    corners = offsets.T

    def to_other_half(value):
        return lax.ppermute(value, "scan", [(0, 1), (1, 0)])

    def to_distance(value, d):
        return lax.ppermute(value, "sec", [(s, s ^ d) for s in range(sections)])

    def exchange(near):
        return [to_distance(value, d) if d else value for d, value in zip(distances(count), near)]

    def exchange_far(values):
        return [to_distance(value, count - far + i) for i, value in enumerate(values)]

    mine, other, far_mine = [], [], []
    source = (obj_amp, obj_phase)
    for c in chunks:
        if c > 0:
            source, mine[-1] = lax.optimization_barrier((source, mine[-1]))
        mine.append(coded(*(array[0, c * rows : (c + 1) * rows] for array in source)))
        other.append(to_other_half(mine[-1]))
        far_mine.append(to_distance(mine[-1], count - far))
    ready = call(ready_kernel, [shape_of(wave, bf16)] + [shape_of((window, window), bf16)] * 2, prefetch=1)
    start, down, across = ready(corners, exit_adjoint)
    other[0], start, down, across = lax.optimization_barrier((other[0], start, down, across))
    near, distant = [], []
    for c in chunks:
        cut = call(
            functools.partial(cut_kernel, c * rows, count),
            [shape_of(wave, bf16)] * (count - far),
            prefetch=1,
            aliases={3 + i: i for i in range(len(near))},
        )
        near = cut(corners, mine[c], other[c], *near)
    far_mine[-1], near = lax.optimization_barrier((far_mine[-1], near))
    for c in chunks:
        cut_far = call(
            functools.partial(cut_far_kernel, c * rows, count), [shape_of((2, rows, window), bf16)] * far, prefetch=1
        )
        kept, given = cut_far(corners, far_mine[c], to_other_half(far_mine[c]))
        distant += [kept, to_distance(given, 1)]
    windows = exchange(near) + distant
    waves, given = call(
        turn_kernel, [shape_of(forward_waves.shape[1:], bf16), shape_of((far,) + wave, bf16)], prefetch=1
    )(corners, forward_waves[0])

    cost = (count * 16 * window**3, count * 2 * window**2)
    first = call(first_kernel, [shape_of(wave, bf16), shape_of((count,) + wave, bf16)], cost=cost, grant=12)
    start, waves, given = lax.optimization_barrier((start, waves, given))
    far_waves = to_distance(given, count - far)
    leave, held = first(start, down, across, *windows)
    for stage in range(1, group_count):
        come = lax.ppermute(
            leave, "sec", [(s, (s - count) ^ (count // 2)) for s in range(count, sections)]
        )
        come, waves, far_waves = lax.optimization_barrier((come, waves, far_waves))
        is_last = stage == group_count - 1
        through = call(
            functools.partial(next_kernel, is_last),
            [shape_of(wave, bf16)] * count if is_last else shape_of(wave, bf16),
            scratch=[pltpu.VMEM((count,) + wave, bf16)] if is_last else [],
            cost=cost,
            grant=12,
        )
        leave = through(start, come, down, across, held)

    def add(c, wave_set, picks, spreads, sums, ends):
        kernel = functools.partial(add_kernel, c * rows, count, picks, bool(sums), ends)
        given = [shape_of(piece, f32), shape_of(piece, bf16)] if ends else shape_of((8, rows, window), f32)
        return call(kernel, given, prefetch=1)(corners, wave_set, *spreads, *sums)

    far_kept, far_given = leave[count - far :]
    far_spreads = [far_kept, to_distance(far_given, 1)]
    came = exchange(leave[: count - far])
    half_sums = []
    for c in chunks:
        keep, away = add(c, far_waves, [0, 1], far_spreads, [], True)
        half_sums.append((keep + to_other_half(away).astype(f32)).astype(bf16))

    order = distances(count)
    cut_at = count // 2 - 1
    early = [add(c, waves, order[:cut_at], came[:cut_at], [], False) for c in chunks]
    result = []
    for c in chunks:
        half_sums[c], early[c] = lax.optimization_barrier((half_sums[c], early[c]))
        far_come = to_distance(half_sums[c], count - far)
        keep, away = add(c, waves, order[cut_at : count - far], came[cut_at:], [early[c]], True)
        result.append((keep, to_other_half(away), far_come))
    out = []
    for c in chunks:
        out = [finish(c, *result[c], (2, half, width), out)]
    return out[0][None]


def solution(mesh):
    in_specs = (
        P("sec", "scan", None),
        P("sec", "scan", None),
        P("sec", "scan", None, None, None),
        P("scan", None, None, None),
        P("scan", None),
    )
    out_specs = P("sec", None, "scan", None)
    return jax.shard_map(
        on_device, mesh=mesh, in_specs=in_specs, out_specs=out_specs, check_vma=False
    )
```

```python
import functools
import math

import jax
import jax.numpy as jnp
from jax import lax
from jax.experimental import pallas as pl
from jax.experimental.pallas import tpu as pltpu
from jax.sharding import PartitionSpec as P

SUBSTEPS = 2
damping = 0.0005
turning = 0.011
code_gain = 83.0
chunk_count = 2
far = 2
f32 = jnp.float32
bf16 = jnp.bfloat16


def call(kernel, out_shape, prefetch=0, scratch=(), cost=(0, 0), grant=6, aliases=None):
    flops, transcendentals = cost

    def run(*args):
        moved = sum(a.size * a.dtype.itemsize for a in jax.tree.leaves((args, out_shape)))
        vmem = pl.BlockSpec(memory_space=pltpu.VMEM)
        return pl.pallas_call(
            kernel,
            grid_spec=pltpu.PrefetchScalarGridSpec(
                num_scalar_prefetch=prefetch,
                grid=(1,),
                in_specs=[vmem] * (len(args) - prefetch),
                out_specs=jax.tree.map(lambda _: vmem, out_shape),
                scratch_shapes=list(scratch),
            ),
            out_shape=out_shape,
            input_output_aliases=aliases or {},
            cost_estimate=pl.CostEstimate(flops=flops, bytes_accessed=moved, transcendentals=transcendentals),
            compiler_params=pltpu.CompilerParams(vmem_limit_bytes=grant * 2**20),
        )(*args)

    return run


def place_in_group(count):
    return lax.rem(lax.axis_index("sec").astype(jnp.int32), count)


def position_at(place, count):
    hops = lax.axis_size("sec") // count - 1 - lax.axis_index("sec").astype(jnp.int32) // count
    return place ^ (count // 2 * lax.rem(hops, 2))


def coded(amp, phase):
    half = 0.5 * phase
    square = half * half
    sine = jnp.full_like(half, 1.0 / math.factorial(13))
    cosine = jnp.full_like(half, 1.0 / math.factorial(12))
    for power in (11, 9, 7, 5, 3, 1):
        sign = -1.0 if power % 4 == 3 else 1.0
        sine = sine * square + sign / math.factorial(power)
        cosine = cosine * square + sign / math.factorial(power - 1)
    sine = sine * half
    trans_re = amp * (1.0 - 2.0 * sine * sine)
    trans_im = amp * (2.0 * sine * cosine)
    return jnp.stack([jnp.exp(code_gain * trans_re).astype(bf16), jnp.exp(code_gain * trans_im).astype(bf16)])


def first_masks(corner_ref, position, base, shape):
    place = lax.axis_index("scan").astype(jnp.int32)
    row = lax.broadcasted_iota(jnp.int32, shape, 0) + base
    col = lax.broadcasted_iota(jnp.int32, shape, 1)
    at_first = (row >= corner_ref[0, position]).astype(jnp.int32)
    return at_first != place, col >= corner_ref[1, position]


def distances(count):
    return sorted(range(count), key=lambda d: (d >= count - far, d > 0, d == 1, d % 2, d))


def select_window(corner_ref, position, base, mine_ref, other_ref):
    _, rows, width = mine_ref.shape
    window = width // 2
    in_mine, in_left = first_masks(corner_ref, position, base, (rows, window))
    for part in range(2):
        left, right = (
            jnp.where(in_mine, mine_ref[part, :, cols].astype(f32), other_ref[part, :, cols].astype(f32))
            for cols in (slice(0, window), slice(window, 2 * window))
        )
        yield jnp.where(in_left, left, right).astype(bf16)


def cut_kernel(base, count, corner_ref, mine_ref, other_ref, *refs):
    own = place_in_group(count)
    here = pl.ds(base, mine_ref.shape[1])
    near = distances(count)[:-far]
    for i, (apart, win_ref) in enumerate(zip(near, refs[-len(near) :])):
        if base:
            win_ref[:, :base] = refs[i][:, :base]
        position = position_at(own ^ apart, count)
        for part, value in enumerate(select_window(corner_ref, position, base, mine_ref, other_ref)):
            win_ref[part, here, :] = value


def cut_far_kernel(base, count, corner_ref, mine_ref, other_ref, *win_refs):
    own = place_in_group(count)
    for apart, win_ref in enumerate(win_refs):
        position = position_at(own ^ apart, count)
        for part, value in enumerate(select_window(corner_ref, position, base, mine_ref, other_ref)):
            win_ref[part] = value


def turned(wave, row_at, col_at):
    window = wave.shape[-1]
    wave = pltpu.roll(wave.astype(f32), lax.rem(row_at, window), 0)
    return pltpu.roll(wave, lax.rem(col_at, window), 1).astype(bf16)


def second_difference(size, break_at):
    row = lax.broadcasted_iota(jnp.int32, (size, size), 0)
    col = lax.broadcasted_iota(jnp.int32, (size, size), 1)
    start = lax.rem(break_at, size)
    before = (lax.rem(row - col + size, size) == 1) & (row != start)
    after = (lax.rem(col - row + size, size) == 1) & (col != start)
    return jnp.where(row == col, -2.0, jnp.where(before | after, 1.0, 0.0)).astype(bf16)


def ready_kernel(corner_ref, exit_ref, start_ref, down_ref, across_ref):
    count = exit_ref.shape[0]
    own = position_at(place_in_group(count), count)
    row_at = corner_ref[0, own]
    col_at = corner_ref[1, own]
    size = start_ref.shape[-1]
    for part in range(2):
        start_ref[part] = turned(exit_ref[own, part], row_at, col_at)
    down_ref[...] = second_difference(size, row_at)
    across_ref[...] = second_difference(size, col_at)


def turn_kernel(corner_ref, wave_ref, turned_ref, given_ref):
    count = wave_ref.shape[0]

    def one(position, _):
        for part in range(2):
            turned_ref[position, part] = turned(
                wave_ref[position, part], corner_ref[0, position], corner_ref[1, position]
            )
        return 0

    lax.fori_loop(0, count, one, 0)
    own = place_in_group(count)
    for i in range(far):
        given_ref[i] = turned_ref[position_at(own ^ (count - far + i), count)]


def back(down, across, chi_re, chi_im):
    def laplacian(field):
        rows = jnp.dot(down, field, preferred_element_type=f32)
        return rows + jnp.dot(field, across, preferred_element_type=f32)

    lap_re = laplacian(chi_re)
    lap_im = laplacian(chi_im)
    lap2_re = laplacian(lap_re.astype(bf16))
    lap2_im = laplacian(lap_im.astype(bf16))
    more_re = 2.0 * lap_re + (damping * lap2_re + turning * lap2_im)
    more_im = 2.0 * lap_im + (damping * lap2_im - turning * lap2_re)
    spread_re = chi_re.astype(f32) + (damping * more_re + turning * more_im)
    spread_im = chi_im.astype(f32) + (damping * more_im - turning * more_re)
    return spread_re, spread_im


def pass_group(down, across, chi_re, chi_im, count, window_of, keep):
    for layer in range(count - 1, -1, -1):
        spread_re, spread_im = back(down, across, chi_re, chi_im)
        keep(layer, spread_re, spread_im)
        win_re, win_im = window_of(layer)
        chi_re = (win_re * spread_re + win_im * spread_im).astype(bf16)
        chi_im = (win_re * spread_im - win_im * spread_re).astype(bf16)
    return chi_re, chi_im


def in_pieces(count, window):
    rows = window // chunk_count
    near = [(apart, slice(0, window)) for apart in distances(count)[:-far]]
    cut = [(count - far + i, slice(c * rows, (c + 1) * rows)) for c in range(chunk_count) for i in range(far)]
    return list(zip(*near, *cut))


def decoded(held_ref, layer):
    return [jnp.log(held_ref[layer, part].astype(f32)) * (1.0 / code_gain) for part in range(2)]


def first_kernel(start_ref, down_ref, across_ref, *refs):
    *win_refs, leave_ref, held_ref = refs
    count, _, window, _ = held_ref.shape
    own = place_in_group(count)
    for win_ref, apart, here in zip(win_refs, *in_pieces(count, window)):
        held_ref[own ^ apart, :, here] = win_ref[...]
    leave_ref[0], leave_ref[1] = pass_group(
        down_ref[...],
        across_ref[...],
        start_ref[0],
        start_ref[1],
        count,
        functools.partial(decoded, held_ref),
        lambda *_: None,
    )


def next_kernel(is_last, start_ref, come_ref, down_ref, across_ref, held_ref, *refs):
    count, _, window, _ = held_ref.shape
    own = place_in_group(count)
    behind = (lax.axis_index("sec") + count).astype(jnp.int32)
    at_end = jnp.full((window, window), behind, jnp.int32) >= lax.axis_size("sec")
    chi_re, chi_im = (
        jnp.where(at_end, start_ref[part].astype(f32), come_ref[part].astype(f32)).astype(bf16) for part in range(2)
    )

    def keep(layer, spread_re, spread_im):
        if is_last:
            refs[-1][layer, 0] = spread_re.astype(bf16)
            refs[-1][layer, 1] = spread_im.astype(bf16)

    chi = pass_group(
        down_ref[...], across_ref[...], chi_re, chi_im, count, functools.partial(decoded, held_ref), keep
    )
    if not is_last:
        refs[0][0], refs[0][1] = chi
        return
    for spread_ref, apart in zip(refs, distances(count)):
        spread_ref[...] = refs[-1][own ^ apart]


def add_kernel(base, count, picks, begun, ends, corner_ref, *refs):
    more = 1 if refs[0].shape[0] == count else 2
    wave_refs, refs = refs[:more], refs[more:]
    wave_ref = wave_refs[0]
    spread_refs, refs = refs[: len(picks)], refs[len(picks) :]
    window = wave_ref.shape[-1]
    rows = window // chunk_count
    tall = 16
    own = place_in_group(count)

    def one(block, _):
        at = pl.multiple_of(block * tall, tall)
        rows_at = pl.ds(at, tall)
        here = pl.ds(base + at, tall)
        sums = [refs[0][i, rows_at, :] if begun else jnp.zeros((tall, window), f32) for i in range(8)]
        for apart, spread_ref in zip(picks, spread_refs):
            position = position_at(own ^ apart, count)
            slot = position if more == 1 else apart
            in_mine, in_left = first_masks(corner_ref, position, base + at, (tall, window))
            wave_re, wave_im = (wave_ref[slot, part, here, :].astype(f32) for part in range(2))
            if more == 2:
                in_last = jnp.full((tall, window), lax.axis_index("sec").astype(jnp.int32), jnp.int32) < count
                wave_re = jnp.where(in_last, wave_re, wave_refs[1][slot, 0, here, :].astype(f32))
                wave_im = jnp.where(in_last, wave_im, wave_refs[1][slot, 1, here, :].astype(f32))
            spread_re, spread_im = (spread_ref[part, here, :].astype(f32) for part in range(2))
            parts = (
                wave_re * spread_re + wave_im * spread_im,
                wave_re * spread_im - wave_im * spread_re,
            )
            for part in range(2):
                own_part = jnp.where(in_mine, parts[part], 0.0)
                sums[4 * part] += parts[part]
                sums[4 * part + 1] += own_part
                sums[4 * part + 2] += jnp.where(in_left, parts[part], 0.0)
                sums[4 * part + 3] += jnp.where(in_left, own_part, 0.0)
        if not ends:
            for i in range(8):
                refs[-1][i, rows_at, :] = sums[i]
            return 0
        own_ref, away_ref = refs[-2:]
        left, right = pl.ds(0, window), pl.ds(window, window)
        for part in range(2):
            every, mine, at_left, mine_left = sums[4 * part : 4 * part + 4]
            own_ref[part, rows_at, left] = mine_left
            own_ref[part, rows_at, right] = mine - mine_left
            away_ref[part, rows_at, left] = (at_left - mine_left).astype(bf16)
            away_ref[part, rows_at, right] = ((every - mine) - (at_left - mine_left)).astype(bf16)
        return 0

    lax.fori_loop(0, rows // tall, one, 0)


def finish(chunk, own, come, far_come, shape, before):
    def kernel(own_ref, come_ref, far_ref, *refs):
        refs[-1][...] = own_ref[...] + (come_ref[...].astype(f32) + far_ref[...].astype(f32))

    vmem = pl.BlockSpec(memory_space=pltpu.VMEM)
    return pl.pallas_call(
        kernel,
        grid=(1,),
        in_specs=[vmem] * 3 + [pl.BlockSpec(memory_space=pl.ANY)] * len(before),
        out_specs=pl.BlockSpec(own.shape, lambda _: (0, chunk, 0)),
        out_shape=shape_of(shape, f32),
        input_output_aliases={3: 0} if before else {},
        compiler_params=pltpu.CompilerParams(vmem_limit_bytes=6 * 2**20),
    )(own, come, far_come, *before)


def shape_of(dims, dtype):
    return jax.ShapeDtypeStruct(dims, dtype)


def on_device(obj_amp, obj_phase, forward_waves, exit_adjoint, offsets):
    sections = lax.axis_size("sec")
    count, _, window, _ = exit_adjoint.shape
    _, half, width = obj_amp.shape
    group_count = sections // count
    chunks = range(chunk_count)
    rows = half // chunk_count
    piece = (2, rows, width)
    wave = (2, window, window)
    corners = offsets.T

    def far_permute(value, in_last):
        return lax.ppermute(
            value, "sec", [(s, s ^ (count - far) if (s < count) == in_last else s) for s in range(sections)]
        )

    def to_other_half(value):
        return lax.ppermute(value, "scan", [(0, 1), (1, 0)])

    def to_distance(value, d):
        return lax.ppermute(value, "sec", [(s, s ^ d) for s in range(sections)])

    def exchange(near):
        return [to_distance(value, d) if d else value for d, value in zip(distances(count), near)]

    def exchange_far(values):
        return [to_distance(value, count - far + i) for i, value in enumerate(values)]

    mine, other, far_mine = [], [], []
    source = (obj_amp, obj_phase)
    for c in chunks:
        if c > 0:
            source, mine[-1] = lax.optimization_barrier((source, mine[-1]))
        mine.append(coded(*(array[0, c * rows : (c + 1) * rows] for array in source)))
        other.append(to_other_half(mine[-1]))
        far_mine.append(to_distance(mine[-1], count - far))
    ready = call(ready_kernel, [shape_of(wave, bf16)] + [shape_of((window, window), bf16)] * 2, prefetch=1)
    start, down, across = ready(corners, exit_adjoint)
    other[0], start, down, across = lax.optimization_barrier((other[0], start, down, across))
    near, distant = [], []
    for c in chunks:
        cut = call(
            functools.partial(cut_kernel, c * rows, count),
            [shape_of(wave, bf16)] * (count - far),
            prefetch=1,
            aliases={3 + i: i for i in range(len(near))},
        )
        near = cut(corners, mine[c], other[c], *near)
    far_mine[-1], near = lax.optimization_barrier((far_mine[-1], near))
    for c in chunks:
        cut_far = call(
            functools.partial(cut_far_kernel, c * rows, count), [shape_of((2, rows, window), bf16)] * far, prefetch=1
        )
        kept, given = cut_far(corners, far_mine[c], to_other_half(far_mine[c]))
        distant += [kept, to_distance(given, 1)]
    windows = exchange(near) + distant
    waves, given = call(
        turn_kernel, [shape_of(forward_waves.shape[1:], bf16), shape_of((far,) + wave, bf16)], prefetch=1
    )(corners, forward_waves[0])

    cost = (count * 16 * window**3, count * 2 * window**2)
    first = call(first_kernel, [shape_of(wave, bf16), shape_of((count,) + wave, bf16)], cost=cost, grant=12)
    start, waves, given = lax.optimization_barrier((start, waves, given))
    far_waves = [far_permute(given, True)]
    leave, held = first(start, down, across, *windows)
    for stage in range(1, group_count):
        come = lax.ppermute(
            leave, "sec", [(s, (s - count) ^ (count // 2)) for s in range(count, sections)]
        )
        come, waves, far_waves, given = lax.optimization_barrier((come, waves, far_waves, given))
        is_last = stage == group_count - 1
        through = call(
            functools.partial(next_kernel, is_last),
            [shape_of(wave, bf16)] * count if is_last else shape_of(wave, bf16),
            scratch=[pltpu.VMEM((count,) + wave, bf16)] if is_last else [],
            cost=cost,
            grant=12,
        )
        leave = through(start, come, down, across, held)

    def add(c, wave_set, picks, spreads, sums, ends):
        kernel = functools.partial(add_kernel, c * rows, count, picks, bool(sums), ends)
        given = [shape_of(piece, f32), shape_of(piece, bf16)] if ends else shape_of((8, rows, window), f32)
        return call(kernel, given, prefetch=1)(corners, *wave_set, *spreads, *sums)

    far_waves.append(far_permute(given, False))
    far_kept, far_given = leave[count - far :]
    far_spreads = [far_kept, to_distance(far_given, 1)]
    came = exchange(leave[: count - far])
    half_sums = []
    for c in chunks:
        keep, away = add(c, far_waves, [0, 1], far_spreads, [], True)
        half_sums.append((keep + to_other_half(away).astype(f32)).astype(bf16))

    order = distances(count)
    cut_at = count // 2 - 1
    early = [add(c, [waves], order[:cut_at], came[:cut_at], [], False) for c in chunks]
    result = []
    for c in chunks:
        half_sums[c], early[c] = lax.optimization_barrier((half_sums[c], early[c]))
        far_come = to_distance(half_sums[c], count - far)
        keep, away = add(c, [waves], order[cut_at : count - far], came[cut_at:], [early[c]], True)
        result.append((keep, to_other_half(away), far_come))
    out = []
    for c in chunks:
        out = [finish(c, *result[c], (2, half, width), out)]
    return out[0][None]


def solution(mesh):
    in_specs = (
        P("sec", "scan", None),
        P("sec", "scan", None),
        P("sec", "scan", None, None, None),
        P("scan", None, None, None),
        P("scan", None),
    )
    out_specs = P("sec", None, "scan", None)
    return jax.shard_map(
        on_device, mesh=mesh, in_specs=in_specs, out_specs=out_specs, check_vma=False
    )
```

```python
import functools
import math

import jax
import jax.numpy as jnp
from jax import lax
from jax.experimental import pallas as pl
from jax.experimental.pallas import tpu as pltpu
from jax.sharding import PartitionSpec as P

SUBSTEPS = 2
damping = 0.0005
turning = 0.011
code_gain = 83.0
chunk_count = 2
far = 2
f32 = jnp.float32
bf16 = jnp.bfloat16


def call(kernel, out_shape, prefetch=0, scratch=(), cost=(0, 0), grant=6, aliases=None):
    flops, transcendentals = cost

    def run(*args):
        moved = sum(a.size * a.dtype.itemsize for a in jax.tree.leaves((args, out_shape)))
        vmem = pl.BlockSpec(memory_space=pltpu.VMEM)
        return pl.pallas_call(
            kernel,
            grid_spec=pltpu.PrefetchScalarGridSpec(
                num_scalar_prefetch=prefetch,
                grid=(1,),
                in_specs=[vmem] * (len(args) - prefetch),
                out_specs=jax.tree.map(lambda _: vmem, out_shape),
                scratch_shapes=list(scratch),
            ),
            out_shape=out_shape,
            input_output_aliases=aliases or {},
            cost_estimate=pl.CostEstimate(flops=flops, bytes_accessed=moved, transcendentals=transcendentals),
            compiler_params=pltpu.CompilerParams(vmem_limit_bytes=grant * 2**20),
        )(*args)

    return run


def place_in_group(count):
    return lax.rem(lax.axis_index("sec").astype(jnp.int32), count)


def position_at(place, count):
    hops = lax.axis_size("sec") // count - 1 - lax.axis_index("sec").astype(jnp.int32) // count
    return place ^ (count // 2 * lax.rem(hops, 2))


def coded(amp, phase):
    half = 0.5 * phase
    square = half * half
    sine = jnp.full_like(half, 1.0 / math.factorial(13))
    cosine = jnp.full_like(half, 1.0 / math.factorial(12))
    for power in (11, 9, 7, 5, 3, 1):
        sign = -1.0 if power % 4 == 3 else 1.0
        sine = sine * square + sign / math.factorial(power)
        cosine = cosine * square + sign / math.factorial(power - 1)
    sine = sine * half
    trans_re = amp * (1.0 - 2.0 * sine * sine)
    trans_im = amp * (2.0 * sine * cosine)
    return jnp.stack([jnp.exp(code_gain * trans_re).astype(bf16), jnp.exp(code_gain * trans_im).astype(bf16)])


def first_masks(corner_ref, position, base, shape):
    place = lax.axis_index("scan").astype(jnp.int32)
    row = lax.broadcasted_iota(jnp.int32, shape, 0) + base
    col = lax.broadcasted_iota(jnp.int32, shape, 1)
    at_first = (row >= corner_ref[0, position]).astype(jnp.int32)
    return at_first != place, col >= corner_ref[1, position]


def distances(count):
    return sorted(range(count), key=lambda d: (d >= count - far, d > 0, d == 1, d % 2, d))


def select_window(corner_ref, position, base, mine_ref, other_ref):
    _, rows, width = mine_ref.shape
    window = width // 2
    in_mine, in_left = first_masks(corner_ref, position, base, (rows, window))
    for part in range(2):
        left, right = (
            jnp.where(in_mine, mine_ref[part, :, cols].astype(f32), other_ref[part, :, cols].astype(f32))
            for cols in (slice(0, window), slice(window, 2 * window))
        )
        yield jnp.where(in_left, left, right).astype(bf16)


def cut_kernel(base, count, corner_ref, mine_ref, other_ref, *refs):
    own = place_in_group(count)
    here = pl.ds(base, mine_ref.shape[1])
    near = distances(count)[:-far]
    for i, (apart, win_ref) in enumerate(zip(near, refs[-len(near) :])):
        if base:
            win_ref[:, :base] = refs[i][:, :base]
        position = position_at(own ^ apart, count)
        for part, value in enumerate(select_window(corner_ref, position, base, mine_ref, other_ref)):
            win_ref[part, here, :] = value


def cut_far_kernel(base, count, corner_ref, mine_ref, other_ref, *win_refs):
    own = place_in_group(count)
    for apart, win_ref in enumerate(win_refs):
        position = position_at(own ^ apart, count)
        for part, value in enumerate(select_window(corner_ref, position, base, mine_ref, other_ref)):
            win_ref[part] = value


def turned(wave, row_at, col_at):
    window = wave.shape[-1]
    wave = pltpu.roll(wave.astype(f32), lax.rem(row_at, window), 0)
    return pltpu.roll(wave, lax.rem(col_at, window), 1).astype(bf16)


def second_difference(size, break_at):
    row = lax.broadcasted_iota(jnp.int32, (size, size), 0)
    col = lax.broadcasted_iota(jnp.int32, (size, size), 1)
    start = lax.rem(break_at, size)
    before = (lax.rem(row - col + size, size) == 1) & (row != start)
    after = (lax.rem(col - row + size, size) == 1) & (col != start)
    return jnp.where(row == col, -2.0, jnp.where(before | after, 1.0, 0.0)).astype(bf16)


def ready_kernel(corner_ref, exit_ref, start_ref, down_ref, across_ref):
    count = exit_ref.shape[0]
    own = position_at(place_in_group(count), count)
    row_at = corner_ref[0, own]
    col_at = corner_ref[1, own]
    size = start_ref.shape[-1]
    for part in range(2):
        start_ref[part] = turned(exit_ref[own, part], row_at, col_at)
    down_ref[...] = second_difference(size, row_at)
    across_ref[...] = second_difference(size, col_at)


def turn_kernel(corner_ref, wave_ref, turned_ref):
    count = wave_ref.shape[0]

    def one(position, _):
        for part in range(2):
            turned_ref[position, part] = turned(
                wave_ref[position, part], corner_ref[0, position], corner_ref[1, position]
            )
        return 0

    lax.fori_loop(0, count, one, 0)


def back(down, across, chi_re, chi_im):
    def laplacian(field):
        rows = jnp.dot(down, field, preferred_element_type=f32)
        return rows + jnp.dot(field, across, preferred_element_type=f32)

    lap_re = laplacian(chi_re)
    lap_im = laplacian(chi_im)
    lap2_re = laplacian(lap_re.astype(bf16))
    lap2_im = laplacian(lap_im.astype(bf16))
    more_re = 2.0 * lap_re + (damping * lap2_re + turning * lap2_im)
    more_im = 2.0 * lap_im + (damping * lap2_im - turning * lap2_re)
    spread_re = chi_re.astype(f32) + (damping * more_re + turning * more_im)
    spread_im = chi_im.astype(f32) + (damping * more_im - turning * more_re)
    return spread_re, spread_im


def pass_group(down, across, chi_re, chi_im, count, window_of, keep):
    for layer in range(count - 1, -1, -1):
        spread_re, spread_im = back(down, across, chi_re, chi_im)
        keep(layer, spread_re, spread_im)
        win_re, win_im = window_of(layer)
        chi_re = (win_re * spread_re + win_im * spread_im).astype(bf16)
        chi_im = (win_re * spread_im - win_im * spread_re).astype(bf16)
    return chi_re, chi_im


def in_pieces(count, window):
    rows = window // chunk_count
    near = [(apart, slice(0, window)) for apart in distances(count)[:-far]]
    cut = [(count - far + i, slice(c * rows, (c + 1) * rows)) for c in range(chunk_count) for i in range(far)]
    return list(zip(*near, *cut))


def decoded(held_ref, layer):
    return [jnp.log(held_ref[layer, part].astype(f32)) * (1.0 / code_gain) for part in range(2)]


def first_kernel(start_ref, down_ref, across_ref, *refs):
    *win_refs, leave_ref, held_ref = refs
    count, _, window, _ = held_ref.shape
    own = place_in_group(count)
    for win_ref, apart, here in zip(win_refs, *in_pieces(count, window)):
        held_ref[own ^ apart, :, here] = win_ref[...]
    leave_ref[0], leave_ref[1] = pass_group(
        down_ref[...],
        across_ref[...],
        start_ref[0],
        start_ref[1],
        count,
        functools.partial(decoded, held_ref),
        lambda *_: None,
    )


def next_kernel(is_last, start_ref, come_ref, down_ref, across_ref, held_ref, *refs):
    count, _, window, _ = held_ref.shape
    own = place_in_group(count)
    behind = (lax.axis_index("sec") + count).astype(jnp.int32)
    at_end = jnp.full((window, window), behind, jnp.int32) >= lax.axis_size("sec")
    chi_re, chi_im = (
        jnp.where(at_end, start_ref[part].astype(f32), come_ref[part].astype(f32)).astype(bf16) for part in range(2)
    )

    def keep(layer, spread_re, spread_im):
        if is_last:
            refs[-1][layer, 0] = spread_re.astype(bf16)
            refs[-1][layer, 1] = spread_im.astype(bf16)

    chi = pass_group(
        down_ref[...], across_ref[...], chi_re, chi_im, count, functools.partial(decoded, held_ref), keep
    )
    if not is_last:
        refs[0][0], refs[0][1] = chi
        return
    for spread_ref, apart, here in zip(refs, *in_pieces(count, window)):
        spread_ref[...] = refs[-1][own ^ apart, :, here]


def add_kernel(base, picks, begun, ends, corner_ref, wave_ref, *refs):
    spread_refs, refs = refs[: len(picks)], refs[len(picks) :]
    count, _, window, _ = wave_ref.shape
    rows = window // chunk_count
    tall = 16
    own = place_in_group(count)

    def one(block, _):
        at = pl.multiple_of(block * tall, tall)
        rows_at = pl.ds(at, tall)
        here = pl.ds(base + at, tall)
        sums = [refs[0][i, rows_at, :] if begun else jnp.zeros((tall, window), f32) for i in range(8)]
        for apart, spread_ref in zip(picks, spread_refs):
            position = position_at(own ^ apart, count)
            there = rows_at if apart >= count - far else here
            in_mine, in_left = first_masks(corner_ref, position, base + at, (tall, window))
            wave_re, wave_im = (wave_ref[position, part, here, :].astype(f32) for part in range(2))
            spread_re, spread_im = (spread_ref[part, there, :].astype(f32) for part in range(2))
            parts = (
                wave_re * spread_re + wave_im * spread_im,
                wave_re * spread_im - wave_im * spread_re,
            )
            for part in range(2):
                own_part = jnp.where(in_mine, parts[part], 0.0)
                sums[4 * part] += parts[part]
                sums[4 * part + 1] += own_part
                sums[4 * part + 2] += jnp.where(in_left, parts[part], 0.0)
                sums[4 * part + 3] += jnp.where(in_left, own_part, 0.0)
        if not ends:
            for i in range(8):
                refs[-1][i, rows_at, :] = sums[i]
            return 0
        own_ref, away_ref = refs[-2:]
        left, right = pl.ds(0, window), pl.ds(window, window)
        for part in range(2):
            every, mine, at_left, mine_left = sums[4 * part : 4 * part + 4]
            own_ref[part, rows_at, left] = mine_left
            own_ref[part, rows_at, right] = mine - mine_left
            away_ref[part, rows_at, left] = (at_left - mine_left).astype(bf16)
            away_ref[part, rows_at, right] = ((every - mine) - (at_left - mine_left)).astype(bf16)
        return 0

    lax.fori_loop(0, rows // tall, one, 0)


def finish(chunk, own, come, shape, before):
    def kernel(own_ref, come_ref, *refs):
        refs[-1][...] = own_ref[...] + come_ref[...].astype(f32)

    vmem = pl.BlockSpec(memory_space=pltpu.VMEM)
    return pl.pallas_call(
        kernel,
        grid=(1,),
        in_specs=[vmem, vmem] + [pl.BlockSpec(memory_space=pl.ANY)] * len(before),
        out_specs=pl.BlockSpec(own.shape, lambda _: (0, chunk, 0)),
        out_shape=shape_of(shape, f32),
        input_output_aliases={2: 0} if before else {},
        compiler_params=pltpu.CompilerParams(vmem_limit_bytes=6 * 2**20),
    )(own, come, *before)


def shape_of(dims, dtype):
    return jax.ShapeDtypeStruct(dims, dtype)


def on_device(obj_amp, obj_phase, forward_waves, exit_adjoint, offsets):
    sections = lax.axis_size("sec")
    count, _, window, _ = exit_adjoint.shape
    _, half, width = obj_amp.shape
    group_count = sections // count
    chunks = range(chunk_count)
    rows = half // chunk_count
    piece = (2, rows, width)
    wave = (2, window, window)
    corners = offsets.T

    def to_other_half(value):
        return lax.ppermute(value, "scan", [(0, 1), (1, 0)])

    def to_distance(value, d):
        return lax.ppermute(value, "sec", [(s, s ^ d) for s in range(sections)])

    def exchange(near):
        return [to_distance(value, d) if d else value for d, value in zip(distances(count), near)]

    def exchange_far(values):
        return [to_distance(value, count - far + i) for i, value in enumerate(values)]

    mine, other = [], []
    source = (obj_amp, obj_phase)
    for c in chunks:
        if c > 0:
            source, mine[-1] = lax.optimization_barrier((source, mine[-1]))
        mine.append(coded(*(array[0, c * rows : (c + 1) * rows] for array in source)))
        other.append(to_other_half(mine[-1]))
    mine = list(lax.optimization_barrier(mine))
    far_mine = [to_distance(value, count - far) for value in mine]
    ready = call(ready_kernel, [shape_of(wave, bf16)] + [shape_of((window, window), bf16)] * 2, prefetch=1)
    start, down, across = ready(corners, exit_adjoint)
    other[0], start, down, across = lax.optimization_barrier((other[0], start, down, across))
    near, distant = [], []
    for c in chunks:
        cut = call(
            functools.partial(cut_kernel, c * rows, count),
            [shape_of(wave, bf16)] * (count - far),
            prefetch=1,
            aliases={3 + i: i for i in range(len(near))},
        )
        near = cut(corners, mine[c], other[c], *near)
    far_mine[-1], near = lax.optimization_barrier((far_mine[-1], near))
    for c in chunks:
        cut_far = call(
            functools.partial(cut_far_kernel, c * rows, count), [shape_of((2, rows, window), bf16)] * far, prefetch=1
        )
        kept, given = cut_far(corners, far_mine[c], to_other_half(far_mine[c]))
        distant += [kept, to_distance(given, 1)]
    windows = exchange(near) + distant
    waves = call(turn_kernel, shape_of(forward_waves.shape[1:], bf16), prefetch=1)(corners, forward_waves[0])

    pieces = [shape_of(wave, bf16)] * (count - far) + [shape_of((2, rows, window), bf16)] * (far * chunk_count)
    cost = (count * 16 * window**3, count * 2 * window**2)
    first = call(first_kernel, [shape_of(wave, bf16), shape_of((count,) + wave, bf16)], cost=cost, grant=12)
    leave, held = first(start, down, across, *windows)
    for stage in range(1, group_count):
        come = lax.ppermute(
            leave, "sec", [(s, (s - count) ^ (count // 2)) for s in range(count, sections)]
        )
        come, waves = lax.optimization_barrier((come, waves))
        is_last = stage == group_count - 1
        through = call(
            functools.partial(next_kernel, is_last),
            pieces if is_last else shape_of(wave, bf16),
            scratch=[pltpu.VMEM((count,) + wave, bf16)] if is_last else [],
            cost=cost,
            grant=12,
        )
        leave = through(start, come, down, across, held)

    near, distant = leave[: count - far], leave[count - far :]
    came_far = [exchange_far(distant[:far])]
    came = exchange(near)
    came_far += [exchange_far(distant[c * far : (c + 1) * far]) for c in chunks[1:]]
    order = distances(count)
    early, late = order[: count // 2 - 1], order[count // 2 - 1 : count - far]
    spread_at = dict(zip(order, came))

    def add(c, picks, sums, ends):
        spreads = [came_far[c][d - count + far] if d >= count - far else spread_at[d] for d in picks]
        kernel = functools.partial(add_kernel, c * rows, picks, bool(sums), ends)
        given = [shape_of(piece, f32), shape_of(piece, bf16)] if ends else shape_of((8, rows, window), f32)
        return call(kernel, given, prefetch=1)(corners, waves, *spreads, *sums)

    done = []
    for c in chunks:
        if c == 0:
            sums = add(c, early + order[-far:], [], False)
            keep, away = add(c, late, [sums], True)
        else:
            sums = add(c, early, [], False)
            sums, away = lax.optimization_barrier((sums, away))
            sums = add(c, late, [sums], False)
            done.append((keep, to_other_half(away)))
            keep, away = add(c, order[-far:], [sums], True)
    done.append((keep, to_other_half(away)))
    result = []
    for c in chunks:
        result = [finish(c, *done[c], (2, half, width), result)]
    return result[0][None]


def solution(mesh):
    in_specs = (
        P("sec", "scan", None),
        P("sec", "scan", None),
        P("sec", "scan", None, None, None),
        P("scan", None, None, None),
        P("scan", None),
    )
    out_specs = P("sec", None, "scan", None)
    return jax.shard_map(
        on_device, mesh=mesh, in_specs=in_specs, out_specs=out_specs, check_vma=False
    )
```

```python
import functools
import math

import jax
import jax.numpy as jnp
from jax import lax
from jax.experimental import pallas as pl
from jax.experimental.pallas import tpu as pltpu
from jax.sharding import PartitionSpec as P

SUBSTEPS = 2
damping = 0.0005
turning = 0.011
code_gain = 83.0
chunk_count = 2
far = 2
f32 = jnp.float32
bf16 = jnp.bfloat16


def call(kernel, out_shape, prefetch=0, scratch=(), cost=(0, 0), grant=6, aliases=None):
    flops, transcendentals = cost

    def run(*args):
        moved = sum(a.size * a.dtype.itemsize for a in jax.tree.leaves((args, out_shape)))
        vmem = pl.BlockSpec(memory_space=pltpu.VMEM)
        return pl.pallas_call(
            kernel,
            grid_spec=pltpu.PrefetchScalarGridSpec(
                num_scalar_prefetch=prefetch,
                grid=(1,),
                in_specs=[vmem] * (len(args) - prefetch),
                out_specs=jax.tree.map(lambda _: vmem, out_shape),
                scratch_shapes=list(scratch),
            ),
            out_shape=out_shape,
            input_output_aliases=aliases or {},
            cost_estimate=pl.CostEstimate(flops=flops, bytes_accessed=moved, transcendentals=transcendentals),
            compiler_params=pltpu.CompilerParams(vmem_limit_bytes=grant * 2**20),
        )(*args)

    return run


def place_in_group(count):
    return lax.rem(lax.axis_index("sec").astype(jnp.int32), count)


def position_at(place, count):
    hops = lax.axis_size("sec") // count - 1 - lax.axis_index("sec").astype(jnp.int32) // count
    return place ^ (count // 2 * lax.rem(hops, 2))


def coded(amp, phase):
    half = 0.5 * phase
    square = half * half
    sine = jnp.full_like(half, 1.0 / math.factorial(13))
    cosine = jnp.full_like(half, 1.0 / math.factorial(12))
    for power in (11, 9, 7, 5, 3, 1):
        sign = -1.0 if power % 4 == 3 else 1.0
        sine = sine * square + sign / math.factorial(power)
        cosine = cosine * square + sign / math.factorial(power - 1)
    sine = sine * half
    trans_re = amp * (1.0 - 2.0 * sine * sine)
    trans_im = amp * (2.0 * sine * cosine)
    return jnp.stack([jnp.exp(code_gain * trans_re).astype(bf16), jnp.exp(code_gain * trans_im).astype(bf16)])


def first_masks(corner_ref, position, base, shape):
    place = lax.axis_index("scan").astype(jnp.int32)
    row = lax.broadcasted_iota(jnp.int32, shape, 0) + base
    col = lax.broadcasted_iota(jnp.int32, shape, 1)
    at_first = (row >= corner_ref[0, position]).astype(jnp.int32)
    return at_first != place, col >= corner_ref[1, position]


def distances(count):
    return sorted(range(count), key=lambda d: (d >= count - far, d > 0, d == 1, d % 2, d))


def select_window(corner_ref, position, base, mine_ref, other_ref):
    _, rows, width = mine_ref.shape
    window = width // 2
    in_mine, in_left = first_masks(corner_ref, position, base, (rows, window))
    for part in range(2):
        left, right = (
            jnp.where(in_mine, mine_ref[part, :, cols].astype(f32), other_ref[part, :, cols].astype(f32))
            for cols in (slice(0, window), slice(window, 2 * window))
        )
        yield jnp.where(in_left, left, right).astype(bf16)


def cut_kernel(base, count, corner_ref, mine_ref, other_ref, *refs):
    own = place_in_group(count)
    here = pl.ds(base, mine_ref.shape[1])
    near = distances(count)[:-far]
    for i, (apart, win_ref) in enumerate(zip(near, refs[-len(near) :])):
        if base:
            win_ref[:, :base] = refs[i][:, :base]
        position = position_at(own ^ apart, count)
        for part, value in enumerate(select_window(corner_ref, position, base, mine_ref, other_ref)):
            win_ref[part, here, :] = value


def cut_far_kernel(base, count, corner_ref, mine_ref, other_ref, *win_refs):
    own = place_in_group(count)
    for apart, win_ref in enumerate(win_refs):
        position = position_at(own ^ apart, count)
        for part, value in enumerate(select_window(corner_ref, position, base, mine_ref, other_ref)):
            win_ref[part] = value


def turned(wave, row_at, col_at):
    window = wave.shape[-1]
    wave = pltpu.roll(wave.astype(f32), lax.rem(row_at, window), 0)
    return pltpu.roll(wave, lax.rem(col_at, window), 1).astype(bf16)


def second_difference(size, break_at):
    row = lax.broadcasted_iota(jnp.int32, (size, size), 0)
    col = lax.broadcasted_iota(jnp.int32, (size, size), 1)
    start = lax.rem(break_at, size)
    before = (lax.rem(row - col + size, size) == 1) & (row != start)
    after = (lax.rem(col - row + size, size) == 1) & (col != start)
    return jnp.where(row == col, -2.0, jnp.where(before | after, 1.0, 0.0)).astype(bf16)


def ready_kernel(corner_ref, exit_ref, start_ref, down_ref, across_ref):
    count = exit_ref.shape[0]
    own = position_at(place_in_group(count), count)
    row_at = corner_ref[0, own]
    col_at = corner_ref[1, own]
    size = start_ref.shape[-1]
    for part in range(2):
        start_ref[part] = turned(exit_ref[own, part], row_at, col_at)
    down_ref[...] = second_difference(size, row_at)
    across_ref[...] = second_difference(size, col_at)


def turn_kernel(corner_ref, wave_ref, turned_ref):
    count = wave_ref.shape[0]

    def one(position, _):
        for part in range(2):
            turned_ref[position, part] = turned(
                wave_ref[position, part], corner_ref[0, position], corner_ref[1, position]
            )
        return 0

    lax.fori_loop(0, count, one, 0)


def back(down, across, chi_re, chi_im):
    def laplacian(field):
        rows = jnp.dot(down, field, preferred_element_type=f32)
        return rows + jnp.dot(field, across, preferred_element_type=f32)

    lap_re = laplacian(chi_re)
    lap_im = laplacian(chi_im)
    lap2_re = laplacian(lap_re.astype(bf16))
    lap2_im = laplacian(lap_im.astype(bf16))
    more_re = 2.0 * lap_re + (damping * lap2_re + turning * lap2_im)
    more_im = 2.0 * lap_im + (damping * lap2_im - turning * lap2_re)
    spread_re = chi_re.astype(f32) + (damping * more_re + turning * more_im)
    spread_im = chi_im.astype(f32) + (damping * more_im - turning * more_re)
    return spread_re, spread_im


def pass_group(down, across, chi_re, chi_im, count, window_of, keep):
    for layer in range(count - 1, -1, -1):
        spread_re, spread_im = back(down, across, chi_re, chi_im)
        keep(layer, spread_re, spread_im)
        win_re, win_im = window_of(layer)
        chi_re = (win_re * spread_re + win_im * spread_im).astype(bf16)
        chi_im = (win_re * spread_im - win_im * spread_re).astype(bf16)
    return chi_re, chi_im


def in_pieces(count, window):
    rows = window // chunk_count
    near = [(apart, slice(0, window)) for apart in distances(count)[:-far]]
    cut = [(count - far + i, slice(c * rows, (c + 1) * rows)) for c in range(chunk_count) for i in range(far)]
    return list(zip(*near, *cut))


def decoded(held_ref, layer):
    return [jnp.log(held_ref[layer, part].astype(f32)) * (1.0 / code_gain) for part in range(2)]


def first_kernel(start_ref, down_ref, across_ref, *refs):
    *win_refs, leave_ref, held_ref = refs
    count, _, window, _ = held_ref.shape
    own = place_in_group(count)
    for win_ref, apart, here in zip(win_refs, *in_pieces(count, window)):
        held_ref[own ^ apart, :, here] = win_ref[...]
    leave_ref[0], leave_ref[1] = pass_group(
        down_ref[...],
        across_ref[...],
        start_ref[0],
        start_ref[1],
        count,
        functools.partial(decoded, held_ref),
        lambda *_: None,
    )


def next_kernel(is_last, start_ref, come_ref, down_ref, across_ref, held_ref, *refs):
    count, _, window, _ = held_ref.shape
    own = place_in_group(count)
    behind = (lax.axis_index("sec") + count).astype(jnp.int32)
    at_end = jnp.full((window, window), behind, jnp.int32) >= lax.axis_size("sec")
    chi_re, chi_im = (
        jnp.where(at_end, start_ref[part].astype(f32), come_ref[part].astype(f32)).astype(bf16) for part in range(2)
    )

    def keep(layer, spread_re, spread_im):
        if is_last:
            refs[-1][layer, 0] = spread_re.astype(bf16)
            refs[-1][layer, 1] = spread_im.astype(bf16)

    chi = pass_group(
        down_ref[...], across_ref[...], chi_re, chi_im, count, functools.partial(decoded, held_ref), keep
    )
    if not is_last:
        refs[0][0], refs[0][1] = chi
        return
    for spread_ref, apart, here in zip(refs, *in_pieces(count, window)):
        spread_ref[...] = refs[-1][own ^ apart, :, here]


def add_kernel(base, picks, begun, ends, corner_ref, wave_ref, *refs):
    spread_refs, refs = refs[: len(picks)], refs[len(picks) :]
    count, _, window, _ = wave_ref.shape
    rows = window // chunk_count
    tall = 16
    own = place_in_group(count)

    def one(block, _):
        at = pl.multiple_of(block * tall, tall)
        rows_at = pl.ds(at, tall)
        here = pl.ds(base + at, tall)
        sums = [refs[0][i, rows_at, :] if begun else jnp.zeros((tall, window), f32) for i in range(8)]
        for apart, spread_ref in zip(picks, spread_refs):
            position = position_at(own ^ apart, count)
            there = rows_at if apart >= count - far else here
            in_mine, in_left = first_masks(corner_ref, position, base + at, (tall, window))
            wave_re, wave_im = (wave_ref[position, part, here, :].astype(f32) for part in range(2))
            spread_re, spread_im = (spread_ref[part, there, :].astype(f32) for part in range(2))
            parts = (
                wave_re * spread_re + wave_im * spread_im,
                wave_re * spread_im - wave_im * spread_re,
            )
            for part in range(2):
                own_part = jnp.where(in_mine, parts[part], 0.0)
                sums[4 * part] += parts[part]
                sums[4 * part + 1] += own_part
                sums[4 * part + 2] += jnp.where(in_left, parts[part], 0.0)
                sums[4 * part + 3] += jnp.where(in_left, own_part, 0.0)
        if not ends:
            for i in range(8):
                refs[-1][i, rows_at, :] = sums[i]
            return 0
        own_ref, away_ref = refs[-2:]
        left, right = pl.ds(0, window), pl.ds(window, window)
        for part in range(2):
            every, mine, at_left, mine_left = sums[4 * part : 4 * part + 4]
            own_ref[part, rows_at, left] = mine_left
            own_ref[part, rows_at, right] = mine - mine_left
            away_ref[part, rows_at, left] = (at_left - mine_left).astype(bf16)
            away_ref[part, rows_at, right] = ((every - mine) - (at_left - mine_left)).astype(bf16)
        return 0

    lax.fori_loop(0, rows // tall, one, 0, unroll=2)


def finish(chunk, own, come, shape, before):
    def kernel(own_ref, come_ref, *refs):
        refs[-1][...] = own_ref[...] + come_ref[...].astype(f32)

    vmem = pl.BlockSpec(memory_space=pltpu.VMEM)
    return pl.pallas_call(
        kernel,
        grid=(1,),
        in_specs=[vmem, vmem] + [pl.BlockSpec(memory_space=pl.ANY)] * len(before),
        out_specs=pl.BlockSpec(own.shape, lambda _: (0, chunk, 0)),
        out_shape=shape_of(shape, f32),
        input_output_aliases={2: 0} if before else {},
        compiler_params=pltpu.CompilerParams(vmem_limit_bytes=6 * 2**20),
    )(own, come, *before)


def shape_of(dims, dtype):
    return jax.ShapeDtypeStruct(dims, dtype)


def on_device(obj_amp, obj_phase, forward_waves, exit_adjoint, offsets):
    sections = lax.axis_size("sec")
    count, _, window, _ = exit_adjoint.shape
    _, half, width = obj_amp.shape
    group_count = sections // count
    chunks = range(chunk_count)
    rows = half // chunk_count
    piece = (2, rows, width)
    wave = (2, window, window)
    corners = offsets.T

    def to_other_half(value):
        return lax.ppermute(value, "scan", [(0, 1), (1, 0)])

    def to_distance(value, d):
        return lax.ppermute(value, "sec", [(s, s ^ d) for s in range(sections)])

    def exchange(near):
        return [to_distance(value, d) if d else value for d, value in zip(distances(count), near)]

    def exchange_far(values):
        return [to_distance(value, count - far + i) for i, value in enumerate(values)]

    mine, other = [], []
    source = (obj_amp, obj_phase)
    for c in chunks:
        if c > 0:
            source, mine[-1] = lax.optimization_barrier((source, mine[-1]))
        mine.append(coded(*(array[0, c * rows : (c + 1) * rows] for array in source)))
        other.append(to_other_half(mine[-1]))
    mine = list(lax.optimization_barrier(mine))
    far_mine = [to_distance(value, count - far) for value in mine]
    ready = call(ready_kernel, [shape_of(wave, bf16)] + [shape_of((window, window), bf16)] * 2, prefetch=1)
    start, down, across = ready(corners, exit_adjoint)
    other[0], start, down, across = lax.optimization_barrier((other[0], start, down, across))
    near, distant = [], []
    for c in chunks:
        cut = call(
            functools.partial(cut_kernel, c * rows, count),
            [shape_of(wave, bf16)] * (count - far),
            prefetch=1,
            aliases={3 + i: i for i in range(len(near))},
        )
        near = cut(corners, mine[c], other[c], *near)
    far_mine[-1], near = lax.optimization_barrier((far_mine[-1], near))
    for c in chunks:
        cut_far = call(
            functools.partial(cut_far_kernel, c * rows, count), [shape_of((2, rows, window), bf16)] * far, prefetch=1
        )
        kept, given = cut_far(corners, far_mine[c], to_other_half(far_mine[c]))
        distant += [kept, to_distance(given, 1)]
    windows = exchange(near) + distant
    waves = call(turn_kernel, shape_of(forward_waves.shape[1:], bf16), prefetch=1)(corners, forward_waves[0])

    pieces = [shape_of(wave, bf16)] * (count - far) + [shape_of((2, rows, window), bf16)] * (far * chunk_count)
    cost = (count * 16 * window**3, count * 2 * window**2)
    first = call(first_kernel, [shape_of(wave, bf16), shape_of((count,) + wave, bf16)], cost=cost, grant=12)
    leave, held = first(start, down, across, *windows)
    for stage in range(1, group_count):
        come = lax.ppermute(
            leave, "sec", [(s, (s - count) ^ (count // 2)) for s in range(count, sections)]
        )
        come, waves = lax.optimization_barrier((come, waves))
        is_last = stage == group_count - 1
        through = call(
            functools.partial(next_kernel, is_last),
            pieces if is_last else shape_of(wave, bf16),
            scratch=[pltpu.VMEM((count,) + wave, bf16)] if is_last else [],
            cost=cost,
            grant=12,
        )
        leave = through(start, come, down, across, held)

    near, distant = leave[: count - far], leave[count - far :]
    came_far = [exchange_far(distant[:far])]
    came = exchange(near)
    came_far += [exchange_far(distant[c * far : (c + 1) * far]) for c in chunks[1:]]
    order = distances(count)
    early, late = order[: count // 2 - 1], order[count // 2 - 1 : count - far]
    spread_at = dict(zip(order, came))

    def add(c, picks, sums, ends):
        spreads = [came_far[c][d - count + far] if d >= count - far else spread_at[d] for d in picks]
        kernel = functools.partial(add_kernel, c * rows, picks, bool(sums), ends)
        given = [shape_of(piece, f32), shape_of(piece, bf16)] if ends else shape_of((8, rows, window), f32)
        return call(kernel, given, prefetch=1)(corners, waves, *spreads, *sums)

    done = []
    for c in chunks:
        if c == 0:
            sums = add(c, early + order[-far:], [], False)
            keep, away = add(c, late, [sums], True)
        else:
            sums = add(c, early, [], False)
            sums, away = lax.optimization_barrier((sums, away))
            sums = add(c, late, [sums], False)
            done.append((keep, to_other_half(away)))
            keep, away = add(c, order[-far:], [sums], True)
    done.append((keep, to_other_half(away)))
    result = []
    for c in chunks:
        result = [finish(c, *done[c], (2, half, width), result)]
    return result[0][None]


def solution(mesh):
    in_specs = (
        P("sec", "scan", None),
        P("sec", "scan", None),
        P("sec", "scan", None, None, None),
        P("scan", None, None, None),
        P("scan", None),
    )
    out_specs = P("sec", None, "scan", None)
    return jax.shard_map(
        on_device, mesh=mesh, in_specs=in_specs, out_specs=out_specs, check_vma=False
    )
```
